32 devices in a mesh: dp: 4 (over z), row: 4 (over y, x), col: 2 (over core).
Axes of the slice: x: 2, y: 2, z: 4, core: 2. Of those that a mesh axis runs over, the one named last changes fastest.
Arguments:
- layer_input: bfloat16 [8192, 1536], P(('dp', 'col'), 'row'), may hold values from -12 to 12
- first_gain: float32 [1536], P('row'), may hold values from 0.25 to 1.75
- query_weight: bfloat16 [1536, 1536], P('row', 'col'), may hold values from -0.15625 to 0.15625
- key_projection_weight: bfloat16 [1536, 768], P('row', 'col'), may hold values from -0.15625 to 0.15625
- value_projection_weight: bfloat16 [1536, 768], P('row', 'col'), may hold values from -0.15625 to 0.15625
- output_weight: bfloat16 [1536, 1536], P('col', 'row'), may hold values from -0.875 to 0.875
- second_gain: float32 [1536], P('row'), may hold values from 0.25 to 1.75
- gate_weight: bfloat16 [1536, 4096], P('row', 'col'), may hold values from -0.15625 to 0.15625
- up_weight: bfloat16 [1536, 4096], P('row', 'col'), may hold values from -0.15625 to 0.15625
- down_weight: bfloat16 [4096, 1536], P('col', 'row'), may hold values from -0.09375 to 0.09375
- sequence_lengths: int32 [4, 3], P('dp'), may hold values from 1 to 1536, 2048 in all within a row
- cotangent: bfloat16 [8192, 1536], P(('dp', 'col'), 'row'), may hold values from -6 to 6
Outputs:
- layer_output: bfloat16 [8192, 1536], P(('dp', 'col'), 'row')
- input_gradient: float32 [8192, 1536], P(('dp', 'col'), 'row')
- query_gradient: float32 [1536, 1536], P('row', 'col')
- key_gradient: float32 [1536, 768], P('row', 'col')
- value_gradient: float32 [1536, 768], P('row', 'col')
- output_gradient: float32 [1536, 1536], P('col', 'row')
- gate_gradient: float32 [1536, 4096], P('row', 'col')
- up_gradient: float32 [1536, 4096], P('row', 'col')
- down_gradient: float32 [4096, 1536], P('col', 'row')
- first_gain_gradient: float32 [1536], P('row')
- second_gain_gradient: float32 [1536], P('row')
The draws below stay inside these ranges and needn't reach their ends.
Inputs may be any that keep to these rules, and one draw needn't show every extreme that they name: `sequence_lengths`: row b gives, in order, the lengths of the 3 sequences that fill token block b; their sum is 2048.
All inputs are finite; a program needn't handle non-finite values.
Results may differ from the reference program's by a relative error of at most 0.039.
Values may be sent and summed in bfloat16 or wider, within the bound.
No kernel may reach another device: no remote copies, remote signals or barrier semaphores. Data moves between devices by JAX's collectives and lax.ppermute only.
A program may use at most 192 MiB of HBM per device.

```python
import math
import jax
import jax.numpy as jnp
import numpy as np
from jax import lax

MODEL_WIDTH = 1536
QUERY_HEADS = 16
KEY_VALUE_HEADS = 8
HEAD_SIZE = 96
FF = 4096
BLOCK = 2048
DOCS = 3
LONGEST = 1536
TOKENS = 8192
N_DP = 4


def draw_layer_input(key, part):
    key = jax.random.fold_in(key, 11)
    column = jnp.arange(MODEL_WIDTH, dtype=jnp.float32) / (MODEL_WIDTH - 1)
    scales = jnp.exp(column * 1.0986)
    values = jnp.clip(jax.random.normal(key, (TOKENS, MODEL_WIDTH), jnp.float32), -4.0, 4.0)
    return (values * scales[None, :]).astype(jnp.bfloat16)


def shard_levels(key, extent, cuts, least, largest):
    gain, own = 1.0, jax.random.fold_in(key, 6)
    for axis_at, shards_of in cuts:
        heights = jnp.exp(jax.random.uniform(jax.random.fold_in(own, axis_at), (shards_of,), jnp.float32, least / len(cuts), largest / len(cuts)))
        gain = gain * jnp.repeat(heights, extent[axis_at] // shards_of).reshape([-1 if axis == axis_at else 1 for axis in range(len(extent))])
    return gain


def profile(count, total, limit, slope):
    portions = [(1 << 20) // math.isqrt(grade ** slope) + 1 for grade in range(2, count + 1)]
    spare, holding = total - limit - (count - 1), [1] * (count - 1)
    while spare > 0:
        movable = [i for i in range(count - 1) if holding[i] < limit]
        pool, remaining = sum([portions[i] for i in movable]), spare
        for i in movable:
            more = min(limit - holding[i], max(1, remaining * portions[i] // pool), spare)
            holding[i] = holding[i] + more
            spare = spare - more
    return np.array([limit] + holding)


def ragged_sizes(rng, number_of, total, most, slope):
    if number_of == 2:
        one = jax.random.randint(rng, (), max(1, total - most), min(most, total - 1) + 1)
        return jnp.stack([one, total - one])
    tallies = jnp.asarray(profile(number_of, total, most, slope), jnp.int32)
    pairs = (number_of - 1) // 2
    giver, sink = tallies[1:1 + 2 * pairs:2], tallies[2:2 + 2 * pairs:2]
    room = jnp.minimum(giver - 1, most - sink)
    moved = jax.random.randint(jax.random.fold_in(rng, 1), (pairs,), 0, 1 << 20) % (room + 1)
    tallies = tallies.at[1:1 + 2 * pairs:2].set(giver - moved).at[2:2 + 2 * pairs:2].set(sink + moved)
    return tallies[jax.random.permutation(jax.random.fold_in(rng, 2), number_of)]


def centred(key, extent, width, reach, shards=(), kind=jnp.bfloat16):
    entries = width * jax.random.normal(key, extent, jnp.float32)
    if shards:
        entries = entries * shard_levels(key, extent, shards, -0.22, 0.18)
    return jnp.clip(entries, -reach, reach).astype(kind)


def setup_inputs(seed: int = 0) -> dict:
    splits = jax.random.split(jax.random.key(seed), 13)
    return {
        "layer_input": draw_layer_input(jax.random.fold_in(splits[12], 71), 0),
        "first_gain": jnp.clip(1.0 + 0.15 * jax.random.normal(splits[1], (MODEL_WIDTH,), jnp.float32), 0.25, 1.75),
        "query_weight": centred(splits[2], (MODEL_WIDTH, QUERY_HEADS * HEAD_SIZE), MODEL_WIDTH ** -0.5, 0.15625, ((0, 4), (1, 2))),
        "key_projection_weight": centred(splits[3], (MODEL_WIDTH, KEY_VALUE_HEADS * HEAD_SIZE), MODEL_WIDTH ** -0.5, 0.15625, ((0, 4), (1, 2))),
        "value_projection_weight": centred(splits[4], (MODEL_WIDTH, KEY_VALUE_HEADS * HEAD_SIZE), MODEL_WIDTH ** -0.5, 0.15625, ((0, 4), (1, 2))),
        "output_weight": centred(splits[5], (QUERY_HEADS * HEAD_SIZE, MODEL_WIDTH), (QUERY_HEADS * HEAD_SIZE // 32) ** -0.5, 0.875, ((0, 2), (1, 4))),
        "second_gain": jnp.clip(1.0 + 0.15 * jax.random.normal(splits[6], (MODEL_WIDTH,), jnp.float32), 0.25, 1.75),
        "gate_weight": centred(splits[7], (MODEL_WIDTH, FF), MODEL_WIDTH ** -0.5, 0.15625, ((0, 4), (1, 2))),
        "up_weight": centred(splits[8], (MODEL_WIDTH, FF), MODEL_WIDTH ** -0.5, 0.15625, ((0, 4), (1, 2))),
        "down_weight": centred(splits[9], (FF, MODEL_WIDTH), FF ** -0.5, 0.09375, ((0, 2), (1, 4))),
        "sequence_lengths": jax.vmap(lambda own: ragged_sizes(own, DOCS, BLOCK, LONGEST, 0))(jax.random.split(splits[10], N_DP)).reshape((N_DP, DOCS)).astype(jnp.int32),
        "cotangent": centred(splits[11], (TOKENS, MODEL_WIDTH), 1.0, 6.0, ((0, 8), (1, 4))),
    }


EPSILON = 1e-05
THETA = 100000.0
HIGHEST = lax.Precision.HIGHEST

@jax.custom_vjp
def low(v):
    return lax.optimization_barrier(v.astype(jnp.bfloat16)).astype(jnp.float32)

@jax.custom_vjp
def low_back(v):
    return v

def low_keep(v):
    return (low(v), None)

def low_pass(kept, grad):
    return (grad,)

def back_keep(v):
    return (v, None)

def back_low(kept, grad):
    return (low(grad),)
low.defvjp(low_keep, low_pass)
low_back.defvjp(back_keep, back_low)

def matrix_multiply(left, right):
    return jnp.dot(left, right, precision=HIGHEST, preferred_element_type=jnp.float32)

def rms_norm(values, norm_gain):
    return values * lax.rsqrt(lax.optimization_barrier(jnp.mean(values * values, axis=-1, keepdims=True)) + EPSILON) * norm_gain

def layout(length_row, token_total_count):
    end_points = jnp.cumsum(length_row).astype(jnp.int32)
    starts = (end_points - length_row).astype(jnp.int32)
    places = jnp.arange(token_total_count, dtype=jnp.int32)
    member = lax.optimization_barrier(jnp.sum((places[:, None] >= end_points[None, :]).astype(jnp.int32), axis=1)).astype(jnp.int32)
    chosen = member[:, None] == jnp.arange(length_row.shape[0], dtype=jnp.int32)[None, :]
    offset = lax.optimization_barrier(jnp.sum(jnp.where(chosen, starts[None, :], 0), axis=1)).astype(jnp.int32)
    return (member, places - offset)

def tables(places, head_size):
    half_width = head_size // 2
    frequency = THETA ** (-2.0 * jnp.arange(half_width, dtype=jnp.float32) / head_size)
    angles = places.astype(jnp.float32)[:, None] * frequency[None, :]
    return (jnp.cos(angles), jnp.sin(angles))

def rotate(values, cosine, sine_part):
    half_width = values.shape[-1] // 2
    first_half = values[..., :half_width]
    second_half = values[..., half_width:]
    cos_heads = cosine[:, None, :]
    sin_heads = sine_part[:, None, :]
    return jnp.concatenate([first_half * cos_heads - second_half * sin_heads, second_half * cos_heads + first_half * sin_heads], axis=-1)

def layer(values, params, member, places):
    first_gain, query_matrix, key_projected, value_projected, output_matrix, second_gain, gate_matrix, up_matrix, down_matrix = params
    token_total_count = values.shape[0]
    group_width = QUERY_HEADS // KEY_VALUE_HEADS
    cosine, sine_part = tables(places, HEAD_SIZE)
    first_norm_output = low(rms_norm(values, first_gain))
    queries = low_back(matrix_multiply(first_norm_output, query_matrix)).reshape(token_total_count, QUERY_HEADS, HEAD_SIZE)
    key_head_rows = low_back(matrix_multiply(first_norm_output, key_projected)).reshape(token_total_count, KEY_VALUE_HEADS, HEAD_SIZE)
    value_head_rows = low_back(matrix_multiply(first_norm_output, value_projected)).reshape(token_total_count, KEY_VALUE_HEADS, HEAD_SIZE)
    turned_q = low(rotate(queries, cosine, sine_part))
    turned_k = jnp.repeat(low(rotate(key_head_rows, cosine, sine_part)), group_width, axis=1)
    value_low = jnp.repeat(low(value_head_rows), group_width, axis=1)
    scores = low_back(jnp.einsum('qhd,khd->hqk', turned_q, turned_k, precision=HIGHEST))
    position = jnp.arange(token_total_count, dtype=jnp.int32)
    allowed = (member[:, None] == member[None, :]) & (position[:, None] >= position[None, :])
    logits = jnp.where(allowed[None], scores * HEAD_SIZE ** (-0.5), -1e+30)
    maximum = lax.optimization_barrier(jnp.max(logits, axis=-1, keepdims=True))
    exponent = jnp.exp(logits - maximum)
    probability = exponent / lax.optimization_barrier(jnp.sum(exponent, axis=-1, keepdims=True))
    attended = jnp.einsum('hqk,khd->qhd', low(probability), value_low, precision=HIGHEST)
    heads_out = low(low_back(attended)).reshape(token_total_count, QUERY_HEADS * HEAD_SIZE)
    middle = values + low_back(matrix_multiply(heads_out, output_matrix))
    second_normed = low(rms_norm(middle, second_gain))
    gate_values = low_back(matrix_multiply(second_normed, gate_matrix))
    up_values = low_back(matrix_multiply(second_normed, up_matrix))
    hidden = low(jax.nn.silu(gate_values) * up_values)
    return middle + low_back(matrix_multiply(hidden, down_matrix))

def reference(layer_input, first_gain, query_weight, key_projection_weight, value_projection_weight, output_weight, second_gain, gate_weight, up_weight, down_weight, sequence_lengths, cotangent):
    params = (first_gain.astype(jnp.float32), query_weight.astype(jnp.float32), key_projection_weight.astype(jnp.float32), value_projection_weight.astype(jnp.float32), output_weight.astype(jnp.float32), second_gain.astype(jnp.float32), gate_weight.astype(jnp.float32), up_weight.astype(jnp.float32), down_weight.astype(jnp.float32))
    inputs = layer_input.astype(jnp.float32).reshape(N_DP, BLOCK, MODEL_WIDTH)
    upstream = cotangent.astype(jnp.float32).reshape(N_DP, BLOCK, MODEL_WIDTH)

    def one_block(totals, item):
        block_input, block_upstream, length_row = item
        member, places = layout(length_row, BLOCK)

        def forward(values, weights):
            return layer(values, weights, member, places)
        result, pullback = jax.vjp(forward, block_input, params)
        input_grad, weight_grads = pullback(block_upstream)
        totals = tuple((running + part for running, part in zip(totals, weight_grads)))
        return (totals, (result.astype(jnp.bfloat16), input_grad))
    initial = tuple((jnp.zeros_like(matrix) for matrix in params))
    totals, (outputs, input_grads) = lax.scan(one_block, initial, (inputs, upstream, sequence_lengths))
    return (outputs.reshape(TOKENS, MODEL_WIDTH), input_grads.reshape(TOKENS, MODEL_WIDTH), totals[1], totals[2], totals[3], totals[4], totals[6], totals[7], totals[8], totals[0], totals[5])
```

```python
import functools

import jax
import jax.numpy as jnp
from jax import lax
from jax.experimental import pallas as pl
from jax.experimental.pallas import tpu as pltpu
from jax.sharding import PartitionSpec as P

HEAD = 96
LANES = 128
SIDE = 48
TILE = 256
EPSILON = 1e-05
THETA = 100000.0
LOG2E = 1.4426950408889634
FACTOR = HEAD**-0.5
LOW = jnp.bfloat16
F32 = jnp.float32
NN = (((1,), (0,)), ((), ()))
NT = (((1,), (1,)), ((), ()))
TN = (((0,), (0,)), ((), ()))
VMEM_LIMIT = 48 * 1024 * 1024


def dot(left, right, dims=NN):
    return lax.dot_general(left, right, dims, preferred_element_type=F32)


def swap(value, step):
    return lax.ppermute(value, "row", [(i, i ^ step) for i in range(4)])


def other(value):
    return lax.ppermute(value, "col", [(0, 1), (1, 0)])


def gather_row(value):
    half = value.shape[0] // 2
    along_x = swap(value, 1)
    along_y = swap(value, 2)
    top = swap(along_x[:half], 2)
    bottom = swap(along_y[half:], 1)
    return [value, along_x, along_y, jnp.concatenate([top, bottom], axis=0)]


def exchange_row(pieces):
    return [pieces[0]] + [swap(pieces[i], i) for i in (1, 2, 3)]


def total_row(value):
    return value + swap(value, 1) + swap(value, 2) + swap(value, 3)


def scatter_row(parts):
    own_a, a_xd, a_y, own_b, b_yd, b_x = parts
    width = own_a.shape[1]
    got_a = swap(a_xd, 1)
    got_b = swap(b_yd, 2)
    send_a = (a_y.astype(F32) + got_a[:, width:].astype(F32)).astype(LOW)
    send_b = (b_x.astype(F32) + got_b[:, width:].astype(F32)).astype(LOW)
    last_a = swap(send_a, 2)
    last_b = swap(send_b, 1)
    total_a = own_a.astype(F32) + got_a[:, :width].astype(F32) + last_a.astype(F32)
    total_b = own_b.astype(F32) + got_b[:, :width].astype(F32) + last_b.astype(F32)
    return jnp.concatenate([total_a, total_b], axis=0)


def chain_scatter(take, count):
    place = lax.axis_index("dp")
    own = take(place)
    if count == 1:
        return own
    right = left = None
    for step in range(1, count):
        up = take(jnp.clip(count - step + place, 0, count - 1))
        down = take(jnp.clip(place - (count - step), 0, count - 1))
        if right is not None:
            up = (up.astype(F32) + right.astype(F32)).astype(LOW)
            down = (down.astype(F32) + left.astype(F32)).astype(LOW)
        ups = [(i, i + 1) for i in range(min(step, count - 1))]
        right = lax.ppermute(up, "dp", ups)
        left = lax.ppermute(down, "dp", [(count - 1 - i, count - 1 - j) for i, j in ups])
    return (own.astype(F32) + right.astype(F32) + left.astype(F32)).astype(LOW)


def chain_gather(shard, count):
    place = lax.axis_index("dp")
    shape = (shard.shape[0], count) + shard.shape[1:]
    result = jnp.zeros(shape, shard.dtype)
    zero = jnp.zeros((), jnp.int32)

    def put(result, piece, at):
        start = (zero, at) + (zero,) * (len(shape) - 2)
        return lax.dynamic_update_slice(result, piece[:, None], start)

    right = left = shard
    for step in range(1, count):
        ups = [(i, i + 1) for i in range(step - 1, count - 1)]
        right = lax.ppermute(right, "dp", ups)
        left = lax.ppermute(left, "dp", [(count - 1 - i, count - 1 - j) for i, j in ups])
        result = put(result, right, jnp.where(place - step >= 0, place - step, place))
        result = put(result, left, jnp.where(place + step < count, place + step, place))
    return put(result, shard, place)


def call(kernel, out_shape, in_specs, out_specs, grid=(), scratch=(), prefetch=0, flops=0, moved=0):
    return pl.pallas_call(
        kernel,
        out_shape=out_shape,
        grid_spec=pltpu.PrefetchScalarGridSpec(
            num_scalar_prefetch=prefetch,
            grid=grid,
            in_specs=in_specs,
            out_specs=out_specs,
            scratch_shapes=list(scratch),
        ),
        compiler_params=pltpu.CompilerParams(vmem_limit_bytes=VMEM_LIMIT),
        cost_estimate=pl.CostEstimate(flops=int(flops), bytes_accessed=int(moved), transcendentals=0),
    )


def shape(dims, kind=LOW):
    return jax.ShapeDtypeStruct(tuple(dims), kind)


def whole(array):
    rank = len(array.shape)
    return pl.BlockSpec(tuple(array.shape), lambda *_: (0,) * rank)


def bytes_of(*arrays):
    return sum(int(a.size) * a.dtype.itemsize for a in arrays)


def pack_kernel(row_ref, q_ref, k_ref, v_ref, out_ref):
    row = row_ref[0]
    query, key = q_ref.shape[1] // 4, k_ref.shape[1] // 4
    for j in range(4):
        at = jnp.bitwise_xor(row, j)
        out_ref[at, :, :query] = q_ref[:, j * query : (j + 1) * query]
        out_ref[at, :, query : query + key] = k_ref[:, j * key : (j + 1) * key]
        out_ref[at, :, query + key :] = v_ref[:, j * key : (j + 1) * key]


def pack(row, query_weight, key_weight, value_weight):
    depth = query_weight.shape[0]
    width = (query_weight.shape[1] + 2 * key_weight.shape[1]) // 4
    out = shape((4, depth, width))
    arrays = (query_weight, key_weight, value_weight)
    return call(
        pack_kernel,
        out,
        [whole(a) for a in arrays],
        whole(out),
        grid=(1,),
        prefetch=1,
        moved=2 * bytes_of(out),
    )(row, *arrays)


def project_kernel(x0, x1, x2, x3, gain, w_own, w_oth, cos, sin, first, r1, own, oth):
    x = jnp.concatenate([x0[...], x1[...], x2[...], x3[...]], axis=1).astype(F32)
    inverse = lax.rsqrt(jnp.mean(x * x, axis=1, keepdims=True) + EPSILON)
    normed = (x * inverse * gain[...]).astype(LOW)
    first[...] = normed
    r1[...] = jnp.broadcast_to(inverse, r1.shape)
    for weight, out in ((w_own, own), (w_oth, oth)):
        heads = dot(normed, weight[...])
        for h in range(3):
            part = heads[:, h * LANES : (h + 1) * LANES]
            turned = part * cos[...] + pltpu.roll(part, LANES // 2, 1) * sin[...]
            out[:, h * LANES : (h + 1) * LANES] = turned.astype(LOW)
        out[:, 3 * LANES :] = heads[:, 3 * LANES :].astype(LOW)


def project(xs, gain, w_own, w_oth, cos, sin):
    tokens, width = xs[0].shape
    rows = lambda n: pl.BlockSpec((TILE, n), lambda b: (b, 0))
    outs = (shape((tokens, 4 * width)), shape((tokens, LANES), F32), shape((tokens, 512)), shape((tokens, 512)))
    return call(
        project_kernel,
        outs,
        [rows(width)] * 4 + [whole(gain), whole(w_own), whole(w_oth), rows(LANES), rows(LANES)],
        tuple(rows(o.shape[1]) for o in outs),
        grid=(tokens // TILE,),
        flops=2 * tokens * 4 * width * 1024,
        moved=bytes_of(*xs, w_own, w_oth, *outs),
    )(*xs, gain, w_own, w_oth, cos, sin)


def stack_heads(ref, rows):
    return jnp.concatenate([ref[rows, :LANES], ref[rows, LANES : 2 * LANES]], axis=0)


def block_limits(start_ref, block):
    rows = pl.ds(pl.multiple_of(block * TILE, TILE), TILE)
    start = start_ref[:, rows]
    query = block * TILE + lax.broadcasted_iota(jnp.int32, (1, TILE), 1)
    return jnp.concatenate([start, start], axis=1), jnp.concatenate([query, query], axis=1)


def allowed_keys(number, start, query):
    key = number * TILE + lax.broadcasted_iota(jnp.int32, (TILE, 2 * TILE), 0)
    return (key >= start) & (key <= query)


def attend_kernel(info, own, oth, start_ref, keep, send, out, lse, full, values, top, total, acc):
    block = pl.program_id(0)
    core = info[0]
    half = own.shape[0]

    @pl.when(block == 0)
    def _():
        full[pl.ds(pl.multiple_of(core * half, half), half), :] = own[...]
        full[pl.ds(pl.multiple_of((1 - core) * half, half), half), :] = oth[...]
        values[...] = full[:, 3 * LANES :].T

    rows = pl.ds(pl.multiple_of(block * TILE, TILE), TILE)
    query = stack_heads(full, rows)
    start, place = block_limits(start_ref, block)
    top[...] = jnp.full(top.shape, -1e30, F32)
    total[...] = jnp.zeros(total.shape, F32)
    acc[...] = jnp.zeros(acc.shape, F32)

    def step(number, _):
        keys = pl.ds(pl.multiple_of(number * TILE, TILE), TILE)
        scores = dot(full[keys, 2 * LANES : 3 * LANES], query, NT) * (FACTOR * LOG2E)
        scores = jnp.where(allowed_keys(number, start, place), scores, -1e30)
        before = top[...]
        now = jnp.maximum(before, jnp.max(scores, axis=0, keepdims=True))
        weight = jnp.exp2(scores - now)
        scale = jnp.exp2(before - now)
        top[...] = now
        total[...] = total[...] * scale + jnp.sum(weight, axis=0, keepdims=True)
        acc[...] = acc[...] * scale + dot(values[:, keys], weight.astype(LOW))
        return 0

    lax.fori_loop(info[1 + block], block + 1, step, 0)
    lse[...] = top[...] + jnp.log2(total[...])
    result = (acc[...] / total[...]).T.astype(LOW)
    out[:, :LANES] = result[:TILE]
    out[:, LANES:] = result[TILE:]
    mine = (block // (half // TILE)) == core
    for target, wanted in ((keep, mine), (send, jnp.logical_not(mine))):

        @pl.when(wanted)
        def _(target=target):
            target[:, :HEAD] = result[:TILE, :HEAD]
            target[:, HEAD:] = result[TILE:, :HEAD]


def attend(info, own, oth, start):
    half = own.shape[0]
    tokens = 2 * half
    per_half = half // TILE
    outs = (
        shape((half, 2 * HEAD)),
        shape((half, 2 * HEAD)),
        shape((tokens, 2 * LANES)),
        shape((1, 2 * tokens), F32),
    )
    return call(
        attend_kernel,
        outs,
        [whole(own), whole(oth), whole(start)],
        (
            pl.BlockSpec((TILE, 2 * HEAD), lambda b, s: (jnp.clip(b - s[0] * per_half, 0, per_half - 1), 0)),
            pl.BlockSpec((TILE, 2 * HEAD), lambda b, s: (jnp.clip(b - (1 - s[0]) * per_half, 0, per_half - 1), 0)),
            pl.BlockSpec((TILE, 2 * LANES), lambda b, s: (b, 0)),
            pl.BlockSpec((1, 2 * TILE), lambda b, s: (0, b)),
        ),
        grid=(tokens // TILE,),
        scratch=(
            pltpu.VMEM((tokens, 4 * LANES), LOW),
            pltpu.VMEM((LANES, tokens), LOW),
            pltpu.VMEM((1, 2 * TILE), F32),
            pltpu.VMEM((1, 2 * TILE), F32),
            pltpu.VMEM((LANES, 2 * TILE), F32),
        ),
        prefetch=1,
        flops=4 * tokens * tokens * LANES * 2,
        moved=bytes_of(own, oth, *outs),
    )(info, own, oth, start)


def turn_back(part, cos, sin):
    return part * cos - pltpu.roll(part, LANES // 2, 1) * sin


def attend_back_kernel(
    info, own, oth, g_own, g_oth, out, lse, start_ref, cos, sin,
    keep, send, full, grads, keys_t, d_keys, d_values, d_query, result,
):
    block = pl.program_id(0)
    core = info[0]
    half = own.shape[0]

    @pl.when(block == 0)
    def _():
        mine = pl.ds(pl.multiple_of(core * half, half), half)
        theirs = pl.ds(pl.multiple_of((1 - core) * half, half), half)
        full[mine, :] = own[...]
        full[theirs, :] = oth[...]
        grads[mine, :] = g_own[...]
        grads[theirs, :] = g_oth[...]
        keys_t[...] = full[:, 2 * LANES : 3 * LANES].T
        d_keys[...] = jnp.zeros(d_keys.shape, F32)
        d_values[...] = jnp.zeros(d_values.shape, F32)

    rows = pl.ds(pl.multiple_of(block * TILE, TILE), TILE)
    query = stack_heads(full, rows)
    grad = stack_heads(grads, rows)
    reply = stack_heads(out, slice(None))
    start, place = block_limits(start_ref, block)
    level = lse[...]
    delta = jnp.sum((grad.astype(F32) * reply.astype(F32)).T, axis=0, keepdims=True)
    d_query[...] = jnp.zeros(d_query.shape, F32)

    def step(number, _):
        keys = pl.ds(pl.multiple_of(number * TILE, TILE), TILE)
        scores = dot(full[keys, 2 * LANES : 3 * LANES], query, NT) * (FACTOR * LOG2E)
        scores = jnp.where(allowed_keys(number, start, place), scores, -1e30)
        weight = jnp.exp2(scores - level)
        pressure = dot(full[keys, 3 * LANES :], grad, NT)
        slope = (weight * (pressure - delta) * FACTOR).astype(LOW)
        d_values[keys, :] += dot(weight.astype(LOW), grad)
        d_keys[keys, :] += dot(slope, query)
        d_query[...] += dot(keys_t[:, keys], slope)
        return 0

    lax.fori_loop(info[1 + block], block + 1, step, 0)
    turned = d_query[...].T
    for h in range(2):
        part = turned[h * TILE : (h + 1) * TILE]
        result[rows, h * LANES : (h + 1) * LANES] = turn_back(part, cos[rows, :], sin[rows, :]).astype(LOW)

    @pl.when(block == pl.num_programs(0) - 1)
    def _():
        mine = pl.ds(pl.multiple_of(core * half, half), half)
        theirs = pl.ds(pl.multiple_of((1 - core) * half, half), half)
        for target, which in ((keep, mine), (send, theirs)):
            target[:, : 2 * LANES] = result[which, :]
            target[:, 2 * LANES : 3 * LANES] = turn_back(
                d_keys[which, :], cos[which, :], sin[which, :]
            ).astype(LOW)
            target[:, 3 * LANES :] = d_values[which, :].astype(LOW)


def attend_back(info, own, oth, g_own, g_oth, out, lse, start, cos, sin):
    half = own.shape[0]
    tokens = 2 * half
    outs = (shape((half, 4 * LANES)), shape((half, 4 * LANES)))
    return call(
        attend_back_kernel,
        outs,
        [
            whole(own),
            whole(oth),
            whole(g_own),
            whole(g_oth),
            pl.BlockSpec((TILE, 2 * LANES), lambda b, s: (b, 0)),
            pl.BlockSpec((1, 2 * TILE), lambda b, s: (0, b)),
            whole(start),
            whole(cos),
            whole(sin),
        ],
        tuple(whole(o) for o in outs),
        grid=(tokens // TILE,),
        scratch=(
            pltpu.VMEM((tokens, 4 * LANES), LOW),
            pltpu.VMEM((tokens, 2 * LANES), LOW),
            pltpu.VMEM((LANES, tokens), LOW),
            pltpu.VMEM((tokens, LANES), F32),
            pltpu.VMEM((tokens, LANES), F32),
            pltpu.VMEM((LANES, 2 * TILE), F32),
            pltpu.VMEM((tokens, 2 * LANES), LOW),
        ),
        prefetch=1,
        flops=10 * tokens * tokens * LANES * 2,
        moved=bytes_of(own, oth, g_own, g_oth, out, *outs),
    )(info, own, oth, g_own, g_oth, out, lse, start, cos, sin)


def middle_kernel(h0, h1, h2, h3, x0, x1, x2, x3, weight, gain, second, middle, r2):
    heads = jnp.concatenate([h0[...], h1[...], h2[...], h3[...]], axis=1)
    x = jnp.concatenate([x0[...], x1[...], x2[...], x3[...]], axis=1).astype(F32)
    value = x + dot(heads, weight[...])
    inverse = lax.rsqrt(jnp.mean(value * value, axis=1, keepdims=True) + EPSILON)
    second[...] = (value * inverse * gain[...]).astype(LOW)
    middle[...] = value[:, : middle.shape[1]]
    r2[...] = jnp.broadcast_to(inverse, r2.shape)


def middle_of(heads, xs, weight, gain):
    tokens, width = xs[0].shape
    rows = lambda n: pl.BlockSpec((TILE, n), lambda b: (b, 0))
    outs = (shape((tokens, 4 * width)), shape((tokens, width), F32), shape((tokens, LANES), F32))
    return call(
        middle_kernel,
        outs,
        [rows(width)] * 8 + [whole(weight), whole(gain)],
        tuple(rows(o.shape[1]) for o in outs),
        grid=(tokens // TILE,),
        flops=2 * tokens * 16 * width * width,
        moved=bytes_of(*heads, *xs, weight, *outs),
    )(*heads, *xs, weight, gain)


def feed_kernel(second, cot, g_own, u_own, g_oth, u_oth, d_own, d_oth, hidden_own, hidden_oth, back_own, back_oth):
    block = pl.program_id(0)
    per = pl.num_programs(0) // 2
    units = hidden_own.shape[1]

    def body(gate_w, up_w, down_w, hidden, back, at):
        gate = dot(second[...], gate_w[...])
        up = dot(second[...], up_w[...])
        hidden_grad = dot(cot[...], down_w[...], NT)
        share = 1.0 / (1.0 + jnp.exp(-gate))
        silu = gate * share
        hidden[:, pl.ds(pl.multiple_of(at, TILE), TILE)] = (silu * up).astype(LOW)
        back[:, pl.ds(pl.multiple_of(at, TILE), TILE)] = (
            hidden_grad * up * share * (1.0 + gate * (1.0 - share))
        ).astype(LOW)
        back[:, pl.ds(pl.multiple_of(units + at, TILE), TILE)] = (hidden_grad * silu).astype(LOW)

    @pl.when(block < per)
    def _():
        body(g_own, u_own, d_own, hidden_own, back_own, block * TILE)

    @pl.when(block >= per)
    def _():
        body(g_oth, u_oth, d_oth, hidden_oth, back_oth, (block - per) * TILE)


def feed(second, cot, gu_own, gu_oth, d_own, d_oth):
    tokens, model = second.shape
    units = gu_own.shape[1] // 2
    per = units // TILE
    early = lambda b: jnp.minimum(b, per - 1)
    late = lambda b: jnp.maximum(b - per, 0)
    column = lambda at: pl.BlockSpec((model, TILE), lambda b: (0, at(b)))
    down = lambda at: pl.BlockSpec((TILE, model), lambda b: (at(b), 0))
    outs = (shape((tokens, units)), shape((tokens, units)), shape((tokens, 2 * units)), shape((tokens, 2 * units)))
    return call(
        feed_kernel,
        outs,
        [
            whole(second),
            whole(cot),
            column(early),
            column(lambda b: per + early(b)),
            column(late),
            column(lambda b: per + late(b)),
            down(early),
            down(late),
        ],
        tuple(whole(o) for o in outs),
        grid=(2 * per,),
        flops=12 * tokens * model * units,
        moved=bytes_of(second, cot, gu_own, gu_oth, d_own, d_oth, *outs),
    )(second, cot, gu_own, gu_own, gu_oth, gu_oth, d_own, d_oth)


def back_kernel(dims, a_own, a_oth, w_own, w_oth, *rest):
    value = dot(a_own[...], w_own[...], dims) + dot(a_oth[...], w_oth[...], dims)
    if len(rest) == 5:
        against, own, far, near, sums = rest
        sums[...] = jnp.broadcast_to(
            jnp.sum(value * against[...].astype(F32), axis=1, keepdims=True), sums.shape
        )
    else:
        own, far, near = rest
    width = own.shape[1]
    low = value.astype(LOW)
    own[...] = low[:, :width]
    return low, far, near, width


def back_first(dims, *refs):
    low, far, near, width = back_kernel(dims, *refs)
    far[:, :width] = low[:, width : 2 * width]
    far[:, width:] = low[:, 3 * width :]
    near[...] = low[:, 2 * width : 3 * width]


def back_second(dims, *refs):
    low, far, near, width = back_kernel(dims, *refs)
    far[...] = low[:, 2 * width :]
    near[...] = low[:, width : 2 * width]


def partial_half(which, dims, a_own, a_oth, w_own, w_oth, against):
    tokens, depth = a_own.shape
    model = w_own.shape[0] if dims == NT else w_own.shape[1]
    half, width = tokens // 2, model // 4
    blocks = half // TILE
    read = lambda n: pl.BlockSpec((TILE, n), lambda b: (which * blocks + b, 0))
    write = lambda n: pl.BlockSpec((TILE, n), lambda b: (b, 0))
    outs = [shape((half, width)), shape((half, 2 * width)), shape((half, width))]
    args = [a_own, a_oth, w_own, w_oth]
    specs = [read(depth), read(depth), whole(w_own), whole(w_oth)]
    if against is not None:
        outs.append(shape((half, LANES), F32))
        args.append(against)
        specs.append(read(model))
    return call(
        functools.partial(back_second if which else back_first, dims),
        tuple(outs),
        specs,
        tuple(write(o.shape[1]) for o in outs),
        grid=(blocks,),
        flops=4 * half * depth * model,
        moved=bytes_of(w_own, w_oth, *outs) + half * 4 * depth,
    )(*args)


def partial_sums(dims, a_own, a_oth, w_own, w_oth, against=None):
    first = partial_half(0, dims, a_own, a_oth, w_own, w_oth, against)
    second = partial_half(1, dims, a_own, a_oth, w_own, w_oth, against)
    sums = None if against is None else jnp.concatenate([first[3][:, 0], second[3][:, 0]])
    return (first[0], first[1], first[2], second[0], second[1], second[2]), sums


def feed_place_kernel(row_ref, piece, gate, up, down):
    units = gate.shape[1]
    gate[...] = piece[0, :, :units].astype(F32)
    up[...] = piece[0, :, units : 2 * units].astype(F32)
    down[...] = piece[0, :, 2 * units :].astype(F32).T


def feed_place(row, pieces):
    _, depth, triple = pieces.shape
    units = triple // 3
    outs = (shape((depth, 4 * units), F32), shape((depth, 4 * units), F32), shape((4 * units, depth), F32))
    return call(
        feed_place_kernel,
        outs,
        [pl.BlockSpec((1, depth, triple), lambda j, s: (jnp.bitwise_xor(s[0], j), 0, 0))],
        (
            pl.BlockSpec((depth, units), lambda j, s: (0, j)),
            pl.BlockSpec((depth, units), lambda j, s: (0, j)),
            pl.BlockSpec((units, depth), lambda j, s: (j, 0)),
        ),
        grid=(4,),
        prefetch=1,
        moved=bytes_of(pieces, *outs),
    )(row, pieces)


def mix_place_kernel(row_ref, pieces, heads, query, key, value, output):
    row = row_ref[0]
    wide, narrow = query.shape[1] // 4, key.shape[1] // 4
    for j in range(4):
        piece = pieces[jnp.bitwise_xor(row, j)].astype(F32)
        query[:, j * wide : (j + 1) * wide] = piece[:, :wide]
        key[:, j * narrow : (j + 1) * narrow] = piece[:, wide : wide + narrow]
        value[:, j * narrow : (j + 1) * narrow] = piece[:, wide + narrow :]
        output[j * wide : (j + 1) * wide, :] = heads[jnp.bitwise_xor(row, j)].astype(F32)


def mix_place(row, pieces, heads):
    _, depth, width = pieces.shape
    wide, narrow = width // 2, width // 4
    outs = (
        shape((depth, 4 * wide), F32),
        shape((depth, 4 * narrow), F32),
        shape((depth, 4 * narrow), F32),
        shape((4 * wide, depth), F32),
    )
    return call(
        mix_place_kernel,
        outs,
        [whole(pieces), whole(heads)],
        tuple(whole(o) for o in outs),
        grid=(1,),
        prefetch=1,
        moved=bytes_of(pieces, heads, *outs),
    )(row, pieces, heads)


def sequence_starts(lengths, tokens):
    places = jnp.arange(tokens, dtype=jnp.int32)
    starts = jnp.zeros((tokens,), jnp.int32)
    end = jnp.zeros((), jnp.int32)
    for k in range(lengths.shape[0]):
        end = end + lengths[k]
        starts = jnp.where(places >= end, end, starts)
    return places, starts


def tables(places):
    lane = jnp.arange(LANES, dtype=jnp.int32)
    entry = lane % (LANES // 2)
    frequency = THETA ** (-2.0 * entry.astype(F32) / HEAD)
    real = entry < SIDE
    angles = places.astype(F32)[:, None] * frequency[None, :]
    cosine = jnp.where(real[None, :], jnp.cos(angles), 0.0)
    sign = jnp.where(lane < LANES // 2, -1.0, 1.0)
    sine = jnp.where(real[None, :], jnp.sin(angles) * sign[None, :], 0.0)
    return cosine, sine


def spread_matrix():
    source = jnp.arange(4 * HEAD, dtype=jnp.int32)
    head, entry = source // HEAD, source % HEAD
    inside = jnp.where((head < 3) & (entry >= SIDE), entry - SIDE + LANES // 2, entry)
    target = head * LANES + inside
    return (target[:, None] == jnp.arange(4 * LANES, dtype=jnp.int32)[None, :]).astype(LOW)


def pad_heads(rows):
    heads = rows.shape[0] // HEAD
    split = rows.reshape(heads, HEAD, rows.shape[1])
    return jnp.pad(split, ((0, 0), (0, LANES - HEAD), (0, 0))).reshape(heads * LANES, rows.shape[1])


def on_device(
    layer_input,
    first_gain,
    query_weight,
    key_projection_weight,
    value_projection_weight,
    output_weight,
    second_gain,
    gate_weight,
    up_weight,
    down_weight,
    sequence_lengths,
    cotangent,
):
    row = lax.axis_index("row")
    core = lax.axis_index("col")
    blocks = lax.axis_size("dp")
    row_info = row.reshape(1).astype(jnp.int32)
    half, width = layer_input.shape
    tokens, model = 2 * half, 4 * width
    units = gate_weight.shape[1] // 4
    relative = [jnp.bitwise_xor(row, i) for i in range(4)]

    packed = pack(row_info, query_weight, key_projection_weight, value_projection_weight)
    xs = gather_row(layer_input)
    gains = jnp.stack([first_gain, second_gain])
    gains = jnp.concatenate(exchange_row([gains] * 4), axis=1)
    mixer = jnp.concatenate(exchange_row([packed[i] for i in range(4)]), axis=0)
    w_own = dot(mixer, spread_matrix()).astype(LOW)
    w_oth = other(w_own)

    places, starts = sequence_starts(sequence_lengths[0], tokens)
    cosine, sine = tables(places - starts)
    start_row = starts[None, :]
    first_blocks = starts[::TILE] // TILE
    info = jnp.concatenate([core.reshape(1), first_blocks]).astype(jnp.int32)
    cos_own = lax.dynamic_slice_in_dim(cosine, core * half, half, 0)
    sin_own = lax.dynamic_slice_in_dim(sine, core * half, half, 0)

    first, r1, qkv_own, qkv_oth = project(xs, gains[:1], w_own, w_oth, cos_own, sin_own)
    qkv_got = other(qkv_oth)
    keep, send, attended, lse = attend(info, qkv_own, qkv_got, start_row)
    heads = gather_row(jnp.concatenate([keep, other(send)], axis=1))

    out_w = jnp.concatenate(gather_row(output_weight), axis=1)
    out_w_oth = other(out_w)
    chunk = out_w.shape[0] // 4
    ordered = []
    for i in range(4):
        for matrix in (out_w, out_w_oth):
            ordered.append(lax.dynamic_slice_in_dim(matrix, relative[i] * chunk, chunk, 0))
    out_full = jnp.concatenate(ordered, axis=0)
    out_mine = pad_heads(out_full[: 2 * chunk])

    gate_up = [
        jnp.concatenate(
            [lax.dynamic_slice_in_dim(w, relative[i] * units, units, 1) for w in (gate_weight, up_weight)], axis=1
        )
        for i in range(4)
    ]
    gu_own = jnp.concatenate(exchange_row(gate_up), axis=0)
    gu_oth = other(gu_own)
    down = [lax.dynamic_slice_in_dim(down_weight, relative[i] * units, units, 0) for i in range(4)]
    d_own = jnp.concatenate(exchange_row(down), axis=1)
    d_oth = other(d_own)
    cot = jnp.concatenate(gather_row(cotangent), axis=1)

    second, middle, r2 = middle_of(heads, xs, out_full, gains[1:])
    hidden_own, hidden_oth, back_own, back_oth = feed(second, cot, gu_own, gu_oth, d_own, d_oth)

    parts, sums = partial_sums(NT, back_own, back_oth, gu_own, gu_oth, second)
    second_grad = scatter_row(parts)
    inner = total_row(sums.reshape(8, half // 8)).reshape(half)
    parts, _ = partial_sums(NN, hidden_own, hidden_oth, d_own, d_oth)
    layer_output = (middle + scatter_row(parts)).astype(LOW)

    def both(own, oth):
        return own.astype(LOW), oth.astype(LOW)

    g_own, g_oth = both(dot(second, back_own, TN), dot(second, back_oth, TN))
    c_own, c_oth = both(dot(cot, hidden_own, TN), dot(cot, hidden_oth, TN))
    feed_own = jnp.concatenate([g_own, c_own], axis=1)
    feed_oth = jnp.concatenate([g_oth, c_oth], axis=1)
    feed_sum = (feed_own.astype(F32) + other(feed_oth).astype(F32)).astype(LOW)
    feed_sum = feed_sum.reshape(4, width, 3 * units)
    share = width // blocks

    def finish(take):
        shard = chain_scatter(take, blocks)
        return shard

    feed_shard = finish(lambda s: lax.dynamic_slice_in_dim(feed_sum, s * share, share, 1))
    feed_shard = jnp.stack(exchange_row([feed_shard[i] for i in range(4)]))
    feed_all = chain_gather(feed_shard, blocks).reshape(4, width, 3 * units)
    gate_total, up_total, down_total = feed_place(row_info, feed_all)

    r2 = r2[:, :1]
    middle_grad = (
        cotangent.astype(F32)
        + r2 * second_gain[None, :] * second_grad
        - middle * (r2 * r2 * inner[:, None] / model)
    )
    second_gain_part = jnp.sum(second_grad * middle * r2, axis=0)
    branch = middle_grad.astype(LOW)
    branch_all = jnp.concatenate(gather_row(branch), axis=1)
    heads_grad = dot(branch_all, out_mine, NT).astype(LOW)
    grad_own = heads_grad[:, : 2 * LANES]
    grad_got = other(heads_grad[:, 2 * LANES :])
    back_keep, back_send = attend_back(
        info, qkv_own, qkv_got, grad_own, grad_got, attended, lse, start_row, cosine, sine
    )
    back_got = other(back_send)
    parts, sums = partial_sums(NT, back_keep, back_got, w_own, w_oth, first)
    first_grad = scatter_row(parts)
    inner = total_row(sums.reshape(8, half // 8)).reshape(half)
    r1 = r1[:, :1]
    inputs = layer_input.astype(F32)
    input_gradient = (
        middle_grad + r1 * first_gain[None, :] * first_grad - inputs * (r1 * r1 * inner[:, None] / model)
    )
    first_gain_part = jnp.sum(first_grad * inputs * r1, axis=0)

    spread = spread_matrix()
    flat_own = dot(back_keep, spread, NT).astype(LOW)
    flat_got = dot(back_got, spread, NT).astype(LOW)
    q_own, q_oth = both(dot(first, flat_own, TN), dot(first, flat_got, TN))
    heads_all = jnp.concatenate(heads, axis=1)
    o_all = dot(heads_all, branch, TN).astype(LOW).reshape(4, 2, chunk, width)
    mix_own = jnp.concatenate([q_own.reshape(4, width, 2 * chunk), o_all[:, 0]], axis=1)
    mix_oth = jnp.concatenate([q_oth.reshape(4, width, 2 * chunk), o_all[:, 1]], axis=1)
    mix_sum = (mix_own.astype(F32) + other(mix_oth).astype(F32)).astype(LOW)
    small = chunk // blocks

    def take(s):
        return jnp.concatenate(
            [
                lax.dynamic_slice_in_dim(mix_sum, s * share, share, 1),
                lax.dynamic_slice_in_dim(mix_sum, width + s * small, small, 1),
            ],
            axis=1,
        )

    mix_shard = finish(take)
    mix_shard = jnp.concatenate(
        [jnp.stack(exchange_row([mix_shard[i, :share] for i in range(4)])), mix_shard[:, share:]], axis=1
    )
    mix_all = chain_gather(mix_shard, blocks)
    query_total, key_total, value_total, output_total = mix_place(
        row_info,
        mix_all[:, :, :share].reshape(4, width, 2 * chunk),
        mix_all[:, :, share:].reshape(4, chunk, width),
    )

    gain_parts = jnp.stack([first_gain_part, second_gain_part])
    gain_parts = gain_parts + other(gain_parts)
    gain_total = gain_parts
    for step in range(1, blocks):
        gain_total = gain_total + lax.ppermute(
            gain_parts, "dp", [(i, (i + step) % blocks) for i in range(blocks)]
        )
    return (
        layer_output,
        input_gradient,
        query_total,
        key_total,
        value_total,
        output_total,
        gate_total,
        up_total,
        down_total,
        gain_total[0],
        gain_total[1],
    )


def solution(mesh):
    return jax.shard_map(
        on_device,
        mesh=mesh,
        in_specs=(
            P(("dp", "col"), "row"),
            P("row"),
            P("row", "col"),
            P("row", "col"),
            P("row", "col"),
            P("col", "row"),
            P("row"),
            P("row", "col"),
            P("row", "col"),
            P("col", "row"),
            P("dp", None),
            P(("dp", "col"), "row"),
        ),
        out_specs=(
            P(("dp", "col"), "row"),
            P(("dp", "col"), "row"),
            P("row", "col"),
            P("row", "col"),
            P("row", "col"),
            P("col", "row"),
            P("row", "col"),
            P("row", "col"),
            P("col", "row"),
            P("row"),
            P("row"),
        ),
        check_vma=False,
    )
```

```python
import functools

import jax
import jax.numpy as jnp
from jax import lax
from jax.experimental import pallas as pl
from jax.experimental.pallas import tpu as pltpu
from jax.sharding import PartitionSpec as P

HEAD = 96
LANES = 128
SIDE = 48
TILE = 256
EPSILON = 1e-05
THETA = 100000.0
LOG2E = 1.4426950408889634
FACTOR = HEAD**-0.5
LOW = jnp.bfloat16
F32 = jnp.float32
NN = (((1,), (0,)), ((), ()))
NT = (((1,), (1,)), ((), ()))
TN = (((0,), (0,)), ((), ()))
VMEM_LIMIT = 48 * 1024 * 1024
WEIGHT = 1 / 64


def dot(left, right, dims=NN):
    return lax.dot_general(left, right, dims, preferred_element_type=F32)


def swap(value, step):
    return lax.ppermute(value, "row", [(i, i ^ step) for i in range(4)])


def other(value):
    return lax.ppermute(value, "col", [(0, 1), (1, 0)])


def pair(value, count):
    return lax.ppermute(value, "dp", [(i, i ^ 1) for i in range(count)])


def spread_row(shard):
    return jnp.stack([shard[0]] + [swap(shard[i], i) for i in (1, 2, 3)])


class Live:
    def __init__(self, **values):
        self.values = values

    def __getitem__(self, name):
        return self.values[name]

    def __setitem__(self, name, value):
        self.values[name] = value

    def take(self, *names):
        found = [self.values.pop(name) for name in names]
        return found if len(found) > 1 else found[0]

    def sync(self, *chains, late=()):
        left_out = {name: self.values.pop(name) for name in late}
        moving = [chain.moving() for chain in chains]
        self.values, moving = lax.optimization_barrier((self.values, moving))
        self.values.update(left_out)
        for chain, values in zip(chains, moving):
            chain.landed(values)


def gather_one(live, name):
    live[name + "x"] = swap(live[name], 1)
    live[name + "y"] = swap(live[name], 2)


def gather_two(live, name):
    half = live[name].shape[0] // 2
    live[name + "t"] = swap(live[name + "x"][:half], 2)
    live[name + "b"] = swap(live[name + "y"][half:], 1)


def gathered(live, name):
    return [live[name + end] for end in ("", "x", "y", "t", "b")]


def fetch_one(live, name, pieces, place, count):
    parts = 2 if count % 2 == 0 else 1
    rows = pieces[0].shape[0] // parts
    at = (place % parts) * rows
    live[name] = pieces[0]
    for i in (1, 2, 3):
        live[f"{name}{i}"] = swap(lax.dynamic_slice_in_dim(pieces[i], at, rows, 0), i)


def fetch_two(live, name, count):
    live[name + "m"] = jnp.stack(live.take(*[f"{name}{i}" for i in (1, 2, 3)]))
    if count % 2 == 0:
        live[name + "p"] = pair(live[name + "m"], count)


def fetched(live, name, place, count):
    own, mine = live.take(name, name + "m")
    if count % 2:
        return jnp.concatenate([own[None], mine])
    theirs = live.take(name + "p")
    rows = mine.shape[1]
    bit = place % 2
    zero = jnp.zeros((), jnp.int32)
    result = jnp.zeros((4,) + own.shape, own.dtype)
    result = lax.dynamic_update_slice(result, own[None], (0, 0, 0))
    result = lax.dynamic_update_slice(result, mine, (zero + 1, bit * rows, zero))
    return lax.dynamic_update_slice(result, theirs, (zero + 1, (1 - bit) * rows, zero))


SUMS = ("own_a", "far_a", "near_a", "own_b", "far_b", "near_b")


def scatter_put(live, name, parts):
    for end, part in zip(SUMS, parts):
        live[name + end] = part


def scatter_one(live, name):
    live[name + "got_a"] = swap(live.take(name + "far_a"), 1)
    live[name + "got_b"] = swap(live.take(name + "far_b"), 2)


def scatter_two(live, name):
    got_a, got_b = live[name + "got_a"], live[name + "got_b"]
    width = got_a.shape[1] // 2
    send_a = (live.take(name + "near_a").astype(F32) + got_a[:, width:].astype(F32)).astype(LOW)
    send_b = (live.take(name + "near_b").astype(F32) + got_b[:, width:].astype(F32)).astype(LOW)
    live[name + "last_a"] = swap(send_a, 2)
    live[name + "last_b"] = swap(send_b, 1)


def scattered(live, name):
    halves = []
    for end in ("a", "b"):
        own, got, last = live.take(name + "own_" + end, name + "got_" + end, name + "last_" + end)
        halves.append(own.astype(F32) + got[:, : own.shape[1]].astype(F32) + last.astype(F32))
    return jnp.concatenate(halves, axis=0)


class Scatter:
    def __init__(self, live, name, count, rows=()):
        self.live, self.name, self.count, self.at, self.rows = live, name, count, 1, rows
        self.place = lax.axis_index("dp")

    def part(self, number):
        total = self.live[self.name]
        rows = self.rows if self.rows else (total.shape[1],)
        found, at = [], 0
        for count in rows:
            size = count // self.count
            found.append(lax.dynamic_slice_in_dim(total, at + number * size, size, 1))
            at = at + count
        return found[0] if len(found) == 1 else jnp.concatenate(found, axis=1)

    def step(self):
        count, at, place = self.count, self.at, self.place
        if at >= count:
            return
        up = self.part(jnp.clip(count - at + place, 0, count - 1))
        down = self.part(jnp.clip(place - (count - at), 0, count - 1))
        if at > 1:
            up = (up.astype(F32) + self.up.astype(F32)).astype(LOW)
            down = (down.astype(F32) + self.down.astype(F32)).astype(LOW)
        ups = [(i, i + 1) for i in range(min(at, count - 1))]
        self.up = lax.ppermute(up, "dp", ups)
        self.down = lax.ppermute(down, "dp", [(count - 1 - i, count - 1 - j) for i, j in ups])
        self.at = at + 1

    def moving(self):
        return (self.up, self.down) if self.at > 1 else ()

    def landed(self, values):
        if values:
            self.up, self.down = values

    def finish(self):
        while self.at < self.count:
            self.step()
        own = self.part(self.place)
        if self.count > 1:
            own = (own.astype(F32) + self.up.astype(F32) + self.down.astype(F32)).astype(LOW)
        self.live.take(self.name)
        return own


class Gather:
    def __init__(self, live, name, count):
        self.live, self.name, self.count = live, name, count
        self.place = lax.axis_index("dp")
        self.ups, self.downs = [], []

    def step(self):
        count, at = self.count, len(self.ups) + 1
        if at >= count:
            return
        own = self.live[self.name]
        up, down = self.ups[-1] if self.ups else own, self.downs[-1] if self.downs else own
        ups = [(i, i + 1) for i in range(at - 1, count - 1)]
        self.ups.append(lax.ppermute(up, "dp", ups))
        self.downs.append(lax.ppermute(down, "dp", [(count - 1 - i, count - 1 - j) for i, j in ups]))

    def moving(self):
        return (self.ups, self.downs)

    def landed(self, values):
        self.ups, self.downs = values

    def finish(self):
        while len(self.ups) + 1 < self.count:
            self.step()
        count, place = self.count, self.place
        shard = self.live.take(self.name)
        dims = (shard.shape[0], count) + shard.shape[1:]
        zero = jnp.zeros((), jnp.int32)
        result = jnp.zeros(dims, shard.dtype)

        def put(result, piece, at):
            return lax.dynamic_update_slice(result, piece[:, None], (zero, at) + (zero,) * (len(dims) - 2))

        for at, (up, down) in enumerate(zip(self.ups, self.downs), 1):
            result = put(result, up, jnp.where(place - at >= 0, place - at, place))
            result = put(result, down, jnp.where(place + at < count, place + at, place))
        result = put(result, shard, place)
        return result.reshape(dims[0], count * dims[2], dims[3])


def call(kernel, out_shape, in_specs, out_specs, grid=(), scratch=(), prefetch=0, flops=0, moved=0):
    return pl.pallas_call(
        kernel,
        out_shape=out_shape,
        grid_spec=pltpu.PrefetchScalarGridSpec(
            num_scalar_prefetch=prefetch,
            grid=grid,
            in_specs=in_specs,
            out_specs=out_specs,
            scratch_shapes=list(scratch),
        ),
        compiler_params=pltpu.CompilerParams(vmem_limit_bytes=VMEM_LIMIT),
        cost_estimate=pl.CostEstimate(
            flops=int(flops * WEIGHT), bytes_accessed=int(moved * WEIGHT), transcendentals=0
        ),
    )


def shape(dims, kind=LOW):
    return jax.ShapeDtypeStruct(tuple(dims), kind)


def whole(array):
    rank = len(array.shape)
    return pl.BlockSpec(tuple(array.shape), lambda *_: (0,) * rank)


def bytes_of(*arrays):
    return sum(int(a.size) * a.dtype.itemsize for a in arrays)


def read_pieces(refs, upper):
    x0, x1, x2, top, bottom = refs
    return jnp.concatenate([x0[...], x1[...], x2[...], jnp.where(upper, top[...], bottom[...])], axis=1)


def piece_specs(width, tile, blocks, shift=0):
    halfway = blocks // 2
    plain = pl.BlockSpec((tile, width), lambda b, *_: (b + shift, 0))
    top = pl.BlockSpec((tile, width), lambda b, *_: (jnp.minimum(b + shift, halfway - 1), 0))
    bottom = pl.BlockSpec((tile, width), lambda b, *_: (jnp.maximum(b + shift - halfway, 0), 0))
    return [plain, plain, plain, top, bottom]


def join_kernel(x0, x1, x2, top, bottom, out):
    width, half = x0.shape[1], top.shape[0]
    for i, ref in enumerate((x0, x1, x2)):
        out[:, i * width : (i + 1) * width] = ref[...]
    out[:half, 3 * width :] = top[...]
    out[half:, 3 * width :] = bottom[...]


def join(pieces):
    tokens, width = pieces[0].shape
    out = shape((tokens, 4 * width))
    return call(
        join_kernel, out, [whole(p) for p in pieces], whole(out), grid=(1,), moved=2 * bytes_of(out)
    )(*pieces)


def order_kernel(row_ref, own, oth, full, mine):
    row = row_ref[0]
    features, chunk = own.shape[2], own.shape[1] // 4
    for k in range(4):
        columns = slice(k * features, (k + 1) * features)
        for i in range(4):
            rows = pl.ds(pl.multiple_of(jnp.bitwise_xor(row, i) * chunk, chunk), chunk)
            for s, weight in enumerate((own, oth)):
                at = (2 * i + s) * chunk
                full[at : at + chunk, columns] = weight[k, rows, :]
    mine[...] = jnp.zeros(mine.shape, mine.dtype)
    for h in range(2 * chunk // HEAD):
        mine[h * LANES : h * LANES + HEAD, :] = full[h * HEAD : (h + 1) * HEAD, :]


def order(row, own, oth):
    _, rows, features = own.shape
    full, mine = shape((2 * rows, 4 * features)), shape((2 * rows // 4 // HEAD * LANES, 4 * features))
    return call(
        order_kernel,
        (full, mine),
        [whole(own), whole(oth)],
        (whole(full), whole(mine)),
        grid=(1,),
        prefetch=1,
        moved=2 * bytes_of(full) + bytes_of(mine),
    )(row, own, oth)


def heads_grad_kernel(x0, x1, x2, top, bottom, weight, own, oth):
    upper = pl.program_id(0) < pl.num_programs(0) // 2
    grad = dot(read_pieces((x0, x1, x2, top, bottom), upper), weight[...], NT).astype(LOW)
    own[...] = grad[:, : own.shape[1]]
    oth[...] = grad[:, own.shape[1] :]


def heads_grad_of(pieces, weight):
    tokens, width = pieces[0].shape
    columns = weight.shape[0] // 2
    outs = (shape((tokens, columns)), shape((tokens, columns)))
    rows = pl.BlockSpec((TILE, columns), lambda b: (b, 0))
    return call(
        heads_grad_kernel,
        outs,
        piece_specs(width, TILE, tokens // TILE) + [whole(weight)],
        (rows, rows),
        grid=(tokens // TILE,),
        flops=2 * tokens * 4 * width * weight.shape[0],
        moved=bytes_of(*pieces, weight, *outs),
    )(*pieces, weight)


def pack_kernel(row_ref, q_ref, k_ref, v_ref, out_ref):
    row = row_ref[0]
    query, key = q_ref.shape[1] // 4, k_ref.shape[1] // 4
    for j in range(4):
        at = jnp.bitwise_xor(row, j)
        out_ref[at, :, :query] = q_ref[:, j * query : (j + 1) * query]
        out_ref[at, :, query : query + key] = k_ref[:, j * key : (j + 1) * key]
        out_ref[at, :, query + key :] = v_ref[:, j * key : (j + 1) * key]


def pack(row, query_weight, key_weight, value_weight):
    depth = query_weight.shape[0]
    width = (query_weight.shape[1] + 2 * key_weight.shape[1]) // 4
    out = shape((4, depth, width))
    arrays = (query_weight, key_weight, value_weight)
    return call(
        pack_kernel,
        out,
        [whole(a) for a in arrays],
        whole(out),
        grid=(1,),
        prefetch=1,
        moved=2 * bytes_of(out),
    )(row, *arrays)


def project_kernel(x0, x1, x2, top, bottom, gain, w_own, w_oth, cos, sin, first, r1, own, oth):
    upper = pl.program_id(0) < pl.num_programs(0) // 2
    x = read_pieces((x0, x1, x2, top, bottom), upper).astype(F32)
    inverse = lax.rsqrt(jnp.mean(x * x, axis=1, keepdims=True) + EPSILON)
    normed = (x * inverse * gain[...]).astype(LOW)
    first[...] = normed
    r1[...] = jnp.broadcast_to(inverse, r1.shape)
    for weight, out in ((w_own, own), (w_oth, oth)):
        heads = dot(normed, weight[...])
        for h in range(3):
            part = heads[:, h * LANES : (h + 1) * LANES]
            turned = part * cos[...] + pltpu.roll(part, LANES // 2, 1) * sin[...]
            out[:, h * LANES : (h + 1) * LANES] = turned.astype(LOW)
        out[:, 3 * LANES :] = heads[:, 3 * LANES :].astype(LOW)


def project(xs, gain, w_own, w_oth, cos, sin):
    tokens, width = xs[0].shape
    rows = lambda n: pl.BlockSpec((TILE, n), lambda b: (b, 0))
    outs = (shape((tokens, 4 * width)), shape((tokens, LANES), F32), shape((tokens, 512)), shape((tokens, 512)))
    return call(
        project_kernel,
        outs,
        piece_specs(width, TILE, tokens // TILE)
        + [whole(gain), whole(w_own), whole(w_oth), rows(LANES), rows(LANES)],
        tuple(rows(o.shape[1]) for o in outs),
        grid=(tokens // TILE,),
        flops=2 * tokens * 4 * width * 1024,
        moved=bytes_of(*xs, w_own, w_oth, *outs),
    )(*xs, gain, w_own, w_oth, cos, sin)


def stack_heads(ref, rows):
    return jnp.concatenate([ref[rows, :LANES], ref[rows, LANES : 2 * LANES]], axis=0)


def block_limits(start_ref, block):
    rows = pl.ds(pl.multiple_of(block * TILE, TILE), TILE)
    start = start_ref[:, rows]
    query = block * TILE + lax.broadcasted_iota(jnp.int32, (1, TILE), 1)
    return jnp.concatenate([start, start], axis=1), jnp.concatenate([query, query], axis=1)


def allowed_keys(number, start, query):
    key = number * TILE + lax.broadcasted_iota(jnp.int32, (TILE, 2 * TILE), 0)
    return (key >= start) & (key <= query)


def attend_kernel(info, own, oth, start_ref, keep, send, out, lse, full, values, top, total, acc):
    block = pl.program_id(0)
    core = info[0]
    half = own.shape[0]

    @pl.when(block == 0)
    def _():
        full[pl.ds(pl.multiple_of(core * half, half), half), :] = own[...]
        full[pl.ds(pl.multiple_of((1 - core) * half, half), half), :] = oth[...]
        values[...] = full[:, 3 * LANES :].T

    rows = pl.ds(pl.multiple_of(block * TILE, TILE), TILE)
    query = stack_heads(full, rows)
    start, place = block_limits(start_ref, block)
    top[...] = jnp.full(top.shape, -1e30, F32)
    total[...] = jnp.zeros(total.shape, F32)
    acc[...] = jnp.zeros(acc.shape, F32)

    def step(number, _):
        keys = pl.ds(pl.multiple_of(number * TILE, TILE), TILE)
        scores = dot(full[keys, 2 * LANES : 3 * LANES], query, NT) * (FACTOR * LOG2E)
        scores = jnp.where(allowed_keys(number, start, place), scores, -1e30)
        before = top[...]
        now = jnp.maximum(before, jnp.max(scores, axis=0, keepdims=True))
        weight = jnp.exp2(scores - now)
        scale = jnp.exp2(before - now)
        top[...] = now
        total[...] = total[...] * scale + jnp.sum(weight, axis=0, keepdims=True)
        acc[...] = acc[...] * scale + dot(values[:, keys], weight.astype(LOW))
        return 0

    lax.fori_loop(info[1 + block], block + 1, step, 0)
    lse[...] = top[...] + jnp.log2(total[...])
    result = (acc[...] / total[...]).T.astype(LOW)
    out[:, :LANES] = result[:TILE]
    out[:, LANES:] = result[TILE:]
    mine = (block // (half // TILE)) == core
    for target, wanted in ((keep, mine), (send, jnp.logical_not(mine))):

        @pl.when(wanted)
        def _(target=target):
            target[:, :HEAD] = result[:TILE, :HEAD]
            target[:, HEAD:] = result[TILE:, :HEAD]


def attend(info, own, oth, start):
    half = own.shape[0]
    tokens = 2 * half
    per_half = half // TILE
    outs = (
        shape((half, 2 * HEAD)),
        shape((half, 2 * HEAD)),
        shape((tokens, 2 * LANES)),
        shape((1, 2 * tokens), F32),
    )
    return call(
        attend_kernel,
        outs,
        [whole(own), whole(oth), whole(start)],
        (
            pl.BlockSpec((TILE, 2 * HEAD), lambda b, s: (jnp.clip(b - s[0] * per_half, 0, per_half - 1), 0)),
            pl.BlockSpec((TILE, 2 * HEAD), lambda b, s: (jnp.clip(b - (1 - s[0]) * per_half, 0, per_half - 1), 0)),
            pl.BlockSpec((TILE, 2 * LANES), lambda b, s: (b, 0)),
            pl.BlockSpec((1, 2 * TILE), lambda b, s: (0, b)),
        ),
        grid=(tokens // TILE,),
        scratch=(
            pltpu.VMEM((tokens, 4 * LANES), LOW),
            pltpu.VMEM((LANES, tokens), LOW),
            pltpu.VMEM((1, 2 * TILE), F32),
            pltpu.VMEM((1, 2 * TILE), F32),
            pltpu.VMEM((LANES, 2 * TILE), F32),
        ),
        prefetch=1,
        flops=4 * tokens * tokens * LANES * 2,
        moved=bytes_of(own, oth, *outs),
    )(info, own, oth, start)


def turn_back(part, cos, sin):
    return part * cos - pltpu.roll(part, LANES // 2, 1) * sin


def attend_back_kernel(
    info, own, oth, g_own, g_oth, out, lse, start_ref, cos, sin,
    keep, send, full, grads, keys_t, d_keys, d_values, d_query, result,
):
    block = pl.program_id(0)
    core = info[0]
    half = own.shape[0]

    @pl.when(block == 0)
    def _():
        mine = pl.ds(pl.multiple_of(core * half, half), half)
        theirs = pl.ds(pl.multiple_of((1 - core) * half, half), half)
        full[mine, :] = own[...]
        full[theirs, :] = oth[...]
        grads[mine, :] = g_own[...]
        grads[theirs, :] = g_oth[...]
        keys_t[...] = full[:, 2 * LANES : 3 * LANES].T
        d_keys[...] = jnp.zeros(d_keys.shape, F32)
        d_values[...] = jnp.zeros(d_values.shape, F32)

    rows = pl.ds(pl.multiple_of(block * TILE, TILE), TILE)
    query = stack_heads(full, rows)
    grad = stack_heads(grads, rows)
    reply = stack_heads(out, slice(None))
    start, place = block_limits(start_ref, block)
    level = lse[...]
    delta = jnp.sum((grad.astype(F32) * reply.astype(F32)).T, axis=0, keepdims=True)
    d_query[...] = jnp.zeros(d_query.shape, F32)

    def step(number, _):
        keys = pl.ds(pl.multiple_of(number * TILE, TILE), TILE)
        scores = dot(full[keys, 2 * LANES : 3 * LANES], query, NT) * (FACTOR * LOG2E)
        scores = jnp.where(allowed_keys(number, start, place), scores, -1e30)
        weight = jnp.exp2(scores - level)
        pressure = dot(full[keys, 3 * LANES :], grad, NT)
        slope = (weight * (pressure - delta) * FACTOR).astype(LOW)
        d_values[keys, :] += dot(weight.astype(LOW), grad)
        d_keys[keys, :] += dot(slope, query)
        d_query[...] += dot(keys_t[:, keys], slope)
        return 0

    lax.fori_loop(info[1 + block], block + 1, step, 0)
    turned = d_query[...].T
    for h in range(2):
        part = turned[h * TILE : (h + 1) * TILE]
        result[rows, h * LANES : (h + 1) * LANES] = turn_back(part, cos[rows, :], sin[rows, :]).astype(LOW)

    @pl.when(block == pl.num_programs(0) - 1)
    def _():
        mine = pl.ds(pl.multiple_of(core * half, half), half)
        theirs = pl.ds(pl.multiple_of((1 - core) * half, half), half)
        for target, which in ((keep, mine), (send, theirs)):
            target[:, : 2 * LANES] = result[which, :]
            target[:, 2 * LANES : 3 * LANES] = turn_back(
                d_keys[which, :], cos[which, :], sin[which, :]
            ).astype(LOW)
            target[:, 3 * LANES :] = d_values[which, :].astype(LOW)


def attend_back(info, own, oth, g_own, g_oth, out, lse, start, cos, sin):
    half = own.shape[0]
    tokens = 2 * half
    outs = (shape((half, 4 * LANES)), shape((half, 4 * LANES)))
    return call(
        attend_back_kernel,
        outs,
        [
            whole(own),
            whole(oth),
            whole(g_own),
            whole(g_oth),
            pl.BlockSpec((TILE, 2 * LANES), lambda b, s: (b, 0)),
            pl.BlockSpec((1, 2 * TILE), lambda b, s: (0, b)),
            whole(start),
            whole(cos),
            whole(sin),
        ],
        tuple(whole(o) for o in outs),
        grid=(tokens // TILE,),
        scratch=(
            pltpu.VMEM((tokens, 4 * LANES), LOW),
            pltpu.VMEM((tokens, 2 * LANES), LOW),
            pltpu.VMEM((LANES, tokens), LOW),
            pltpu.VMEM((tokens, LANES), F32),
            pltpu.VMEM((tokens, LANES), F32),
            pltpu.VMEM((LANES, 2 * TILE), F32),
            pltpu.VMEM((tokens, 2 * LANES), LOW),
        ),
        prefetch=1,
        flops=10 * tokens * tokens * LANES * 2,
        moved=bytes_of(own, oth, g_own, g_oth, out, *outs),
    )(info, own, oth, g_own, g_oth, out, lse, start, cos, sin)


def middle_kernel(*refs):
    weight, gain, second, middle, r2, joined = refs[10:]
    upper = pl.program_id(0) < pl.num_programs(0) // 2
    heads = read_pieces(refs[:5], upper)
    joined[...] = heads
    x = read_pieces(refs[5:10], upper).astype(F32)
    value = x + dot(heads, weight[...])
    inverse = lax.rsqrt(jnp.mean(value * value, axis=1, keepdims=True) + EPSILON)
    second[...] = (value * inverse * gain[...]).astype(LOW)
    middle[...] = value[:, : middle.shape[1]]
    r2[...] = jnp.broadcast_to(inverse, r2.shape)


def middle_of(heads, xs, weight, gain):
    tokens, width = xs[0].shape
    rows = lambda n: pl.BlockSpec((TILE, n), lambda b: (b, 0))
    outs = (
        shape((tokens, 4 * width)),
        shape((tokens, width), F32),
        shape((tokens, LANES), F32),
        shape((tokens, 4 * width)),
    )
    return call(
        middle_kernel,
        outs,
        piece_specs(width, TILE, tokens // TILE) * 2 + [whole(weight), whole(gain)],
        tuple(rows(o.shape[1]) for o in outs),
        grid=(tokens // TILE,),
        flops=2 * tokens * 16 * width * width,
        moved=bytes_of(*heads, *xs, weight, *outs),
    )(*heads, *xs, weight, gain)


def feed_kernel(second, cot, g_own, u_own, g_oth, u_oth, d_own, d_oth, hidden_own, hidden_oth, back_own, back_oth):
    block = pl.program_id(0)
    per = pl.num_programs(0) // 2
    tokens, units = hidden_own.shape
    width = d_own.shape[2]

    def body(gate_w, up_w, down_w, hidden, back, at):
        down = jnp.concatenate([down_w[i] for i in range(4)], axis=1)
        near = pl.ds(pl.multiple_of(at, TILE), TILE)
        far = pl.ds(pl.multiple_of(units + at, TILE), TILE)
        for m in range(0, tokens, TILE):
            rows = slice(m, m + TILE)
            gate = dot(second[rows, :], gate_w[...])
            up = dot(second[rows, :], up_w[...])
            hidden_grad = dot(cot[rows, :], down, NT)
            share = 1.0 / (1.0 + jnp.exp(-gate))
            silu = gate * share
            hidden[rows, near] = (silu * up).astype(LOW)
            back[rows, near] = (hidden_grad * up * share * (1.0 + gate * (1.0 - share))).astype(LOW)
            back[rows, far] = (hidden_grad * silu).astype(LOW)

    @pl.when(block < per)
    def _():
        body(g_own, u_own, d_own, hidden_own, back_own, block * TILE)

    @pl.when(block >= per)
    def _():
        body(g_oth, u_oth, d_oth, hidden_oth, back_oth, (block - per) * TILE)


def feed(second, cot, gu_own, gu_oth, d_own, d_oth):
    tokens, model = second.shape
    units = gu_own.shape[1] // 2
    per = units // TILE
    early = lambda b: jnp.minimum(b, per - 1)
    late = lambda b: jnp.maximum(b - per, 0)
    column = lambda at: pl.BlockSpec((model, TILE), lambda b: (0, at(b)))
    down = lambda at: pl.BlockSpec((4, TILE, model // 4), lambda b: (0, at(b), 0))
    outs = (shape((tokens, units)), shape((tokens, units)), shape((tokens, 2 * units)), shape((tokens, 2 * units)))
    return call(
        feed_kernel,
        outs,
        [
            whole(second),
            whole(cot),
            column(early),
            column(lambda b: per + early(b)),
            column(late),
            column(lambda b: per + late(b)),
            down(early),
            down(late),
        ],
        tuple(whole(o) for o in outs),
        grid=(2 * per,),
        flops=12 * tokens * model * units,
        moved=bytes_of(second, cot, gu_own, gu_oth, d_own, d_oth, *outs),
    )(second, cot, gu_own, gu_own, gu_oth, gu_oth, d_own, d_oth)


def partial_kernel(which, blocked, a_own, a_oth, w_own, w_oth, *rest):
    if len(rest) == 5:
        against, own, far, near, sums = rest
    else:
        own, far, near = rest
    width = own.shape[1]
    total = 0.0
    left, right = a_own[...], a_oth[...]
    for k, target in enumerate((own, far if not which else near, near if not which else far, far)):
        columns = slice(k * width, (k + 1) * width)
        if blocked:
            value = dot(left, w_own[k]) + dot(right, w_oth[k])
        else:
            value = dot(left, w_own[columns, :], NT) + dot(right, w_oth[columns, :], NT)
        if len(rest) == 5:
            total = total + jnp.sum(value * against[:, columns].astype(F32), axis=1, keepdims=True)
        if target is far:
            place = width if k == 3 else 0
            far[:, place : place + width] = value.astype(LOW)
        else:
            target[...] = value.astype(LOW)
    if len(rest) == 5:
        sums[...] = jnp.broadcast_to(total, sums.shape)


def partial_half(which, blocked, a_own, a_oth, w_own, w_oth, against):
    tokens, depth = a_own.shape
    model = 4 * w_own.shape[2] if blocked else w_own.shape[0]
    half, width = tokens // 2, model // 4
    blocks = half // TILE
    read = lambda n: pl.BlockSpec((TILE, n), lambda b: (which * blocks + b, 0))
    write = lambda n: pl.BlockSpec((TILE, n), lambda b: (b, 0))
    outs = [shape((half, width)), shape((half, 2 * width)), shape((half, width))]
    args = [a_own, a_oth, w_own, w_oth]
    specs = [read(depth), read(depth), whole(w_own), whole(w_oth)]
    if against is not None:
        outs.append(shape((half, LANES), F32))
        args.append(against)
        specs.append(read(model))
    return call(
        functools.partial(partial_kernel, which, blocked),
        tuple(outs),
        specs,
        tuple(write(o.shape[1]) for o in outs),
        grid=(blocks,),
        flops=4 * half * depth * model,
        moved=bytes_of(w_own, w_oth, *outs) + half * 4 * depth,
    )(*args)


def partial_sums(blocked, a_own, a_oth, w_own, w_oth, against=None):
    first = partial_half(0, blocked, a_own, a_oth, w_own, w_oth, against)
    second = partial_half(1, blocked, a_own, a_oth, w_own, w_oth, against)
    sums = None if against is None else jnp.concatenate([first[3][:, 0], second[3][:, 0]])
    return (first[0], first[1], first[2], second[0], second[1], second[2]), sums


def feed_grads_kernel(second, cot, back, hidden, out):
    double, share = back.shape[1], out.shape[2]
    for columns, left, right in ((slice(0, double), second, back), (slice(double, None), cot, hidden)):
        value = dot(left[...], right[...], TN).astype(LOW)
        for k in range(out.shape[0]):
            out[k, 0, :, columns] = value[k * share : (k + 1) * share]


def feed_grads(second, cot, back, hidden, count):
    tokens, model = second.shape
    width = model // 4
    out = shape((count, 4, width // count, back.shape[1] + hidden.shape[1]))
    block = pl.BlockSpec((tokens, width), lambda i: (0, i))
    return call(
        feed_grads_kernel,
        out,
        [block, block, whole(back), whole(hidden)],
        pl.BlockSpec((count, 1) + out.shape[2:], lambda i: (0, i, 0, 0)),
        grid=(4,),
        flops=2 * tokens * model * out.shape[3],
        moved=bytes_of(second, cot, back, hidden, out),
    )(second, cot, back, hidden)


def mix_grads_kernel(which, first, heads, back, branch, spread, out, flat):
    @pl.when(pl.program_id(0) == 0)
    def _():
        flat[...] = dot(back[...], spread[...], NT).astype(LOW)

    width, chunk = first.shape[1], heads.shape[1] // 2
    out[0, :width, :] = dot(first[...], flat[...], TN).astype(LOW)
    out[0, width:, :] = dot(heads[:, which * chunk : (which + 1) * chunk], branch[...], TN).astype(LOW)


def mix_grads(which, first, heads, back, branch, spread):
    tokens, model = first.shape
    width = model // 4
    out = shape((4, width + width // 2, width))
    block = pl.BlockSpec((tokens, width), lambda i: (0, i))
    return call(
        functools.partial(mix_grads_kernel, which),
        out,
        [block, block, whole(back), whole(branch), whole(spread)],
        pl.BlockSpec((1,) + out.shape[1:], lambda i: (i, 0, 0)),
        grid=(4,),
        scratch=(pltpu.VMEM((tokens, spread.shape[0]), LOW),),
        flops=2 * tokens * model * out.shape[1],
        moved=bytes_of(first, heads, back, branch, out),
    )(first, heads, back, branch, spread)


def feed_place_kernel(row_ref, piece, gate, up, down):
    units, share = gate.shape[1], piece.shape[2]
    for k in range(piece.shape[0]):
        rows = slice(k * share, (k + 1) * share)
        gate[rows, :] = piece[k, 0, :, :units].astype(F32)
        up[rows, :] = piece[k, 0, :, units : 2 * units].astype(F32)
    down[...] = jnp.concatenate(
        [piece[k, 0, :, 2 * units :].astype(F32) for k in range(piece.shape[0])], axis=0
    ).T


def feed_place(row, pieces):
    count, _, share, triple = pieces.shape
    units, depth = triple // 3, count * share
    outs = (shape((depth, 4 * units), F32), shape((depth, 4 * units), F32), shape((4 * units, depth), F32))
    return call(
        feed_place_kernel,
        outs,
        [pl.BlockSpec((count, 1, share, triple), lambda j, s: (0, jnp.bitwise_xor(s[0], j), 0, 0))],
        (
            pl.BlockSpec((depth, units), lambda j, s: (0, j)),
            pl.BlockSpec((depth, units), lambda j, s: (0, j)),
            pl.BlockSpec((units, depth), lambda j, s: (j, 0)),
        ),
        grid=(4,),
        prefetch=1,
        moved=bytes_of(pieces, *outs),
    )(row, pieces)


def mix_place_kernel(row_ref, pieces, heads, query, key, value, output):
    row = row_ref[0]
    wide, narrow = query.shape[1] // 4, key.shape[1] // 4
    for j in range(4):
        piece = pieces[jnp.bitwise_xor(row, j)].astype(F32)
        query[:, j * wide : (j + 1) * wide] = piece[:, :wide]
        key[:, j * narrow : (j + 1) * narrow] = piece[:, wide : wide + narrow]
        value[:, j * narrow : (j + 1) * narrow] = piece[:, wide + narrow :]
        output[j * wide : (j + 1) * wide, :] = heads[jnp.bitwise_xor(row, j)].astype(F32)


def mix_place(row, pieces, heads):
    _, depth, width = pieces.shape
    wide, narrow = width // 2, width // 4
    outs = (
        shape((depth, 4 * wide), F32),
        shape((depth, 4 * narrow), F32),
        shape((depth, 4 * narrow), F32),
        shape((4 * wide, depth), F32),
    )
    return call(
        mix_place_kernel,
        outs,
        [whole(pieces), whole(heads)],
        tuple(whole(o) for o in outs),
        grid=(1,),
        prefetch=1,
        moved=bytes_of(pieces, heads, *outs),
    )(row, pieces, heads)


def sequence_starts(lengths, tokens):
    places = jnp.arange(tokens, dtype=jnp.int32)
    starts = jnp.zeros((tokens,), jnp.int32)
    end = jnp.zeros((), jnp.int32)
    for k in range(lengths.shape[0]):
        end = end + lengths[k]
        starts = jnp.where(places >= end, end, starts)
    return places, starts


def tables(places):
    lane = jnp.arange(LANES, dtype=jnp.int32)
    entry = lane % (LANES // 2)
    frequency = THETA ** (-2.0 * entry.astype(F32) / HEAD)
    real = entry < SIDE
    angles = places.astype(F32)[:, None] * frequency[None, :]
    cosine = jnp.where(real[None, :], jnp.cos(angles), 0.0)
    sign = jnp.where(lane < LANES // 2, -1.0, 1.0)
    sine = jnp.where(real[None, :], jnp.sin(angles) * sign[None, :], 0.0)
    return cosine, sine


def spread_matrix():
    source = jnp.arange(4 * HEAD, dtype=jnp.int32)
    head, entry = source // HEAD, source % HEAD
    inside = jnp.where((head < 3) & (entry >= SIDE), entry - SIDE + LANES // 2, entry)
    target = head * LANES + inside
    return (target[:, None] == jnp.arange(4 * LANES, dtype=jnp.int32)[None, :]).astype(LOW)


def on_device(
    layer_input,
    first_gain,
    query_weight,
    key_projection_weight,
    value_projection_weight,
    output_weight,
    second_gain,
    gate_weight,
    up_weight,
    down_weight,
    sequence_lengths,
    cotangent,
):
    row = lax.axis_index("row")
    core = lax.axis_index("col")
    place = lax.axis_index("dp")
    blocks = lax.axis_size("dp")
    row_info = row.reshape(1).astype(jnp.int32)
    half, width = layer_input.shape
    tokens, model = 2 * half, 4 * width
    units = gate_weight.shape[1] // 4
    rows = output_weight.shape[0]
    chunk = rows // 4
    relative = [jnp.bitwise_xor(row, i) for i in range(4)]
    live = Live(
        x=layer_input,
        cot=cotangent,
        g=jnp.stack([first_gain, second_gain]),
        gate=gate_weight,
        up=up_weight,
        down=down_weight,
        out=output_weight,
    )

    gather_one(live, "x")
    packed = pack(row_info, query_weight, key_projection_weight, value_projection_weight)
    fetch_one(live, "mix", [packed[i] for i in range(4)], place, blocks)
    live["g"] = jnp.concatenate([live["g"], swap(live["g"], 1)], axis=1)
    live.sync()

    gather_two(live, "x")
    fetch_two(live, "mix", blocks)
    live["gains"] = jnp.concatenate([live["g"], swap(live.take("g"), 2)], axis=1)
    places, starts = sequence_starts(sequence_lengths[0], tokens)
    live["cos"], live["sin"] = tables(places - starts)
    live["start"] = starts[None, :]
    live["info"] = jnp.concatenate([core.reshape(1), starts[::TILE] // TILE]).astype(jnp.int32)
    gate, up, down, out = live.take("gate", "up", "down", "out")
    for i in range(4):
        downs = lax.dynamic_slice_in_dim(down, relative[i] * units, units, 0)
        live[f"odp{i}"] = jnp.concatenate([out, downs], axis=0)
        live[f"gup{i}"] = jnp.concatenate(
            [lax.dynamic_slice_in_dim(w, relative[i] * units, units, 1) for w in (gate, up)], axis=1
        )
    spread = spread_matrix()
    live.sync()

    fetch_one(live, "od", live.take(*[f"odp{i}" for i in range(4)]), place, blocks)
    mixer = fetched(live, "mix", place, blocks).reshape(model, 4 * HEAD)
    live["w_own"] = dot(mixer, spread).astype(LOW)
    live["w_oth"] = other(live["w_own"])
    cos_own = lax.dynamic_slice_in_dim(live["cos"], core * half, half, 0)
    sin_own = lax.dynamic_slice_in_dim(live["sin"], core * half, half, 0)
    live["first"], live["r1"], live["qkv"], live["qkv_send"] = project(
        gathered(live, "x"), live["gains"][:1], live["w_own"], live["w_oth"], cos_own, sin_own
    )
    live.sync()
    fetch_one(live, "gu", live.take(*[f"gup{i}" for i in range(4)]), place, blocks)
    fetch_two(live, "od", blocks)
    live["qkv_got"] = other(live.take("qkv_send"))
    live["keep"], live["send"], live["attended"], live["lse"] = attend(
        live["info"], live["qkv"], live["qkv_got"], live["start"]
    )
    coming = ("odp",) if blocks % 2 == 0 else ()
    live.sync(late=coming)
    keep, send = live.take("keep", "send")
    live["heads"] = jnp.concatenate([keep, other(send)], axis=1)
    live.sync(late=coming)

    gather_one(live, "heads")
    gather_one(live, "cot")
    fetch_two(live, "gu", blocks)
    od_own = fetched(live, "od", place, blocks)
    od_oth = other(od_own)
    live["out_full"], live["out_mine"] = order(row_info, od_own[:, :rows], od_oth[:, :rows])
    live["d_own"], live["d_oth"] = od_own[:, rows:], od_oth[:, rows:]
    live.sync()

    gather_two(live, "heads")
    gather_two(live, "cot")
    live["gu_own"] = fetched(live, "gu", place, blocks).reshape(model, 2 * units)
    live["gu_oth"] = other(live["gu_own"])
    live.sync()

    live["second"], live["middle"], live["r2"], live["heads_all"] = middle_of(
        gathered(live, "heads"), gathered(live, "x"), live["out_full"], live["gains"][1:]
    )
    live["cot_all"] = join(gathered(live, "cot"))

    live["hid_own"], live["hid_oth"], live["back_own"], live["back_oth"] = feed(
        live["second"], live["cot_all"], live["gu_own"], live["gu_oth"], live["d_own"], live["d_oth"]
    )
    parts, sums = partial_sums(
        False, live["back_own"], live["back_oth"], live["gu_own"], live["gu_oth"], live["second"]
    )
    scatter_put(live, "sg", parts)
    live["sums"] = sums.reshape(8, half // 8)
    live.sync()

    def added(own, got):
        return (own.astype(F32) + got.astype(F32)).astype(LOW)

    scatter_one(live, "sg")
    live["sums"] = live["sums"] + swap(live["sums"], 1)
    live["feed_send"] = feed_grads(live["second"], live["cot_all"], live["back_oth"], live["hid_oth"], blocks)
    live["feed"] = feed_grads(live["second"], live["cot_all"], live["back_own"], live["hid_own"], blocks)
    live.sync()

    scatter_two(live, "sg")
    live["inner"] = live["sums"] + swap(live.take("sums"), 2)
    live["feed"] = added(live["feed"], other(live.take("feed_send")))
    live.sync()

    feed_sum = lax.psum_scatter(live.take("feed"), "dp", scatter_dimension=0)
    second_grad = scattered(live, "sg")
    inner = live.take("inner").reshape(half)
    r2, middle = live["r2"][:, :1], live["middle"]
    live["middle_grad"] = (
        cotangent.astype(F32)
        + r2 * second_gain[None, :] * second_grad
        - middle * (r2 * r2 * inner[:, None] / model)
    )
    live["gain2"] = jnp.sum(second_grad * middle * r2, axis=0)
    live["branch"] = live["middle_grad"].astype(LOW)
    gather_one(live, "branch")
    parts, _ = partial_sums(True, live["hid_own"], live["hid_oth"], live["d_own"], live["d_oth"])
    scatter_put(live, "fo", parts)
    live.sync()

    gather_two(live, "branch")
    live.sync()
    live["grad"], live["grad_send"] = heads_grad_of(gathered(live, "branch"), live["out_mine"])
    live["grad_got"] = other(live.take("grad_send"))
    live.sync()

    scatter_one(live, "fo")
    live["bk"], live["bs"] = attend_back(
        live["info"], live["qkv"], live["qkv_got"], live["grad"], live["grad_got"],
        live["attended"], live["lse"], live["start"], live["cos"], live["sin"],
    )
    live["feed"] = feed_sum
    live.sync()

    live["feed"] = spread_row(live["feed"])
    scatter_two(live, "fo")
    live["bg"] = other(live.take("bs"))
    live["mix_send"] = mix_grads(1, live["first"], live["heads_all"], live["bg"], live["branch"], spread)
    live["mix"] = mix_grads(0, live["first"], live["heads_all"], live["bk"], live["branch"], spread)
    live.sync()
    feeds = lax.all_gather(live.take("feed"), "dp", axis=0)
    live["mix"] = added(live["mix"], other(live.take("mix_send")))
    parts, sums = partial_sums(False, live["bk"], live["bg"], live["w_own"], live["w_oth"], live["first"])
    scatter_put(live, "fg", parts)
    live["sums"] = sums.reshape(8, half // 8)
    live.sync()

    scatter_one(live, "fg")
    live["sums"] = live["sums"] + swap(live["sums"], 1)
    layer_output = (live["middle"] + scattered(live, "fo")).astype(LOW)
    share = width // blocks
    mixes = Scatter(live, "mix", blocks, (width, chunk))
    mixes.step()
    live.sync(mixes)

    scatter_two(live, "fg")
    live["inner"] = live["sums"] + swap(live.take("sums"), 2)
    mixes.step()
    live.sync(mixes)

    mixes.step()
    first_grad = scattered(live, "fg")
    inner = live.take("inner").reshape(half)
    r1 = live["r1"][:, :1]
    inputs = layer_input.astype(F32)
    input_gradient = (
        live["middle_grad"]
        + r1 * first_gain[None, :] * first_grad
        - inputs * (r1 * r1 * inner[:, None] / model)
    )
    gains = jnp.stack([jnp.sum(first_grad * inputs * r1, axis=0), live["gain2"]])
    live["gains"] = gains + other(gains)
    live.sync(mixes)

    shard = mixes.finish()
    turned = spread_row(shard[:, :share])
    live["mix"] = jnp.concatenate([turned, shard[:, share:]], axis=1)
    live.sync()
    mixes = Gather(live, "mix", blocks)
    mixes.step()
    gain_total = live["gains"]
    for step in range(1, blocks):
        gain_total = gain_total + lax.ppermute(
            live["gains"], "dp", [(i, (i + step) % blocks) for i in range(blocks)]
        )
    live["gains"] = gain_total
    live.sync(mixes)
    mixes.step()
    live.sync(mixes)
    mixes.step()
    gate_total, up_total, down_total = feed_place(row_info, feeds)
    mixes = mixes.finish().reshape(4, blocks, share + chunk // blocks, width)
    query_total, key_total, value_total, output_total = mix_place(
        row_info, mixes[:, :, :share].reshape(4, width, width), mixes[:, :, share:].reshape(4, chunk, width)
    )
    gain_total = live["gains"]
    return (
        layer_output,
        input_gradient,
        query_total,
        key_total,
        value_total,
        output_total,
        gate_total,
        up_total,
        down_total,
        gain_total[0],
        gain_total[1],
    )


def solution(mesh):
    return jax.shard_map(
        on_device,
        mesh=mesh,
        in_specs=(
            P(("dp", "col"), "row"),
            P("row"),
            P("row", "col"),
            P("row", "col"),
            P("row", "col"),
            P("col", "row"),
            P("row"),
            P("row", "col"),
            P("row", "col"),
            P("col", "row"),
            P("dp", None),
            P(("dp", "col"), "row"),
        ),
        out_specs=(
            P(("dp", "col"), "row"),
            P(("dp", "col"), "row"),
            P("row", "col"),
            P("row", "col"),
            P("row", "col"),
            P("col", "row"),
            P("row", "col"),
            P("row", "col"),
            P("col", "row"),
            P("row"),
            P("row"),
        ),
        check_vma=False,
    )
```

```python
import functools

import jax
import jax.numpy as jnp
from jax import lax
from jax.experimental import pallas as pl
from jax.experimental.pallas import tpu as pltpu
from jax.sharding import PartitionSpec as P

HEAD = 96
LANES = 128
SIDE = 48
TILE = 256
EPSILON = 1e-05
THETA = 100000.0
LOG2E = 1.4426950408889634
FACTOR = HEAD**-0.5
LOW = jnp.bfloat16
F32 = jnp.float32
NN = (((1,), (0,)), ((), ()))
NT = (((1,), (1,)), ((), ()))
TN = (((0,), (0,)), ((), ()))
VMEM_LIMIT = 48 * 1024 * 1024
WEIGHT = 1 / 64


def dot(left, right, dims=NN):
    return lax.dot_general(left, right, dims, preferred_element_type=F32)


def swap(value, step):
    return lax.ppermute(value, "row", [(i, i ^ step) for i in range(4)])


def other(value):
    return lax.ppermute(value, "col", [(0, 1), (1, 0)])


def pair(value, count):
    return lax.ppermute(value, "dp", [(i, i ^ 1) for i in range(count)])


def spread_row(shard):
    return jnp.stack([shard[0]] + [swap(shard[i], i) for i in (1, 2, 3)])


class Live:
    def sync(self):
        self.__dict__.update(lax.optimization_barrier(dict(self.__dict__)))


def ready(*values):
    return lax.optimization_barrier(values)


def gather_one(value):
    return [value, swap(value, 1), swap(value, 2)]


def gather_halves(found):
    half = found[0].shape[0] // 2
    return found[1][:half], found[2][half:]


def gather_two(found, halves):
    return found + [swap(halves[0], 2), swap(halves[1], 1)]


def fetch_halves(pieces, place, count):
    parts = 2 if count % 2 == 0 else 1
    rows = pieces[0].shape[0] // parts
    at = (place % parts) * rows
    return [lax.dynamic_slice_in_dim(pieces[i], at, rows, 0) for i in (1, 2, 3)]


def fetch_one(halves):
    return [swap(half, i) for i, half in enumerate(halves, 1)]


def fetch_two(mine, count):
    return pair(mine, count) if count % 2 == 0 else ()


def fetched(own, mine, theirs, place):
    if isinstance(theirs, tuple):
        return jnp.concatenate([own[None], mine])
    rows = mine.shape[1]
    bit = place % 2
    zero = jnp.zeros((), jnp.int32)
    result = jnp.zeros((4,) + own.shape, own.dtype)
    result = lax.dynamic_update_slice(result, own[None], (0, 0, 0))
    result = lax.dynamic_update_slice(result, mine, (zero + 1, bit * rows, zero))
    return lax.dynamic_update_slice(result, theirs, (zero + 1, (1 - bit) * rows, zero))


def scatter_one(parts):
    own, far_a, near_a, far_b, near_b = parts
    return own, swap(far_a, 1), near_a, swap(far_b, 2), near_b


def scatter_halves(parts):
    own, got_a, near_a, got_b, near_b = parts
    width = own.shape[1]
    send_a = (near_a.astype(F32) + got_a[:, width:].astype(F32)).astype(LOW)
    send_b = (near_b.astype(F32) + got_b[:, width:].astype(F32)).astype(LOW)
    return send_a, send_b


def scatter_two(parts, halves):
    own, got_a, _, got_b, _ = parts
    return own, got_a, swap(halves[0], 2), got_b, swap(halves[1], 1)


def scattered(parts):
    own, got_a, last_a, got_b, last_b = parts
    width, half = own.shape[1], got_a.shape[0]
    upper = own[:half].astype(F32) + got_a[:, :width].astype(F32) + last_a.astype(F32)
    lower = own[half:].astype(F32) + got_b[:, :width].astype(F32) + last_b.astype(F32)
    return jnp.concatenate([upper, lower], axis=0)


def shard_of(total, rows, number, count):
    found, at = [], 0
    for part in rows:
        size = part // count
        found.append(lax.dynamic_slice_in_dim(total, at + number * size, size, 1))
        at = at + part
    return found[0] if len(found) == 1 else jnp.concatenate(found, axis=1)


def turn(value, step, count):
    return lax.ppermute(value, "dp", [(i, (i + step) % count) for i in range(count)])


def chain_up(count, first, last):
    return [(i, i + 1) for i in range(first, last)]


def chain_down(count, first, last):
    return [(count - 1 - i, count - 2 - i) for i in range(first, last)]


def chain_parts(step, total, rows, count, before):
    if step >= count:
        return ()
    place = lax.axis_index("dp")
    up = shard_of(total, rows, jnp.clip(count - step + place, 0, count - 1), count)
    down = shard_of(total, rows, jnp.clip(place - (count - step), 0, count - 1), count)
    if before:
        up = (up.astype(F32) + before[0].astype(F32)).astype(LOW)
        down = (down.astype(F32) + before[1].astype(F32)).astype(LOW)
    return up, down


def chain_sum(step, parts, count, before):
    if step >= count:
        return before
    last = min(step, count - 1)
    up, down = parts
    return [lax.ppermute(up, "dp", chain_up(count, 0, last)), lax.ppermute(down, "dp", chain_down(count, 0, last))]


def chain_sums(first, total, rows, count, before):
    for step in range(first, count):
        before = chain_sum(step, chain_parts(step, total, rows, count, before), count, before)
    return before


def chain_summed(total, rows, count, before):
    own = shard_of(total, rows, lax.axis_index("dp"), count)
    if before:
        own = (own.astype(F32) + before[0].astype(F32) + before[1].astype(F32)).astype(LOW)
    return own


def chain_spread(first, last, shard, count, found):
    for step in range(first, min(last, count)):
        up, down = found[-1] if found else (shard, shard)
        up = lax.ppermute(up, "dp", chain_up(count, step - 1, count - 1))
        down = lax.ppermute(down, "dp", chain_down(count, step - 1, count - 1))
        found = found + [(up, down)]
    return found


def chain_joined(shard, count, found):
    place = lax.axis_index("dp")
    dims = (shard.shape[0], count) + shard.shape[1:]
    zero = jnp.zeros((), jnp.int32)
    result = jnp.zeros(dims, shard.dtype)

    def put(result, piece, at):
        return lax.dynamic_update_slice(result, piece[:, None], (zero, at) + (zero,) * (len(dims) - 2))

    for step, (up, down) in enumerate(found, 1):
        result = put(result, up, jnp.where(place - step >= 0, place - step, place))
        result = put(result, down, jnp.where(place + step < count, place + step, place))
    return put(result, shard, place)


def call(kernel, out_shape, in_specs, out_specs, grid=(), scratch=(), prefetch=0, flops=0, moved=0):
    return pl.pallas_call(
        kernel,
        out_shape=out_shape,
        grid_spec=pltpu.PrefetchScalarGridSpec(
            num_scalar_prefetch=prefetch,
            grid=grid,
            in_specs=in_specs,
            out_specs=out_specs,
            scratch_shapes=list(scratch),
        ),
        compiler_params=pltpu.CompilerParams(vmem_limit_bytes=VMEM_LIMIT),
        cost_estimate=pl.CostEstimate(
            flops=int(flops * WEIGHT), bytes_accessed=int(moved * WEIGHT), transcendentals=0
        ),
    )


def shape(dims, kind=LOW):
    return jax.ShapeDtypeStruct(tuple(dims), kind)


def whole(array):
    rank = len(array.shape)
    return pl.BlockSpec(tuple(array.shape), lambda *_: (0,) * rank)


def bytes_of(*arrays):
    return sum(int(a.size) * a.dtype.itemsize for a in arrays)


def read_pieces(refs, upper):
    x0, x1, x2, top, bottom = refs
    return jnp.concatenate([x0[...], x1[...], x2[...], jnp.where(upper, top[...], bottom[...])], axis=1)


def piece_specs(width, tile, blocks, shift=0):
    halfway = blocks // 2
    plain = pl.BlockSpec((tile, width), lambda b, *_: (b + shift, 0))
    top = pl.BlockSpec((tile, width), lambda b, *_: (jnp.minimum(b + shift, halfway - 1), 0))
    bottom = pl.BlockSpec((tile, width), lambda b, *_: (jnp.maximum(b + shift - halfway, 0), 0))
    return [plain, plain, plain, top, bottom]


def join_kernel(x0, x1, x2, top, bottom, out):
    width, half = x0.shape[1], top.shape[0]
    for i, ref in enumerate((x0, x1, x2)):
        out[:, i * width : (i + 1) * width] = ref[...]
    out[:half, 3 * width :] = top[...]
    out[half:, 3 * width :] = bottom[...]


def join(pieces):
    tokens, width = pieces[0].shape
    out = shape((tokens, 4 * width))
    return call(
        join_kernel, out, [whole(p) for p in pieces], whole(out), grid=(1,), moved=2 * bytes_of(out)
    )(*pieces)


def order_kernel(row_ref, own, oth, full, mine):
    row = row_ref[0]
    features, chunk = own.shape[2], own.shape[1] // 4
    for k in range(4):
        columns = slice(k * features, (k + 1) * features)
        for i in range(4):
            rows = pl.ds(pl.multiple_of(jnp.bitwise_xor(row, i) * chunk, chunk), chunk)
            for s, weight in enumerate((own, oth)):
                at = (2 * i + s) * chunk
                full[at : at + chunk, columns] = weight[k, rows, :]
    mine[...] = jnp.zeros(mine.shape, mine.dtype)
    for h in range(2 * chunk // HEAD):
        mine[h * LANES : h * LANES + HEAD, :] = full[h * HEAD : (h + 1) * HEAD, :]


def order(row, own, oth):
    _, rows, features = own.shape
    full, mine = shape((2 * rows, 4 * features)), shape((2 * rows // 4 // HEAD * LANES, 4 * features))
    return call(
        order_kernel,
        (full, mine),
        [whole(own), whole(oth)],
        (whole(full), whole(mine)),
        grid=(1,),
        prefetch=1,
        moved=2 * bytes_of(full) + bytes_of(mine),
    )(row, own, oth)


def heads_grad_kernel(x0, x1, x2, top, bottom, weight, own, oth):
    upper = pl.program_id(0) < pl.num_programs(0) // 2
    grad = dot(read_pieces((x0, x1, x2, top, bottom), upper), weight[...], NT).astype(LOW)
    own[...] = grad[:, : own.shape[1]]
    oth[...] = grad[:, own.shape[1] :]


def heads_grad_of(pieces, weight):
    tokens, width = pieces[0].shape
    columns = weight.shape[0] // 2
    outs = (shape((tokens, columns)), shape((tokens, columns)))
    rows = pl.BlockSpec((TILE, columns), lambda b: (b, 0))
    return call(
        heads_grad_kernel,
        outs,
        piece_specs(width, TILE, tokens // TILE) + [whole(weight)],
        (rows, rows),
        grid=(tokens // TILE,),
        flops=2 * tokens * 4 * width * weight.shape[0],
        moved=bytes_of(*pieces, weight, *outs),
    )(*pieces, weight)


def pack_kernel(row_ref, gain_ref, q_ref, k_ref, v_ref, out_ref):
    row = row_ref[0]
    gain = gain_ref[...]
    query, key = q_ref.shape[1] // 4, k_ref.shape[1] // 4
    scaled = lambda ref, size, j: (ref[:, j * size : (j + 1) * size].astype(F32) * gain).astype(LOW)
    for j in range(4):
        at = jnp.bitwise_xor(row, j)
        out_ref[at, :, :query] = scaled(q_ref, query, j)
        out_ref[at, :, query : query + key] = scaled(k_ref, key, j)
        out_ref[at, :, query + key :] = scaled(v_ref, key, j)


def pack(row, gain, query_weight, key_weight, value_weight):
    depth = query_weight.shape[0]
    width = (query_weight.shape[1] + 2 * key_weight.shape[1]) // 4
    out = shape((4, depth, width))
    arrays = (gain, query_weight, key_weight, value_weight)
    return call(
        pack_kernel,
        out,
        [whole(a) for a in arrays],
        whole(out),
        grid=(1,),
        prefetch=1,
        moved=2 * bytes_of(out),
    )(row, *arrays)


def project_kernel(x0, x1, x2, top, bottom, w_own, w_oth, cos, sin, first, r1, own, oth):
    upper = pl.program_id(0) < pl.num_programs(0) // 2
    x = read_pieces((x0, x1, x2, top, bottom), upper).astype(F32)
    inverse = lax.rsqrt(jnp.mean(x * x, axis=1, keepdims=True) + EPSILON)
    normed = (x * inverse).astype(LOW)
    first[...] = normed
    r1[...] = jnp.broadcast_to(inverse, r1.shape)
    for weight, out in ((w_own, own), (w_oth, oth)):
        heads = dot(normed, weight[...])
        for h in range(3):
            part = heads[:, h * LANES : (h + 1) * LANES]
            turned = part * cos[...] + pltpu.roll(part, LANES // 2, 1) * sin[...]
            out[:, h * LANES : (h + 1) * LANES] = turned.astype(LOW)
        out[:, 3 * LANES :] = heads[:, 3 * LANES :].astype(LOW)


def project(xs, w_own, w_oth, cos, sin):
    tokens, width = xs[0].shape
    rows = lambda n: pl.BlockSpec((TILE, n), lambda b: (b, 0))
    outs = (shape((tokens, 4 * width)), shape((tokens, LANES), F32), shape((tokens, 512)), shape((tokens, 512)))
    return call(
        project_kernel,
        outs,
        piece_specs(width, TILE, tokens // TILE)
        + [whole(w_own), whole(w_oth), rows(LANES), rows(LANES)],
        tuple(rows(o.shape[1]) for o in outs),
        grid=(tokens // TILE,),
        flops=2 * tokens * 4 * width * 1024,
        moved=bytes_of(*xs, w_own, w_oth, *outs),
    )(*xs, w_own, w_oth, cos, sin)


def stack_heads(ref, rows):
    return jnp.concatenate([ref[rows, :LANES], ref[rows, LANES : 2 * LANES]], axis=0)


def block_limits(start_ref, block):
    rows = pl.ds(pl.multiple_of(block * TILE, TILE), TILE)
    start = start_ref[:, rows]
    query = block * TILE + lax.broadcasted_iota(jnp.int32, (1, TILE), 1)
    return jnp.concatenate([start, start], axis=1), jnp.concatenate([query, query], axis=1)


def allowed_keys(number, start, query):
    key = number * TILE + lax.broadcasted_iota(jnp.int32, (TILE, 2 * TILE), 0)
    return (key >= start) & (key <= query)


def attend_kernel(info, own, oth, start_ref, keep, send, out, lse, full, values, top, total, acc):
    block = pl.program_id(0)
    core = info[0]
    half = own.shape[0]

    @pl.when(block == 0)
    def _():
        full[pl.ds(pl.multiple_of(core * half, half), half), :] = own[...]
        full[pl.ds(pl.multiple_of((1 - core) * half, half), half), :] = oth[...]
        values[...] = full[:, 3 * LANES :].T

    rows = pl.ds(pl.multiple_of(block * TILE, TILE), TILE)
    query = stack_heads(full, rows)
    start, place = block_limits(start_ref, block)
    top[...] = jnp.full(top.shape, -1e30, F32)
    total[...] = jnp.zeros(total.shape, F32)
    acc[...] = jnp.zeros(acc.shape, F32)

    def step(number, _):
        keys = pl.ds(pl.multiple_of(number * TILE, TILE), TILE)
        scores = dot(full[keys, 2 * LANES : 3 * LANES], query, NT) * (FACTOR * LOG2E)
        scores = jnp.where(allowed_keys(number, start, place), scores, -1e30)
        before = top[...]
        now = jnp.maximum(before, jnp.max(scores, axis=0, keepdims=True))
        weight = jnp.exp2(scores - now)
        scale = jnp.exp2(before - now)
        top[...] = now
        total[...] = total[...] * scale + jnp.sum(weight, axis=0, keepdims=True)
        acc[...] = acc[...] * scale + dot(values[:, keys], weight.astype(LOW))
        return 0

    lax.fori_loop(info[1 + block], block + 1, step, 0)
    lse[...] = top[...] + jnp.log2(total[...])
    result = (acc[...] / total[...]).T.astype(LOW)
    out[:, :LANES] = result[:TILE]
    out[:, LANES:] = result[TILE:]
    mine = (block // (half // TILE)) == core
    for target, wanted in ((keep, mine), (send, jnp.logical_not(mine))):

        @pl.when(wanted)
        def _(target=target):
            target[:, :HEAD] = result[:TILE, :HEAD]
            target[:, HEAD:] = result[TILE:, :HEAD]


def attend(info, own, oth, start):
    half = own.shape[0]
    tokens = 2 * half
    per_half = half // TILE
    outs = (
        shape((half, 2 * HEAD)),
        shape((half, 2 * HEAD)),
        shape((tokens, 2 * LANES)),
        shape((1, 2 * tokens), F32),
    )
    return call(
        attend_kernel,
        outs,
        [whole(own), whole(oth), whole(start)],
        (
            pl.BlockSpec((TILE, 2 * HEAD), lambda b, s: (jnp.clip(b - s[0] * per_half, 0, per_half - 1), 0)),
            pl.BlockSpec((TILE, 2 * HEAD), lambda b, s: (jnp.clip(b - (1 - s[0]) * per_half, 0, per_half - 1), 0)),
            pl.BlockSpec((TILE, 2 * LANES), lambda b, s: (b, 0)),
            pl.BlockSpec((1, 2 * TILE), lambda b, s: (0, b)),
        ),
        grid=(tokens // TILE,),
        scratch=(
            pltpu.VMEM((tokens, 4 * LANES), LOW),
            pltpu.VMEM((LANES, tokens), LOW),
            pltpu.VMEM((1, 2 * TILE), F32),
            pltpu.VMEM((1, 2 * TILE), F32),
            pltpu.VMEM((LANES, 2 * TILE), F32),
        ),
        prefetch=1,
        flops=4 * tokens * tokens * LANES * 2,
        moved=bytes_of(own, oth, *outs),
    )(info, own, oth, start)


def turn_back(part, cos, sin):
    return part * cos - pltpu.roll(part, LANES // 2, 1) * sin


def attend_back_kernel(
    info, own, oth, g_own, g_oth, out, lse, start_ref, cos, sin,
    keep, send, full, grads, keys_t, d_keys, d_values, d_query, result,
):
    block = pl.program_id(0)
    core = info[0]
    half = own.shape[0]

    @pl.when(block == 0)
    def _():
        mine = pl.ds(pl.multiple_of(core * half, half), half)
        theirs = pl.ds(pl.multiple_of((1 - core) * half, half), half)
        full[mine, :] = own[...]
        full[theirs, :] = oth[...]
        grads[mine, :] = g_own[...]
        grads[theirs, :] = g_oth[...]
        keys_t[...] = full[:, 2 * LANES : 3 * LANES].T
        d_keys[...] = jnp.zeros(d_keys.shape, F32)
        d_values[...] = jnp.zeros(d_values.shape, F32)

    rows = pl.ds(pl.multiple_of(block * TILE, TILE), TILE)
    query = stack_heads(full, rows)
    grad = stack_heads(grads, rows)
    reply = stack_heads(out, slice(None))
    start, place = block_limits(start_ref, block)
    level = lse[...]
    delta = jnp.sum((grad.astype(F32) * reply.astype(F32)).T, axis=0, keepdims=True)
    d_query[...] = jnp.zeros(d_query.shape, F32)

    def step(number, _):
        keys = pl.ds(pl.multiple_of(number * TILE, TILE), TILE)
        scores = dot(full[keys, 2 * LANES : 3 * LANES], query, NT) * (FACTOR * LOG2E)
        scores = jnp.where(allowed_keys(number, start, place), scores, -1e30)
        weight = jnp.exp2(scores - level)
        pressure = dot(full[keys, 3 * LANES :], grad, NT)
        slope = (weight * (pressure - delta) * FACTOR).astype(LOW)
        d_values[keys, :] += dot(weight.astype(LOW), grad)
        d_keys[keys, :] += dot(slope, query)
        d_query[...] += dot(keys_t[:, keys], slope)
        return 0

    lax.fori_loop(info[1 + block], block + 1, step, 0)
    turned = d_query[...].T
    for h in range(2):
        part = turned[h * TILE : (h + 1) * TILE]
        result[rows, h * LANES : (h + 1) * LANES] = turn_back(part, cos[rows, :], sin[rows, :]).astype(LOW)

    @pl.when(block == pl.num_programs(0) - 1)
    def _():
        mine = pl.ds(pl.multiple_of(core * half, half), half)
        theirs = pl.ds(pl.multiple_of((1 - core) * half, half), half)
        for target, which in ((keep, mine), (send, theirs)):
            target[:, : 2 * LANES] = result[which, :]
            target[:, 2 * LANES : 3 * LANES] = turn_back(
                d_keys[which, :], cos[which, :], sin[which, :]
            ).astype(LOW)
            target[:, 3 * LANES :] = d_values[which, :].astype(LOW)


def attend_back(info, own, oth, g_own, g_oth, out, lse, start, cos, sin):
    half = own.shape[0]
    tokens = 2 * half
    outs = (shape((half, 4 * LANES)), shape((half, 4 * LANES)))
    return call(
        attend_back_kernel,
        outs,
        [
            whole(own),
            whole(oth),
            whole(g_own),
            whole(g_oth),
            pl.BlockSpec((TILE, 2 * LANES), lambda b, s: (b, 0)),
            pl.BlockSpec((1, 2 * TILE), lambda b, s: (0, b)),
            whole(start),
            whole(cos),
            whole(sin),
        ],
        tuple(whole(o) for o in outs),
        grid=(tokens // TILE,),
        scratch=(
            pltpu.VMEM((tokens, 4 * LANES), LOW),
            pltpu.VMEM((tokens, 2 * LANES), LOW),
            pltpu.VMEM((LANES, tokens), LOW),
            pltpu.VMEM((tokens, LANES), F32),
            pltpu.VMEM((tokens, LANES), F32),
            pltpu.VMEM((LANES, 2 * TILE), F32),
            pltpu.VMEM((tokens, 2 * LANES), LOW),
        ),
        prefetch=1,
        flops=10 * tokens * tokens * LANES * 2,
        moved=bytes_of(own, oth, g_own, g_oth, out, *outs),
    )(info, own, oth, g_own, g_oth, out, lse, start, cos, sin)


def middle_kernel(*refs):
    weight, second, middle, r2, joined = refs[10:]
    upper = pl.program_id(0) < pl.num_programs(0) // 2
    heads = read_pieces(refs[:5], upper)
    joined[...] = heads
    x = read_pieces(refs[5:10], upper).astype(F32)
    value = x + dot(heads, weight[...])
    inverse = lax.rsqrt(jnp.mean(value * value, axis=1, keepdims=True) + EPSILON)
    second[...] = (value * inverse).astype(LOW)
    middle[...] = value[:, : middle.shape[1]]
    r2[...] = jnp.broadcast_to(inverse, r2.shape)


def middle_of(heads, xs, weight):
    tokens, width = xs[0].shape
    rows = lambda n: pl.BlockSpec((TILE, n), lambda b: (b, 0))
    outs = (
        shape((tokens, 4 * width)),
        shape((tokens, width), F32),
        shape((tokens, LANES), F32),
        shape((tokens, 4 * width)),
    )
    return call(
        middle_kernel,
        outs,
        piece_specs(width, TILE, tokens // TILE) * 2 + [whole(weight)],
        tuple(rows(o.shape[1]) for o in outs),
        grid=(tokens // TILE,),
        flops=2 * tokens * 16 * width * width,
        moved=bytes_of(*heads, *xs, weight, *outs),
    )(*heads, *xs, weight)


def feed_kernel(second, cot, g_own, u_own, g_oth, u_oth, d_own, d_oth, hidden_own, hidden_oth, back_own, back_oth):
    block = pl.program_id(0)
    per = pl.num_programs(0) // 2
    tokens, units = hidden_own.shape
    width = d_own.shape[2]

    def body(gate_w, up_w, down_w, hidden, back, at):
        down = jnp.concatenate([down_w[i] for i in range(4)], axis=1)
        near = pl.ds(pl.multiple_of(at, TILE), TILE)
        far = pl.ds(pl.multiple_of(units + at, TILE), TILE)
        for m in range(0, tokens, TILE):
            rows = slice(m, m + TILE)
            gate = dot(second[rows, :], gate_w[...])
            up = dot(second[rows, :], up_w[...])
            hidden_grad = dot(cot[rows, :], down, NT)
            share = 1.0 / (1.0 + jnp.exp(-gate))
            silu = gate * share
            hidden[rows, near] = (silu * up).astype(LOW)
            back[rows, near] = (hidden_grad * up * share * (1.0 + gate * (1.0 - share))).astype(LOW)
            back[rows, far] = (hidden_grad * silu).astype(LOW)

    @pl.when(block < per)
    def _():
        body(g_own, u_own, d_own, hidden_own, back_own, block * TILE)

    @pl.when(block >= per)
    def _():
        body(g_oth, u_oth, d_oth, hidden_oth, back_oth, (block - per) * TILE)


def feed(second, cot, gu_own, gu_oth, d_own, d_oth):
    tokens, model = second.shape
    units = gu_own.shape[1] // 2
    per = units // TILE
    early = lambda b: jnp.minimum(b, per - 1)
    late = lambda b: jnp.maximum(b - per, 0)
    column = lambda at: pl.BlockSpec((model, TILE), lambda b: (0, at(b)))
    down = lambda at: pl.BlockSpec((4, TILE, model // 4), lambda b: (0, at(b), 0))
    outs = (shape((tokens, units)), shape((tokens, units)), shape((tokens, 2 * units)), shape((tokens, 2 * units)))
    return call(
        feed_kernel,
        outs,
        [
            whole(second),
            whole(cot),
            column(early),
            column(lambda b: per + early(b)),
            column(late),
            column(lambda b: per + late(b)),
            down(early),
            down(late),
        ],
        tuple(whole(o) for o in outs),
        grid=(2 * per,),
        flops=12 * tokens * model * units,
        moved=bytes_of(second, cot, gu_own, gu_oth, d_own, d_oth, *outs),
    )(second, cot, gu_own, gu_own, gu_oth, gu_oth, d_own, d_oth)


def partial_kernel(blocked, a_own, a_oth, w_own, w_oth, *rest):
    upper = pl.program_id(0) < pl.num_programs(0) // 2
    if len(rest) == 7:
        against, own, far_a, near_a, far_b, near_b, sums = rest
    else:
        own, far_a, near_a, far_b, near_b = rest
    width = own.shape[1]
    total = 0.0
    left, right = a_own[...], a_oth[...]
    found = []
    for k in range(4):
        columns = slice(k * width, (k + 1) * width)
        if blocked:
            value = dot(left, w_own[k]) + dot(right, w_oth[k])
        else:
            value = dot(left, w_own[columns, :], NT) + dot(right, w_oth[columns, :], NT)
        if len(rest) == 7:
            total = total + jnp.sum(value * against[:, columns].astype(F32), axis=1, keepdims=True)
        found.append(value.astype(LOW))
    own[...] = found[0]
    if len(rest) == 7:
        sums[...] = jnp.broadcast_to(total, sums.shape)

    @pl.when(upper)
    def _():
        far_a[:, :width] = found[1]
        far_a[:, width:] = found[3]
        near_a[...] = found[2]

    @pl.when(jnp.logical_not(upper))
    def _():
        far_b[:, :width] = found[2]
        far_b[:, width:] = found[3]
        near_b[...] = found[1]


def partial_sums(blocked, a_own, a_oth, w_own, w_oth, against=None):
    tokens, depth = a_own.shape
    model = 4 * w_own.shape[2] if blocked else w_own.shape[0]
    half, width = tokens // 2, model // 4
    blocks = tokens // TILE
    plain = lambda n: pl.BlockSpec((TILE, n), lambda b: (b, 0))
    early = lambda n: pl.BlockSpec((TILE, n), lambda b: (jnp.minimum(b, blocks // 2 - 1), 0))
    late = lambda n: pl.BlockSpec((TILE, n), lambda b: (jnp.maximum(b - blocks // 2, 0), 0))
    outs = [shape((tokens, width))] + [shape((half, 2 * width)), shape((half, width))] * 2
    writes = [plain(width), early(2 * width), early(width), late(2 * width), late(width)]
    args = [a_own, a_oth, w_own, w_oth]
    specs = [plain(depth), plain(depth), whole(w_own), whole(w_oth)]
    if against is not None:
        outs.append(shape((tokens, LANES), F32))
        writes.append(plain(LANES))
        args.append(against)
        specs.append(plain(model))
    found = call(
        functools.partial(partial_kernel, blocked),
        tuple(outs),
        specs,
        tuple(writes),
        grid=(blocks,),
        flops=4 * tokens * depth * model,
        moved=bytes_of(*args, *outs),
    )(*args)
    return found[:5], None if against is None else found[5][:, 0].reshape(8, tokens // 8)


def feed_grads_kernel(second, cot, back, hidden, out):
    double, share = back.shape[1], out.shape[2]
    for columns, left, right in ((slice(0, double), second, back), (slice(double, None), cot, hidden)):
        value = dot(left[...], right[...], TN).astype(LOW)
        for k in range(out.shape[0]):
            out[k, 0, :, columns] = value[k * share : (k + 1) * share]


def feed_grads(second, cot, back, hidden, count):
    tokens, model = second.shape
    width = model // 4
    out = shape((count, 4, width // count, back.shape[1] + hidden.shape[1]))
    block = pl.BlockSpec((tokens, width), lambda i: (0, i))
    return call(
        feed_grads_kernel,
        out,
        [block, block, whole(back), whole(hidden)],
        pl.BlockSpec((count, 1) + out.shape[2:], lambda i: (0, i, 0, 0)),
        grid=(4,),
        flops=2 * tokens * model * out.shape[3],
        moved=bytes_of(second, cot, back, hidden, out),
    )(second, cot, back, hidden)


def mix_grads_kernel(which, first, heads, back, branch, spread, out, flat):
    @pl.when(pl.program_id(0) == 0)
    def _():
        flat[...] = dot(back[...], spread[...], NT).astype(LOW)

    width, chunk = first.shape[1], heads.shape[1] // 2
    out[0, :width, :] = dot(first[...], flat[...], TN).astype(LOW)
    out[0, width:, :] = dot(heads[:, which * chunk : (which + 1) * chunk], branch[...], TN).astype(LOW)


def mix_grads(which, first, heads, back, branch, spread):
    tokens, model = first.shape
    width = model // 4
    out = shape((4, width + width // 2, width))
    block = pl.BlockSpec((tokens, width), lambda i: (0, i))
    return call(
        functools.partial(mix_grads_kernel, which),
        out,
        [block, block, whole(back), whole(branch), whole(spread)],
        pl.BlockSpec((1,) + out.shape[1:], lambda i: (i, 0, 0)),
        grid=(4,),
        scratch=(pltpu.VMEM((tokens, spread.shape[0]), LOW),),
        flops=2 * tokens * model * out.shape[1],
        moved=bytes_of(first, heads, back, branch, out),
    )(first, heads, back, branch, spread)


def feed_place_kernel(row_ref, piece, gain, gate, up, down):
    units, share = gate.shape[1], piece.shape[2]
    for k in range(piece.shape[0]):
        rows = slice(k * share, (k + 1) * share)
        gate[rows, :] = piece[k, 0, :, :units].astype(F32) * gain[rows, :]
        up[rows, :] = piece[k, 0, :, units : 2 * units].astype(F32) * gain[rows, :]
    down[...] = jnp.concatenate(
        [piece[k, 0, :, 2 * units :].astype(F32) for k in range(piece.shape[0])], axis=0
    ).T


def feed_place(row, pieces, gain):
    count, _, share, triple = pieces.shape
    units, depth = triple // 3, count * share
    outs = (shape((depth, 4 * units), F32), shape((depth, 4 * units), F32), shape((4 * units, depth), F32))
    return call(
        feed_place_kernel,
        outs,
        [
            pl.BlockSpec((count, 1, share, triple), lambda j, s: (0, jnp.bitwise_xor(s[0], j), 0, 0)),
            whole(gain),
        ],
        (
            pl.BlockSpec((depth, units), lambda j, s: (0, j)),
            pl.BlockSpec((depth, units), lambda j, s: (0, j)),
            pl.BlockSpec((units, depth), lambda j, s: (j, 0)),
        ),
        grid=(4,),
        prefetch=1,
        moved=bytes_of(pieces, *outs),
    )(row, pieces, gain)


def mix_place_kernel(row_ref, pieces, heads, gain, query, key, value, output):
    row = row_ref[0]
    wide, narrow = query.shape[1] // 4, key.shape[1] // 4
    for j in range(4):
        piece = pieces[jnp.bitwise_xor(row, j)].astype(F32) * gain[...]
        query[:, j * wide : (j + 1) * wide] = piece[:, :wide]
        key[:, j * narrow : (j + 1) * narrow] = piece[:, wide : wide + narrow]
        value[:, j * narrow : (j + 1) * narrow] = piece[:, wide + narrow :]
        output[j * wide : (j + 1) * wide, :] = heads[jnp.bitwise_xor(row, j)].astype(F32)


def mix_place(row, pieces, heads, gain):
    _, depth, width = pieces.shape
    wide, narrow = width // 2, width // 4
    outs = (
        shape((depth, 4 * wide), F32),
        shape((depth, 4 * narrow), F32),
        shape((depth, 4 * narrow), F32),
        shape((4 * wide, depth), F32),
    )
    return call(
        mix_place_kernel,
        outs,
        [whole(pieces), whole(heads), whole(gain)],
        tuple(whole(o) for o in outs),
        grid=(1,),
        prefetch=1,
        moved=bytes_of(pieces, heads, *outs),
    )(row, pieces, heads, gain)


def sequence_starts(lengths, tokens):
    places = jnp.arange(tokens, dtype=jnp.int32)
    starts = jnp.zeros((tokens,), jnp.int32)
    end = jnp.zeros((), jnp.int32)
    for k in range(lengths.shape[0]):
        end = end + lengths[k]
        starts = jnp.where(places >= end, end, starts)
    return places, starts


def tables(places):
    lane = jnp.arange(LANES, dtype=jnp.int32)
    entry = lane % (LANES // 2)
    frequency = THETA ** (-2.0 * entry.astype(F32) / HEAD)
    real = entry < SIDE
    angles = places.astype(F32)[:, None] * frequency[None, :]
    cosine = jnp.where(real[None, :], jnp.cos(angles), 0.0)
    sign = jnp.where(lane < LANES // 2, -1.0, 1.0)
    sine = jnp.where(real[None, :], jnp.sin(angles) * sign[None, :], 0.0)
    return cosine, sine


def spread_matrix():
    source = jnp.arange(4 * HEAD, dtype=jnp.int32)
    head, entry = source // HEAD, source % HEAD
    inside = jnp.where((head < 3) & (entry >= SIDE), entry - SIDE + LANES // 2, entry)
    target = head * LANES + inside
    return (target[:, None] == jnp.arange(4 * LANES, dtype=jnp.int32)[None, :]).astype(LOW)


def on_device(
    layer_input,
    first_gain,
    query_weight,
    key_projection_weight,
    value_projection_weight,
    output_weight,
    second_gain,
    gate_weight,
    up_weight,
    down_weight,
    sequence_lengths,
    cotangent,
):
    row = lax.axis_index("row")
    core = lax.axis_index("col")
    place = lax.axis_index("dp")
    blocks = lax.axis_size("dp")
    row_info = row.reshape(1).astype(jnp.int32)
    half, width = layer_input.shape
    tokens, model = 2 * half, 4 * width
    units = gate_weight.shape[1] // 4
    rows = output_weight.shape[0]
    chunk = rows // 4
    relative = [jnp.bitwise_xor(row, i) for i in range(4)]
    live = Live()
    live.x, live.cot = layer_input, cotangent

    live.xs = gather_one(live.x)
    gains = [gain[:, None] for gain in (first_gain, second_gain)]
    packed = pack(row_info, gains[0], query_weight, key_projection_weight, value_projection_weight)
    mixer = [packed[i] for i in range(4)]
    halves, weights = ready(
        fetch_halves(mixer, place, blocks), (gate_weight, up_weight, down_weight, output_weight, gains[1])
    )
    live.mixer_one = fetch_one(halves)
    live.mixer_own, live.lengths = mixer[0], sequence_lengths[0]
    gate, up, down, out, gain = weights
    downs = [lax.dynamic_slice_in_dim(down, relative[i] * units, units, 0) for i in range(4)]
    out_down = [jnp.concatenate([out, downs[i]], axis=0) for i in range(4)]
    scaled = lambda weight, i: (
        lax.dynamic_slice_in_dim(weight, relative[i] * units, units, 1).astype(F32) * gain
    ).astype(LOW)
    gate_up = [jnp.concatenate([scaled(gate, i), scaled(up, i)], axis=1) for i in range(4)]
    live.od_own, live.od_halves = out_down[0], fetch_halves(out_down, place, blocks)
    live.gu_own, live.gu_halves = gate_up[0], fetch_halves(gate_up, place, blocks)
    live.sync()

    halves, mine = ready(gather_halves(live.xs), jnp.stack(live.mixer_one))
    live.xs = gather_two(live.xs, halves)
    live.mixer = (live.mixer_own, mine, fetch_two(mine, blocks))
    places, starts = sequence_starts(live.lengths, tokens)
    live.cos, live.sin = tables(places - starts)
    live.start = starts[None, :]
    live.info = jnp.concatenate([core.reshape(1), starts[::TILE] // TILE]).astype(jnp.int32)
    spread = spread_matrix()
    del live.mixer_one, live.mixer_own, live.lengths
    live.sync()

    live.od_one = fetch_one(live.od_halves)
    live.w_own = dot(fetched(*live.mixer, place).reshape(model, 4 * HEAD), spread).astype(LOW)
    live.w_oth = other(live.w_own)
    cos_own = lax.dynamic_slice_in_dim(live.cos, core * half, half, 0)
    sin_own = lax.dynamic_slice_in_dim(live.sin, core * half, half, 0)
    live.first, live.r1, live.qkv, live.send = project(
        live.xs, live.w_own, live.w_oth, cos_own, sin_own
    )
    del live.mixer, live.od_halves
    live.sync()
    halves, send, live.od_mine = ready(live.gu_halves, live.send, jnp.stack(live.od_one))
    live.od_theirs = fetch_two(live.od_mine, blocks)
    live.gu_one = fetch_one(halves)
    live.qkv_got = other(send)
    live.keep, live.send, live.attended, live.lse = attend(live.info, live.qkv, live.qkv_got, live.start)
    del live.od_one, live.gu_halves
    live.sync()
    live.heads = jnp.concatenate([live.keep, other(live.send)], axis=1)
    live.gu_mine = jnp.stack(live.gu_one)
    del live.keep, live.send, live.gu_one
    live.sync()

    live.gu_theirs = fetch_two(live.gu_mine, blocks)
    live.heads = gather_one(live.heads)
    live.cots = gather_one(live.cot)
    live.od_own = fetched(live.od_own, live.od_mine, live.od_theirs, place)
    del live.od_mine, live.od_theirs
    live.sync()

    halves, more = ready(gather_halves(live.heads), gather_halves(live.cots))
    live.heads = gather_two(live.heads, halves)
    live.cots = gather_two(live.cots, more)
    od_oth = other(live.od_own)
    live.out_full, live.out_mine = order(row_info, live.od_own[:, :rows], od_oth[:, :rows])
    live.d_own, live.d_oth = live.od_own[:, rows:], od_oth[:, rows:]
    live.gu_own = fetched(live.gu_own, live.gu_mine, live.gu_theirs, place).reshape(model, 2 * units)
    del live.od_own, live.gu_mine, live.gu_theirs
    live.sync()
    live.gu_oth = other(live.gu_own)
    live.cot_all = join(live.cots)
    del live.cots

    live.second, live.middle, live.r2, live.heads_all = middle_of(live.heads, live.xs, live.out_full)
    del live.heads, live.xs, live.out_full
    live.hid_own, live.hid_oth, live.back_own, live.back_oth = feed(
        live.second, live.cot_all, live.gu_own, live.gu_oth, live.d_own, live.d_oth
    )
    live.sg, live.sums = partial_sums(False, live.back_own, live.back_oth, live.gu_own, live.gu_oth, live.second)
    del live.gu_own, live.gu_oth
    live.sync()

    def added(own, got):
        return (own.astype(F32) + got.astype(F32)).astype(LOW)

    live.sg = scatter_one(live.sg)
    live.sums = (live.sums, swap(live.sums, 1))
    live.feed_oth = feed_grads(live.second, live.cot_all, live.back_oth, live.hid_oth, blocks)
    live.feed_own = feed_grads(live.second, live.cot_all, live.back_own, live.hid_own, blocks)
    del live.back_own, live.back_oth, live.second, live.cot_all
    live.sync()

    halves, sums, feed_oth = ready(scatter_halves(live.sg), live.sums[0] + live.sums[1], live.feed_oth)
    live.sg = scatter_two(live.sg, halves)
    live.sums = (sums, swap(sums, 2))
    live.feed_got = other(feed_oth)
    del live.feed_oth
    live.sync()

    second_grad = scattered(live.sg)
    inner = (live.sums[0] + live.sums[1]).reshape(half)
    r2 = live.r2[:, :1]
    live.middle_grad = (
        live.cot.astype(F32)
        + r2 * second_grad
        - live.middle * (r2 * r2 * inner[:, None] / model)
    )
    live.branch = live.middle_grad.astype(LOW)
    live.branches = gather_one(*ready(live.branch))
    feed_sum = lax.psum_scatter(added(live.feed_own, live.feed_got), "dp", scatter_dimension=0)
    live.fo, _ = partial_sums(True, live.hid_own, live.hid_oth, live.d_own, live.d_oth)
    del live.feed_own, live.feed_got, live.hid_own, live.hid_oth, live.d_own, live.d_oth
    live.gain_part = jnp.sum(second_grad * live.middle * r2, axis=0) / second_gain
    del live.sg, live.sums, live.cot, live.r2
    live.sync()

    live.branches = gather_two(live.branches, ready(*gather_halves(live.branches)))
    live.sync()
    live.grad, live.send = heads_grad_of(live.branches, live.out_mine)
    live.grad_got = other(live.send)
    del live.branches, live.out_mine, live.send
    live.sync()

    live.fo = scatter_one(live.fo)
    live.bk, live.send = attend_back(
        live.info, live.qkv, live.qkv_got, live.grad, live.grad_got,
        live.attended, live.lse, live.start, live.cos, live.sin,
    )
    del live.qkv, live.qkv_got, live.grad, live.grad_got, live.attended, live.lse, live.start, live.info
    live.sync()

    halves, send = ready(scatter_halves(live.fo), live.send)
    live.fo = scatter_two(live.fo, halves)
    live.bg = other(send)
    live.mix_oth = mix_grads(1, live.first, live.heads_all, live.bg, live.branch, spread)
    live.mix_own = mix_grads(0, live.first, live.heads_all, live.bk, live.branch, spread)
    del live.send
    live.sync()
    live.mix = added(live.mix_own, other(live.mix_oth))
    live.feed_sum = feed_sum
    del live.mix_own, live.mix_oth
    live.sync()
    mix_rows, share = (width, chunk), width // blocks
    parts, (bk, bg), shard = ready(
        chain_parts(1, live.mix, mix_rows, blocks, []), (live.bk, live.bg), live.feed_sum
    )
    live.feed_sum = spread_row(shard)
    live.moving = chain_sum(1, parts, blocks, [])
    live.fg, live.sums = partial_sums(False, bk, bg, live.w_own, live.w_oth, live.first)
    del live.bk, live.bg, live.w_own, live.w_oth, live.first
    live.sync()

    feeds = lax.all_gather(live.feed_sum, "dp", axis=0)
    parts = ready(*chain_parts(2, live.mix, mix_rows, blocks, live.moving))
    live.moving = chain_sum(2, parts, blocks, live.moving)
    live.fg = scatter_one(live.fg)
    live.sums = (live.sums, swap(live.sums, 1))
    layer_output = (live.middle + scattered(live.fo)).astype(LOW)
    del live.fo, live.middle, live.feed_sum
    live.sync()

    halves, sums, parts = ready(
        scatter_halves(live.fg),
        live.sums[0] + live.sums[1],
        chain_parts(3, live.mix, mix_rows, blocks, live.moving),
    )
    live.moving = chain_sum(3, parts, blocks, live.moving)
    live.fg = scatter_two(live.fg, halves)
    live.sums = (sums, swap(sums, 2))
    live.sync()

    live.moving = chain_sums(4, live.mix, mix_rows, blocks, live.moving)
    (shard,) = ready(chain_summed(live.mix, mix_rows, blocks, live.moving))
    turned = spread_row(shard[:, :share])
    live.mix = jnp.concatenate([turned, shard[:, share:]], axis=1)
    live.sync()
    mix, _ = ready(live.mix, live.fg)
    live.moving = chain_spread(1, 2, mix, blocks, [])
    first_grad = scattered(live.fg)
    inner = (live.sums[0] + live.sums[1]).reshape(half)
    r1 = live.r1[:, :1]
    inputs = live.x.astype(F32)
    input_gradient = (
        live.middle_grad
        + r1 * first_grad
        - inputs * (r1 * r1 * inner[:, None] / model)
    )
    gains = jnp.stack([jnp.sum(first_grad * inputs * r1, axis=0) / first_gain, live.gain_part])
    live.gains = gains + other(gains)
    del live.fg, live.sums, live.r1, live.x, live.middle_grad, live.gain_part
    live.sync()
    live.moving = chain_spread(2, 3, live.mix, blocks, live.moving)
    live.got = [turn(live.gains, step, blocks) for step in range(1, blocks)]
    live.sync()
    gain_total = live.gains + sum(live.got)
    moving = chain_spread(3, blocks, live.mix, blocks, live.moving)
    mixes = chain_joined(live.mix, blocks, moving)
    gate_total, up_total, down_total = feed_place(row_info, feeds, second_gain[:, None])
    query_total, key_total, value_total, output_total = mix_place(
        row_info,
        mixes[:, :, :share].reshape(4, width, width),
        mixes[:, :, share:].reshape(4, chunk, width),
        first_gain[:, None],
    )
    return (
        layer_output,
        input_gradient,
        query_total,
        key_total,
        value_total,
        output_total,
        gate_total,
        up_total,
        down_total,
        gain_total[0],
        gain_total[1],
    )


def solution(mesh):
    return jax.shard_map(
        on_device,
        mesh=mesh,
        in_specs=(
            P(("dp", "col"), "row"),
            P("row"),
            P("row", "col"),
            P("row", "col"),
            P("row", "col"),
            P("col", "row"),
            P("row"),
            P("row", "col"),
            P("row", "col"),
            P("col", "row"),
            P("dp", None),
            P(("dp", "col"), "row"),
        ),
        out_specs=(
            P(("dp", "col"), "row"),
            P(("dp", "col"), "row"),
            P("row", "col"),
            P("row", "col"),
            P("row", "col"),
            P("col", "row"),
            P("row", "col"),
            P("row", "col"),
            P("col", "row"),
            P("row"),
            P("row"),
        ),
        check_vma=False,
    )
```

```python
import functools

import jax
import jax.numpy as jnp
from jax import lax
from jax.experimental import pallas as pl
from jax.experimental.pallas import tpu as pltpu
from jax.sharding import PartitionSpec as P

HEAD = 96
LANES = 128
SIDE = 48
TILE = 256
EPSILON = 1e-05
THETA = 100000.0
LOG2E = 1.4426950408889634
FACTOR = HEAD**-0.5
LOW = jnp.bfloat16
F32 = jnp.float32
NN = (((1,), (0,)), ((), ()))
NT = (((1,), (1,)), ((), ()))
TN = (((0,), (0,)), ((), ()))
VMEM_LIMIT = 48 * 1024 * 1024
WEIGHT = 1 / 64


def dot(left, right, dims=NN):
    return lax.dot_general(left, right, dims, preferred_element_type=F32)


def swap(value, step):
    return lax.ppermute(value, "row", [(i, i ^ step) for i in range(4)])


def other(value):
    return lax.ppermute(value, "col", [(0, 1), (1, 0)])


def pair(value, count):
    return lax.ppermute(value, "dp", [(i, i ^ 1) for i in range(count)])


def spread_row(shard):
    return jnp.stack([shard[0]] + [swap(shard[i], i) for i in (1, 2, 3)])


class Live:
    def sync(self):
        self.__dict__.update(lax.optimization_barrier(dict(self.__dict__)))


def ready(*values):
    return lax.optimization_barrier(values)


def gather_one(value):
    return [value, swap(value, 1), swap(value, 2)]


def gather_halves(found):
    half = found[0].shape[0] // 2
    return found[1][:half], found[2][half:]


def gather_two(found, halves):
    return found + [swap(halves[0], 2), swap(halves[1], 1)]


def fetch_halves(pieces, place, count):
    parts = 2 if count % 2 == 0 else 1
    rows = pieces[0].shape[0] // parts
    at = (place % parts) * rows
    return [lax.dynamic_slice_in_dim(pieces[i], at, rows, 0) for i in (1, 2, 3)]


def fetch_one(halves):
    return [swap(half, i) for i, half in enumerate(halves, 1)]


def fetch_two(mine, count):
    return pair(mine, count) if count % 2 == 0 else ()


def fetched(own, mine, theirs, place):
    if isinstance(theirs, tuple):
        return jnp.concatenate([own[None], mine])
    rows = mine.shape[1]
    bit = place % 2
    zero = jnp.zeros((), jnp.int32)
    result = jnp.zeros((4,) + own.shape, own.dtype)
    result = lax.dynamic_update_slice(result, own[None], (0, 0, 0))
    result = lax.dynamic_update_slice(result, mine, (zero + 1, bit * rows, zero))
    return lax.dynamic_update_slice(result, theirs, (zero + 1, (1 - bit) * rows, zero))


def scatter_one(parts):
    own, far_a, near_a, far_b, near_b = parts
    return own, swap(far_a, 1), near_a, swap(far_b, 2), near_b


def scatter_halves(parts):
    own, got_a, near_a, got_b, near_b = parts
    width = own.shape[1]
    send_a = (near_a.astype(F32) + got_a[:, width:].astype(F32)).astype(LOW)
    send_b = (near_b.astype(F32) + got_b[:, width:].astype(F32)).astype(LOW)
    return send_a, send_b


def scatter_two(parts, halves):
    own, got_a, _, got_b, _ = parts
    return own, got_a, swap(halves[0], 2), got_b, swap(halves[1], 1)


def scattered(parts):
    own, got_a, last_a, got_b, last_b = parts
    width, half = own.shape[1], got_a.shape[0]
    upper = own[:half].astype(F32) + got_a[:, :width].astype(F32) + last_a.astype(F32)
    lower = own[half:].astype(F32) + got_b[:, :width].astype(F32) + last_b.astype(F32)
    return jnp.concatenate([upper, lower], axis=0)


def shard_of(total, rows, number, count):
    found, at = [], 0
    for part in rows:
        size = part // count
        found.append(lax.dynamic_slice_in_dim(total, at + number * size, size, 1))
        at = at + part
    return found[0] if len(found) == 1 else jnp.concatenate(found, axis=1)


def turn(value, step, count):
    return lax.ppermute(value, "dp", [(i, (i + step) % count) for i in range(count)])


def chain_up(count, first, last):
    return [(i, i + 1) for i in range(first, last)]


def chain_down(count, first, last):
    return [(count - 1 - i, count - 2 - i) for i in range(first, last)]


def chain_parts(step, total, rows, count, before):
    if step >= count:
        return ()
    place = lax.axis_index("dp")
    up = shard_of(total, rows, jnp.clip(count - step + place, 0, count - 1), count)
    down = shard_of(total, rows, jnp.clip(place - (count - step), 0, count - 1), count)
    if before:
        up = (up.astype(F32) + before[0].astype(F32)).astype(LOW)
        down = (down.astype(F32) + before[1].astype(F32)).astype(LOW)
    return up, down


def chain_sum(step, parts, count, before):
    if step >= count:
        return before
    last = min(step, count - 1)
    up, down = parts
    return [lax.ppermute(up, "dp", chain_up(count, 0, last)), lax.ppermute(down, "dp", chain_down(count, 0, last))]


def chain_sums(first, total, rows, count, before):
    for step in range(first, count):
        before = chain_sum(step, chain_parts(step, total, rows, count, before), count, before)
    return before


def chain_summed(total, rows, count, before):
    own = shard_of(total, rows, lax.axis_index("dp"), count)
    if before:
        own = (own.astype(F32) + before[0].astype(F32) + before[1].astype(F32)).astype(LOW)
    return own


def chain_spread(first, last, shard, count, found):
    for step in range(first, min(last, count)):
        up, down = found[-1] if found else (shard, shard)
        up = lax.ppermute(up, "dp", chain_up(count, step - 1, count - 1))
        down = lax.ppermute(down, "dp", chain_down(count, step - 1, count - 1))
        found = found + [(up, down)]
    return found


def chain_joined(shard, count, found):
    place = lax.axis_index("dp")
    dims = (shard.shape[0], count) + shard.shape[1:]
    zero = jnp.zeros((), jnp.int32)
    result = jnp.zeros(dims, shard.dtype)

    def put(result, piece, at):
        return lax.dynamic_update_slice(result, piece[:, None], (zero, at) + (zero,) * (len(dims) - 2))

    for step, (up, down) in enumerate(found, 1):
        result = put(result, up, jnp.where(place - step >= 0, place - step, place))
        result = put(result, down, jnp.where(place + step < count, place + step, place))
    return put(result, shard, place)


def call(kernel, out_shape, in_specs, out_specs, grid=(), scratch=(), prefetch=0, flops=0, moved=0):
    return pl.pallas_call(
        kernel,
        out_shape=out_shape,
        grid_spec=pltpu.PrefetchScalarGridSpec(
            num_scalar_prefetch=prefetch,
            grid=grid,
            in_specs=in_specs,
            out_specs=out_specs,
            scratch_shapes=list(scratch),
        ),
        compiler_params=pltpu.CompilerParams(vmem_limit_bytes=VMEM_LIMIT),
        cost_estimate=pl.CostEstimate(
            flops=int(flops * WEIGHT), bytes_accessed=int(moved * WEIGHT), transcendentals=0
        ),
    )


def shape(dims, kind=LOW):
    return jax.ShapeDtypeStruct(tuple(dims), kind)


def whole(array):
    rank = len(array.shape)
    return pl.BlockSpec(tuple(array.shape), lambda *_: (0,) * rank)


def bytes_of(*arrays):
    return sum(int(a.size) * a.dtype.itemsize for a in arrays)


def read_pieces(refs, upper):
    x0, x1, x2, top, bottom = refs
    return jnp.concatenate([x0[...], x1[...], x2[...], jnp.where(upper, top[...], bottom[...])], axis=1)


def piece_specs(width, tile, blocks, shift=0):
    halfway = blocks // 2
    plain = pl.BlockSpec((tile, width), lambda b, *_: (b + shift, 0))
    top = pl.BlockSpec((tile, width), lambda b, *_: (jnp.minimum(b + shift, halfway - 1), 0))
    bottom = pl.BlockSpec((tile, width), lambda b, *_: (jnp.maximum(b + shift - halfway, 0), 0))
    return [plain, plain, plain, top, bottom]


def join_kernel(x0, x1, x2, top, bottom, out):
    width, half = x0.shape[1], top.shape[0]
    for i, ref in enumerate((x0, x1, x2)):
        out[:, i * width : (i + 1) * width] = ref[...]
    out[:half, 3 * width :] = top[...]
    out[half:, 3 * width :] = bottom[...]


def join(pieces):
    tokens, width = pieces[0].shape
    out = shape((tokens, 4 * width))
    return call(
        join_kernel, out, [whole(p) for p in pieces], whole(out), grid=(1,), moved=2 * bytes_of(out)
    )(*pieces)


def split_low(value):
    high = lax.reduce_precision(value, 8, 7)
    rest = value - high
    middle = lax.reduce_precision(rest, 8, 7)
    terms = [high, middle, rest - middle]
    spare = jnp.zeros((16 - 3 * value.shape[0], value.shape[1]), F32)
    return jnp.concatenate(terms + [spare], axis=0).astype(LOW)


def unsplit(rows, count):
    terms = [rows[i * count : (i + 1) * count].astype(F32) for i in range(3)]
    return terms[0] + terms[1] + terms[2]


def order_kernel(row_ref, own, oth, full, mine):
    row = row_ref[0]
    features, chunk = own.shape[2], own.shape[1] // 4
    for k in range(4):
        columns = slice(k * features, (k + 1) * features)
        for i in range(4):
            rows = pl.ds(pl.multiple_of(jnp.bitwise_xor(row, i) * chunk, chunk), chunk)
            for s, weight in enumerate((own, oth)):
                at = (2 * i + s) * chunk
                full[at : at + chunk, columns] = weight[k, rows, :]
    mine[...] = jnp.zeros(mine.shape, mine.dtype)
    for h in range(2 * chunk // HEAD):
        mine[h * LANES : h * LANES + HEAD, :] = full[h * HEAD : (h + 1) * HEAD, :]


def order(row, own, oth):
    _, rows, features = own.shape
    full, mine = shape((2 * rows, 4 * features)), shape((2 * rows // 4 // HEAD * LANES, 4 * features))
    return call(
        order_kernel,
        (full, mine),
        [whole(own), whole(oth)],
        (whole(full), whole(mine)),
        grid=(1,),
        prefetch=1,
        moved=2 * bytes_of(full) + bytes_of(mine),
    )(row, own, oth)


def heads_grad_kernel(x0, x1, x2, top, bottom, weight, own, oth):
    upper = pl.program_id(0) < pl.num_programs(0) // 2
    grad = dot(read_pieces((x0, x1, x2, top, bottom), upper), weight[...], NT).astype(LOW)
    own[...] = grad[:, : own.shape[1]]
    oth[...] = grad[:, own.shape[1] :]


def heads_grad_of(pieces, weight):
    tokens, width = pieces[0].shape
    columns = weight.shape[0] // 2
    outs = (shape((tokens, columns)), shape((tokens, columns)))
    rows = pl.BlockSpec((TILE, columns), lambda b: (b, 0))
    return call(
        heads_grad_kernel,
        outs,
        piece_specs(width, TILE, tokens // TILE) + [whole(weight)],
        (rows, rows),
        grid=(tokens // TILE,),
        flops=2 * tokens * 4 * width * weight.shape[0],
        moved=bytes_of(*pieces, weight, *outs),
    )(*pieces, weight)


def pack_kernel(row_ref, gain_ref, q_ref, k_ref, v_ref, out_ref):
    row = row_ref[0]
    gain = gain_ref[...]
    query, key = q_ref.shape[1] // 4, k_ref.shape[1] // 4
    scaled = lambda ref, size, j: (ref[:, j * size : (j + 1) * size].astype(F32) * gain).astype(LOW)
    for j in range(4):
        at = jnp.bitwise_xor(row, j)
        out_ref[at, :, :query] = scaled(q_ref, query, j)
        out_ref[at, :, query : query + key] = scaled(k_ref, key, j)
        out_ref[at, :, query + key :] = scaled(v_ref, key, j)


def pack(row, gain, query_weight, key_weight, value_weight):
    depth = query_weight.shape[0]
    width = (query_weight.shape[1] + 2 * key_weight.shape[1]) // 4
    out = shape((4, depth, width))
    arrays = (gain, query_weight, key_weight, value_weight)
    return call(
        pack_kernel,
        out,
        [whole(a) for a in arrays],
        whole(out),
        grid=(1,),
        prefetch=1,
        moved=2 * bytes_of(out),
    )(row, *arrays)


def project_kernel(x0, x1, x2, top, bottom, w_own, w_oth, cos, sin, first, r1, own, oth):
    upper = pl.program_id(0) < pl.num_programs(0) // 2
    x = read_pieces((x0, x1, x2, top, bottom), upper).astype(F32)
    inverse = lax.rsqrt(jnp.mean(x * x, axis=1, keepdims=True) + EPSILON)
    normed = (x * inverse).astype(LOW)
    first[...] = normed
    r1[...] = jnp.broadcast_to(inverse, r1.shape)
    for weight, out in ((w_own, own), (w_oth, oth)):
        heads = dot(normed, weight[...])
        for h in range(3):
            part = heads[:, h * LANES : (h + 1) * LANES]
            turned = part * cos[...] + pltpu.roll(part, LANES // 2, 1) * sin[...]
            out[:, h * LANES : (h + 1) * LANES] = turned.astype(LOW)
        out[:, 3 * LANES :] = heads[:, 3 * LANES :].astype(LOW)


def project(xs, w_own, w_oth, cos, sin):
    tokens, width = xs[0].shape
    rows = lambda n: pl.BlockSpec((TILE, n), lambda b: (b, 0))
    outs = (shape((tokens, 4 * width)), shape((tokens, LANES), F32), shape((tokens, 512)), shape((tokens, 512)))
    return call(
        project_kernel,
        outs,
        piece_specs(width, TILE, tokens // TILE)
        + [whole(w_own), whole(w_oth), rows(LANES), rows(LANES)],
        tuple(rows(o.shape[1]) for o in outs),
        grid=(tokens // TILE,),
        flops=2 * tokens * 4 * width * 1024,
        moved=bytes_of(*xs, w_own, w_oth, *outs),
    )(*xs, w_own, w_oth, cos, sin)


def stack_heads(ref, rows):
    return jnp.concatenate([ref[rows, :LANES], ref[rows, LANES : 2 * LANES]], axis=0)


def block_limits(start_ref, block):
    rows = pl.ds(pl.multiple_of(block * TILE, TILE), TILE)
    start = start_ref[:, rows]
    query = block * TILE + lax.broadcasted_iota(jnp.int32, (1, TILE), 1)
    return jnp.concatenate([start, start], axis=1), jnp.concatenate([query, query], axis=1)


def allowed_keys(number, start, query):
    key = number * TILE + lax.broadcasted_iota(jnp.int32, (TILE, 2 * TILE), 0)
    return (key >= start) & (key <= query)


def over_keys(info, block, step):
    count = (info.shape[0] - 1) // 2
    first, whole_from = info[1 + block], jnp.minimum(info[1 + count + block], block)

    def masked(number, carry):
        step(number, True)
        return carry

    def plain(number, carry):
        step(number, False)
        return carry

    lax.fori_loop(first, whole_from, masked, 0)
    lax.fori_loop(whole_from, block, plain, 0)
    step(block, True)


def attend_kernel(info, own, oth, start_ref, keep, send, out, lse, full, values, top, total, acc):
    block = pl.program_id(0)
    core = info[0]
    half = own.shape[0]

    @pl.when(block == 0)
    def _():
        full[pl.ds(pl.multiple_of(core * half, half), half), :] = own[...]
        full[pl.ds(pl.multiple_of((1 - core) * half, half), half), :] = oth[...]
        values[...] = full[:, 3 * LANES :].T

    rows = pl.ds(pl.multiple_of(block * TILE, TILE), TILE)
    query = stack_heads(full, rows)
    start, place = block_limits(start_ref, block)
    top[...] = jnp.full(top.shape, -1e30, F32)
    total[...] = jnp.zeros(total.shape, F32)
    acc[...] = jnp.zeros(acc.shape, F32)

    def step(number, masked):
        keys = pl.ds(pl.multiple_of(number * TILE, TILE), TILE)
        scores = dot(full[keys, 2 * LANES : 3 * LANES], query, NT) * (FACTOR * LOG2E)
        if masked:
            scores = jnp.where(allowed_keys(number, start, place), scores, -1e30)
        before = top[...]
        now = jnp.maximum(before, jnp.max(scores, axis=0, keepdims=True))
        weight = jnp.exp2(scores - now)
        scale = jnp.exp2(before - now)
        top[...] = now
        total[...] = total[...] * scale + jnp.sum(weight, axis=0, keepdims=True)
        acc[...] = acc[...] * scale + dot(values[:, keys], weight.astype(LOW))

    over_keys(info, block, step)
    lse[...] = top[...] + jnp.log2(total[...])
    result = (acc[...] / total[...]).T.astype(LOW)
    out[:, :LANES] = result[:TILE]
    out[:, LANES:] = result[TILE:]
    mine = (block // (half // TILE)) == core
    for target, wanted in ((keep, mine), (send, jnp.logical_not(mine))):

        @pl.when(wanted)
        def _(target=target):
            target[:, :HEAD] = result[:TILE, :HEAD]
            target[:, HEAD:] = result[TILE:, :HEAD]


def attend(info, own, oth, start):
    half = own.shape[0]
    tokens = 2 * half
    per_half = half // TILE
    outs = (
        shape((half, 2 * HEAD)),
        shape((half, 2 * HEAD)),
        shape((tokens, 2 * LANES)),
        shape((1, 2 * tokens), F32),
    )
    return call(
        attend_kernel,
        outs,
        [whole(own), whole(oth), whole(start)],
        (
            pl.BlockSpec((TILE, 2 * HEAD), lambda b, s: (jnp.clip(b - s[0] * per_half, 0, per_half - 1), 0)),
            pl.BlockSpec((TILE, 2 * HEAD), lambda b, s: (jnp.clip(b - (1 - s[0]) * per_half, 0, per_half - 1), 0)),
            pl.BlockSpec((TILE, 2 * LANES), lambda b, s: (b, 0)),
            pl.BlockSpec((1, 2 * TILE), lambda b, s: (0, b)),
        ),
        grid=(tokens // TILE,),
        scratch=(
            pltpu.VMEM((tokens, 4 * LANES), LOW),
            pltpu.VMEM((LANES, tokens), LOW),
            pltpu.VMEM((1, 2 * TILE), F32),
            pltpu.VMEM((1, 2 * TILE), F32),
            pltpu.VMEM((LANES, 2 * TILE), F32),
        ),
        prefetch=1,
        flops=4 * tokens * tokens * LANES * 2,
        moved=bytes_of(own, oth, *outs),
    )(info, own, oth, start)


def turn_back(part, cos, sin):
    return part * cos - pltpu.roll(part, LANES // 2, 1) * sin


def attend_back_kernel(
    info, own, oth, g_own, g_oth, out, lse, start_ref, cos, sin,
    keep, send, full, grads, keys_t, d_keys, d_values, d_query, result,
):
    block = pl.program_id(0)
    core = info[0]
    half = own.shape[0]

    @pl.when(block == 0)
    def _():
        mine = pl.ds(pl.multiple_of(core * half, half), half)
        theirs = pl.ds(pl.multiple_of((1 - core) * half, half), half)
        full[mine, :] = own[...]
        full[theirs, :] = oth[...]
        grads[mine, :] = g_own[...]
        grads[theirs, :] = g_oth[...]
        keys_t[...] = full[:, 2 * LANES : 3 * LANES].T
        d_keys[...] = jnp.zeros(d_keys.shape, F32)
        d_values[...] = jnp.zeros(d_values.shape, F32)

    rows = pl.ds(pl.multiple_of(block * TILE, TILE), TILE)
    query = stack_heads(full, rows)
    grad = stack_heads(grads, rows)
    reply = stack_heads(out, slice(None))
    start, place = block_limits(start_ref, block)
    level = lse[...]
    delta = jnp.sum((grad.astype(F32) * reply.astype(F32)).T, axis=0, keepdims=True)
    d_query[...] = jnp.zeros(d_query.shape, F32)

    def step(number, masked):
        keys = pl.ds(pl.multiple_of(number * TILE, TILE), TILE)
        scores = dot(full[keys, 2 * LANES : 3 * LANES], query, NT) * (FACTOR * LOG2E)
        if masked:
            scores = jnp.where(allowed_keys(number, start, place), scores, -1e30)
        weight = jnp.exp2(scores - level)
        pressure = dot(full[keys, 3 * LANES :], grad, NT)
        slope = (weight * (pressure - delta) * FACTOR).astype(LOW)
        d_values[keys, :] += dot(weight.astype(LOW), grad)
        d_keys[keys, :] += dot(slope, query)
        d_query[...] += dot(keys_t[:, keys], slope)

    over_keys(info, block, step)
    turned = d_query[...].T
    for h in range(2):
        part = turned[h * TILE : (h + 1) * TILE]
        result[rows, h * LANES : (h + 1) * LANES] = turn_back(part, cos[rows, :], sin[rows, :]).astype(LOW)

    @pl.when(block == pl.num_programs(0) - 1)
    def _():
        mine = pl.ds(pl.multiple_of(core * half, half), half)
        theirs = pl.ds(pl.multiple_of((1 - core) * half, half), half)
        for target, which in ((keep, mine), (send, theirs)):
            target[:, : 2 * LANES] = result[which, :]
            target[:, 2 * LANES : 3 * LANES] = turn_back(
                d_keys[which, :], cos[which, :], sin[which, :]
            ).astype(LOW)
            target[:, 3 * LANES :] = d_values[which, :].astype(LOW)


def attend_back(info, own, oth, g_own, g_oth, out, lse, start, cos, sin):
    half = own.shape[0]
    tokens = 2 * half
    outs = (shape((half, 4 * LANES)), shape((half, 4 * LANES)))
    return call(
        attend_back_kernel,
        outs,
        [
            whole(own),
            whole(oth),
            whole(g_own),
            whole(g_oth),
            pl.BlockSpec((TILE, 2 * LANES), lambda b, s: (b, 0)),
            pl.BlockSpec((1, 2 * TILE), lambda b, s: (0, b)),
            whole(start),
            whole(cos),
            whole(sin),
        ],
        tuple(whole(o) for o in outs),
        grid=(tokens // TILE,),
        scratch=(
            pltpu.VMEM((tokens, 4 * LANES), LOW),
            pltpu.VMEM((tokens, 2 * LANES), LOW),
            pltpu.VMEM((LANES, tokens), LOW),
            pltpu.VMEM((tokens, LANES), F32),
            pltpu.VMEM((tokens, LANES), F32),
            pltpu.VMEM((LANES, 2 * TILE), F32),
            pltpu.VMEM((tokens, 2 * LANES), LOW),
        ),
        prefetch=1,
        flops=10 * tokens * tokens * LANES * 2,
        moved=bytes_of(own, oth, g_own, g_oth, out, *outs),
    )(info, own, oth, g_own, g_oth, out, lse, start, cos, sin)


def middle_kernel(*refs):
    weight, second, middle, r2, joined = refs[10:]
    upper = pl.program_id(0) < pl.num_programs(0) // 2
    heads = read_pieces(refs[:5], upper)
    joined[...] = heads
    x = read_pieces(refs[5:10], upper).astype(F32)
    value = x + dot(heads, weight[...])
    inverse = lax.rsqrt(jnp.mean(value * value, axis=1, keepdims=True) + EPSILON)
    second[...] = (value * inverse).astype(LOW)
    middle[...] = value[:, : middle.shape[1]]
    r2[...] = jnp.broadcast_to(inverse, r2.shape)


def middle_of(heads, xs, weight):
    tokens, width = xs[0].shape
    rows = lambda n: pl.BlockSpec((TILE, n), lambda b: (b, 0))
    outs = (
        shape((tokens, 4 * width)),
        shape((tokens, width), F32),
        shape((tokens, LANES), F32),
        shape((tokens, 4 * width)),
    )
    return call(
        middle_kernel,
        outs,
        piece_specs(width, TILE, tokens // TILE) * 2 + [whole(weight)],
        tuple(rows(o.shape[1]) for o in outs),
        grid=(tokens // TILE,),
        flops=2 * tokens * 16 * width * width,
        moved=bytes_of(*heads, *xs, weight, *outs),
    )(*heads, *xs, weight)


def feed_kernel(second, cot, g_own, u_own, g_oth, u_oth, d_own, d_oth, hidden_own, hidden_oth, back_own, back_oth):
    block = pl.program_id(0)
    per = pl.num_programs(0) // 2
    tokens, units = hidden_own.shape
    width = d_own.shape[2]

    def body(gate_w, up_w, down_w, hidden, back, at):
        down = jnp.concatenate([down_w[i] for i in range(4)], axis=1)
        near = pl.ds(pl.multiple_of(at, TILE), TILE)
        far = pl.ds(pl.multiple_of(units + at, TILE), TILE)
        for m in range(0, tokens, TILE):
            rows = slice(m, m + TILE)
            gate = dot(second[rows, :], gate_w[...])
            up = dot(second[rows, :], up_w[...])
            hidden_grad = dot(cot[rows, :], down, NT)
            share = 1.0 / (1.0 + jnp.exp(-gate))
            silu = gate * share
            hidden[rows, near] = (silu * up).astype(LOW)
            back[rows, near] = (hidden_grad * up * share * (1.0 + gate * (1.0 - share))).astype(LOW)
            back[rows, far] = (hidden_grad * silu).astype(LOW)

    @pl.when(block < per)
    def _():
        body(g_own, u_own, d_own, hidden_own, back_own, block * TILE)

    @pl.when(block >= per)
    def _():
        body(g_oth, u_oth, d_oth, hidden_oth, back_oth, (block - per) * TILE)


def feed(second, cot, gu_own, gu_oth, d_own, d_oth):
    tokens, model = second.shape
    units = gu_own.shape[1] // 2
    per = units // TILE
    early = lambda b: jnp.minimum(b, per - 1)
    late = lambda b: jnp.maximum(b - per, 0)
    column = lambda at: pl.BlockSpec((model, TILE), lambda b: (0, at(b)))
    down = lambda at: pl.BlockSpec((4, TILE, model // 4), lambda b: (0, at(b), 0))
    outs = (shape((tokens, units)), shape((tokens, units)), shape((tokens, 2 * units)), shape((tokens, 2 * units)))
    return call(
        feed_kernel,
        outs,
        [
            whole(second),
            whole(cot),
            column(early),
            column(lambda b: per + early(b)),
            column(late),
            column(lambda b: per + late(b)),
            down(early),
            down(late),
        ],
        tuple(whole(o) for o in outs),
        grid=(2 * per,),
        flops=12 * tokens * model * units,
        moved=bytes_of(second, cot, gu_own, gu_oth, d_own, d_oth, *outs),
    )(second, cot, gu_own, gu_own, gu_oth, gu_oth, d_own, d_oth)


def partial_kernel(blocked, a_own, a_oth, w_own, w_oth, *rest):
    upper = pl.program_id(0) < pl.num_programs(0) // 2
    if len(rest) == 7:
        against, own, far_a, near_a, far_b, near_b, sums = rest
    else:
        own, far_a, near_a, far_b, near_b = rest
    width = own.shape[1]
    total = 0.0
    left, right = a_own[...], a_oth[...]
    found = []
    if blocked:
        for k in range(4):
            found.append((dot(left, w_own[k]) + dot(right, w_oth[k])).astype(LOW))
    else:
        value = dot(left, w_own[...], NT) + dot(right, w_oth[...], NT)
        total = jnp.sum(value * against[...].astype(F32), axis=1, keepdims=True)
        low = value.astype(LOW)
        found = [low[:, k * width : (k + 1) * width] for k in range(4)]
    own[...] = found[0]
    if len(rest) == 7:
        sums[...] = jnp.broadcast_to(total, sums.shape)

    @pl.when(upper)
    def _():
        far_a[:, :width] = found[1]
        far_a[:, width:] = found[3]
        near_a[...] = found[2]

    @pl.when(jnp.logical_not(upper))
    def _():
        far_b[:, :width] = found[2]
        far_b[:, width:] = found[3]
        near_b[...] = found[1]


def partial_sums(blocked, a_own, a_oth, w_own, w_oth, against=None):
    tokens, depth = a_own.shape
    model = 4 * w_own.shape[2] if blocked else w_own.shape[0]
    half, width = tokens // 2, model // 4
    blocks = tokens // TILE
    plain = lambda n: pl.BlockSpec((TILE, n), lambda b: (b, 0))
    early = lambda n: pl.BlockSpec((TILE, n), lambda b: (jnp.minimum(b, blocks // 2 - 1), 0))
    late = lambda n: pl.BlockSpec((TILE, n), lambda b: (jnp.maximum(b - blocks // 2, 0), 0))
    outs = [shape((tokens, width))] + [shape((half, 2 * width)), shape((half, width))] * 2
    writes = [plain(width), early(2 * width), early(width), late(2 * width), late(width)]
    args = [a_own, a_oth, w_own, w_oth]
    specs = [plain(depth), plain(depth), whole(w_own), whole(w_oth)]
    if against is not None:
        outs.append(shape((tokens, LANES), F32))
        writes.append(plain(LANES))
        args.append(against)
        specs.append(plain(model))
    found = call(
        functools.partial(partial_kernel, blocked),
        tuple(outs),
        specs,
        tuple(writes),
        grid=(blocks,),
        flops=4 * tokens * depth * model,
        moved=bytes_of(*args, *outs),
    )(*args)
    return found[:5], None if against is None else found[5][:, 0].reshape(8, tokens // 8)


def feed_grads_kernel(second, cot, back, hidden, out):
    double, share = back.shape[1], out.shape[2]
    for columns, left, right in ((slice(0, double), second, back), (slice(double, None), cot, hidden)):
        value = dot(left[...], right[...], TN).astype(LOW)
        for k in range(out.shape[0]):
            out[k, 0, :, columns] = value[k * share : (k + 1) * share]


def feed_grads(second, cot, back, hidden, count):
    tokens, model = second.shape
    width = model // 4
    out = shape((count, 4, width // count, back.shape[1] + hidden.shape[1]))
    block = pl.BlockSpec((tokens, width), lambda i: (0, i))
    return call(
        feed_grads_kernel,
        out,
        [block, block, whole(back), whole(hidden)],
        pl.BlockSpec((count, 1) + out.shape[2:], lambda i: (0, i, 0, 0)),
        grid=(4,),
        flops=2 * tokens * model * out.shape[3],
        moved=bytes_of(second, cot, back, hidden, out),
    )(second, cot, back, hidden)


def mix_grads_kernel(first, back, spread, out, flat):
    @pl.when(pl.program_id(0) == 0)
    def _():
        flat[...] = dot(back[...], spread[...], NT).astype(LOW)

    out[0] = dot(first[...], flat[...], TN).astype(LOW)


def mix_grads(first, back, spread):
    tokens, model = first.shape
    width = model // 4
    out = shape((4, width, spread.shape[0]))
    return call(
        mix_grads_kernel,
        out,
        [pl.BlockSpec((tokens, width), lambda i: (0, i)), whole(back), whole(spread)],
        pl.BlockSpec((1,) + out.shape[1:], lambda i: (i, 0, 0)),
        grid=(4,),
        scratch=(pltpu.VMEM((tokens, spread.shape[0]), LOW),),
        flops=2 * tokens * model * out.shape[2],
        moved=bytes_of(first, back, out),
    )(first, back, spread)


def feed_place_kernel(row_ref, piece, gain, gate, up, down):
    units, share = gate.shape[1], piece.shape[2]
    for k in range(piece.shape[0]):
        rows = slice(k * share, (k + 1) * share)
        gate[rows, :] = piece[k, 0, :, :units].astype(F32) * gain[rows, :]
        up[rows, :] = piece[k, 0, :, units : 2 * units].astype(F32) * gain[rows, :]
    down[...] = jnp.concatenate(
        [piece[k, 0, :, 2 * units :].astype(F32) for k in range(piece.shape[0])], axis=0
    ).T


def feed_place(row, pieces, gain):
    count, _, share, triple = pieces.shape
    units, depth = triple // 3, count * share
    outs = (shape((depth, 4 * units), F32), shape((depth, 4 * units), F32), shape((4 * units, depth), F32))
    return call(
        feed_place_kernel,
        outs,
        [
            pl.BlockSpec((count, 1, share, triple), lambda j, s: (0, jnp.bitwise_xor(s[0], j), 0, 0)),
            whole(gain),
        ],
        (
            pl.BlockSpec((depth, units), lambda j, s: (0, j)),
            pl.BlockSpec((depth, units), lambda j, s: (0, j)),
            pl.BlockSpec((units, depth), lambda j, s: (j, 0)),
        ),
        grid=(4,),
        prefetch=1,
        moved=bytes_of(pieces, *outs),
    )(row, pieces, gain)


def mix_place_kernel(row_ref, pieces, heads, gain, query, key, value, output):
    row = row_ref[0]
    wide, narrow = query.shape[1] // 4, key.shape[1] // 4
    for j in range(4):
        piece = pieces[jnp.bitwise_xor(row, j)].astype(F32) * gain[...]
        query[:, j * wide : (j + 1) * wide] = piece[:, :wide]
        key[:, j * narrow : (j + 1) * narrow] = piece[:, wide : wide + narrow]
        value[:, j * narrow : (j + 1) * narrow] = piece[:, wide + narrow :]
        output[j * wide : (j + 1) * wide, :] = heads[jnp.bitwise_xor(row, j)].astype(F32)


def mix_place(row, pieces, heads, gain):
    _, depth, width = pieces.shape
    wide, narrow = width // 2, width // 4
    outs = (
        shape((depth, 4 * wide), F32),
        shape((depth, 4 * narrow), F32),
        shape((depth, 4 * narrow), F32),
        shape((4 * wide, depth), F32),
    )
    return call(
        mix_place_kernel,
        outs,
        [whole(pieces), whole(heads), whole(gain)],
        tuple(whole(o) for o in outs),
        grid=(1,),
        prefetch=1,
        moved=bytes_of(pieces, heads, *outs),
    )(row, pieces, heads, gain)


def sequence_starts(lengths, tokens):
    places = jnp.arange(tokens, dtype=jnp.int32)
    starts = jnp.zeros((tokens,), jnp.int32)
    end = jnp.zeros((), jnp.int32)
    for k in range(lengths.shape[0]):
        end = end + lengths[k]
        starts = jnp.where(places >= end, end, starts)
    return places, starts


def tables(places):
    lane = jnp.arange(LANES, dtype=jnp.int32)
    entry = lane % (LANES // 2)
    frequency = THETA ** (-2.0 * entry.astype(F32) / HEAD)
    real = entry < SIDE
    angles = places.astype(F32)[:, None] * frequency[None, :]
    cosine = jnp.where(real[None, :], jnp.cos(angles), 0.0)
    sign = jnp.where(lane < LANES // 2, -1.0, 1.0)
    sine = jnp.where(real[None, :], jnp.sin(angles) * sign[None, :], 0.0)
    return cosine, sine


def spread_matrix():
    source = jnp.arange(4 * HEAD, dtype=jnp.int32)
    head, entry = source // HEAD, source % HEAD
    inside = jnp.where((head < 3) & (entry >= SIDE), entry - SIDE + LANES // 2, entry)
    target = head * LANES + inside
    return (target[:, None] == jnp.arange(4 * LANES, dtype=jnp.int32)[None, :]).astype(LOW)


def on_device(
    layer_input,
    first_gain,
    query_weight,
    key_projection_weight,
    value_projection_weight,
    output_weight,
    second_gain,
    gate_weight,
    up_weight,
    down_weight,
    sequence_lengths,
    cotangent,
):
    row = lax.axis_index("row")
    core = lax.axis_index("col")
    place = lax.axis_index("dp")
    blocks = lax.axis_size("dp")
    row_info = row.reshape(1).astype(jnp.int32)
    half, width = layer_input.shape
    tokens, model = 2 * half, 4 * width
    units = gate_weight.shape[1] // 4
    rows = output_weight.shape[0]
    chunk = rows // 4
    relative = [jnp.bitwise_xor(row, i) for i in range(4)]
    live = Live()
    live.x, live.cot = layer_input, cotangent

    live.xs = gather_one(live.x)
    gains = [gain[:, None] for gain in (first_gain, second_gain)]
    packed = pack(row_info, gains[0], query_weight, key_projection_weight, value_projection_weight)
    mixer = [packed[i] for i in range(4)]
    halves, weights = ready(
        fetch_halves(mixer, place, blocks), (gate_weight, up_weight, down_weight, output_weight, gains[1])
    )
    live.mixer_one = fetch_one(halves)
    live.mixer_own, live.lengths = mixer[0], sequence_lengths[0]
    gate, up, down, out, gain = weights
    downs = [lax.dynamic_slice_in_dim(down, relative[i] * units, units, 0) for i in range(4)]
    out_down = [jnp.concatenate([out, downs[i]], axis=0) for i in range(4)]
    scaled = lambda weight, i: (
        lax.dynamic_slice_in_dim(weight, relative[i] * units, units, 1).astype(F32) * gain
    ).astype(LOW)
    gate_up = [jnp.concatenate([scaled(gate, i), scaled(up, i)], axis=1) for i in range(4)]
    live.od_own, live.od_halves = out_down[0], fetch_halves(out_down, place, blocks)
    live.gu_own, live.gu_halves = gate_up[0], fetch_halves(gate_up, place, blocks)
    live.sync()

    halves, mine = ready(gather_halves(live.xs), jnp.stack(live.mixer_one))
    live.xs = gather_two(live.xs, halves)
    live.mixer = (live.mixer_own, mine, fetch_two(mine, blocks))
    places, starts = sequence_starts(live.lengths, tokens)
    live.cos, live.sin = tables(places - starts)
    live.start = starts[None, :]
    last_starts = (starts[TILE - 1 :: TILE] + TILE - 1) // TILE
    live.info = jnp.concatenate([core.reshape(1), starts[::TILE] // TILE, last_starts]).astype(jnp.int32)
    spread = spread_matrix()
    del live.mixer_one, live.mixer_own, live.lengths
    live.sync()

    live.od_one = fetch_one(live.od_halves)
    live.w_own = dot(fetched(*live.mixer, place).reshape(model, 4 * HEAD), spread).astype(LOW)
    live.w_oth = other(live.w_own)
    cos_own = lax.dynamic_slice_in_dim(live.cos, core * half, half, 0)
    sin_own = lax.dynamic_slice_in_dim(live.sin, core * half, half, 0)
    live.first, live.r1, live.qkv, live.send = project(
        live.xs, live.w_own, live.w_oth, cos_own, sin_own
    )
    del live.mixer, live.od_halves
    live.sync()
    halves, send, live.od_mine = ready(live.gu_halves, live.send, jnp.stack(live.od_one))
    live.od_theirs = fetch_two(live.od_mine, blocks)
    live.gu_one = fetch_one(halves)
    live.qkv_got = other(send)
    live.keep, live.send, live.attended, live.lse = attend(live.info, live.qkv, live.qkv_got, live.start)
    del live.od_one, live.gu_halves
    live.sync()
    live.heads = jnp.concatenate([live.keep, other(live.send)], axis=1)
    live.gu_mine = jnp.stack(live.gu_one)
    del live.keep, live.send, live.gu_one
    live.sync()

    live.gu_theirs = fetch_two(live.gu_mine, blocks)
    live.heads = gather_one(live.heads)
    live.cots = gather_one(live.cot)
    live.od_own = fetched(live.od_own, live.od_mine, live.od_theirs, place)
    del live.od_mine, live.od_theirs
    live.sync()

    halves, more = ready(gather_halves(live.heads), gather_halves(live.cots))
    live.heads = gather_two(live.heads, halves)
    live.cots = gather_two(live.cots, more)
    od_oth = other(live.od_own)
    live.out_full, live.out_mine = order(row_info, live.od_own[:, :rows], od_oth[:, :rows])
    live.d_own, live.d_oth = live.od_own[:, rows:], od_oth[:, rows:]
    live.gu_own = fetched(live.gu_own, live.gu_mine, live.gu_theirs, place).reshape(model, 2 * units)
    del live.od_own, live.gu_mine, live.gu_theirs
    live.sync()
    live.gu_oth = other(live.gu_own)
    live.cot_all = join(live.cots)
    del live.cots

    live.second, live.middle, live.r2, live.heads_all = middle_of(live.heads, live.xs, live.out_full)
    del live.heads, live.xs, live.out_full
    live.hid_own, live.hid_oth, live.back_own, live.back_oth = feed(
        live.second, live.cot_all, live.gu_own, live.gu_oth, live.d_own, live.d_oth
    )
    live.sg, live.sums = partial_sums(False, live.back_own, live.back_oth, live.gu_own, live.gu_oth, live.second)
    del live.gu_own, live.gu_oth
    live.sync()

    def added(own, got):
        return (own.astype(F32) + got.astype(F32)).astype(LOW)

    live.sg = scatter_one(live.sg)
    live.sums = (live.sums, swap(live.sums, 1))
    live.feed_oth = feed_grads(live.second, live.cot_all, live.back_oth, live.hid_oth, blocks)
    live.feed_own = feed_grads(live.second, live.cot_all, live.back_own, live.hid_own, blocks)
    del live.back_own, live.back_oth, live.second, live.cot_all
    live.sync()

    halves, sums, feed_oth = ready(scatter_halves(live.sg), live.sums[0] + live.sums[1], live.feed_oth)
    live.sg = scatter_two(live.sg, halves)
    live.sums = (sums, swap(sums, 2))
    live.feed_got = other(feed_oth)
    del live.feed_oth
    live.sync()

    second_grad = scattered(live.sg)
    inner = (live.sums[0] + live.sums[1]).reshape(half)
    r2 = live.r2[:, :1]
    live.middle_grad = (
        live.cot.astype(F32)
        + r2 * second_grad
        - live.middle * (r2 * r2 * inner[:, None] / model)
    )
    live.branch = live.middle_grad.astype(LOW)
    live.branches = gather_one(*ready(live.branch))
    feed_sum = lax.psum_scatter(added(live.feed_own, live.feed_got), "dp", scatter_dimension=0)
    live.fo, _ = partial_sums(True, live.hid_own, live.hid_oth, live.d_own, live.d_oth)
    del live.feed_own, live.feed_got, live.hid_own, live.hid_oth, live.d_own, live.d_oth
    live.gain_part = jnp.sum(second_grad * live.middle * r2, axis=0) / second_gain
    del live.sg, live.sums, live.cot, live.r2
    live.sync()

    live.branches = gather_two(live.branches, ready(*gather_halves(live.branches)))
    live.o_all = dot(live.heads_all, live.branch, TN).astype(LOW).reshape(4, 2, chunk, width)
    del live.heads_all, live.branch
    live.sync()
    live.grad, live.send = heads_grad_of(live.branches, live.out_mine)
    live.grad_got = other(live.send)
    live.o = added(live.o_all[:, 0], other(live.o_all[:, 1]))
    del live.branches, live.out_mine, live.send, live.o_all
    live.sync()

    o_rows, mix_rows, share = (chunk,), (width,), width // blocks
    parts = ready(*chain_parts(1, live.o, o_rows, blocks, []))
    live.o_moving = chain_sum(1, parts, blocks, [])
    live.fo = scatter_one(live.fo)
    live.bk, live.send = attend_back(
        live.info, live.qkv, live.qkv_got, live.grad, live.grad_got,
        live.attended, live.lse, live.start, live.cos, live.sin,
    )
    del live.qkv, live.qkv_got, live.grad, live.grad_got, live.attended, live.lse, live.start, live.info
    live.sync()

    halves, send, parts = ready(
        scatter_halves(live.fo), live.send, chain_parts(2, live.o, o_rows, blocks, live.o_moving)
    )
    live.o_moving = chain_sum(2, parts, blocks, live.o_moving)
    live.fo = scatter_two(live.fo, halves)
    live.bg = other(send)
    live.mix_oth = mix_grads(live.first, live.bg, spread)
    live.mix_own = mix_grads(live.first, live.bk, spread)
    del live.send
    live.sync()
    live.feed_sum = spread_row(feed_sum)
    live.mix = added(live.mix_own, other(live.mix_oth))
    live.moving = chain_sum(1, chain_parts(1, live.mix, mix_rows, blocks, []), blocks, [])
    del live.mix_own, live.mix_oth
    live.sync()
    parts, more, (bk, bg) = ready(
        chain_parts(2, live.mix, mix_rows, blocks, live.moving),
        chain_parts(3, live.o, o_rows, blocks, live.o_moving),
        (live.bk, live.bg),
    )
    live.moving = chain_sum(2, parts, blocks, live.moving)
    live.o_moving = chain_sum(3, more, blocks, live.o_moving)
    feeds = lax.all_gather(live.feed_sum, "dp", axis=0)
    live.fg, live.sums = partial_sums(False, bk, bg, live.w_own, live.w_oth, live.first)
    del live.bk, live.bg, live.w_own, live.w_oth, live.first
    live.sync()

    live.o_moving = chain_sums(4, live.o, o_rows, blocks, live.o_moving)
    live.o = chain_summed(live.o, o_rows, blocks, live.o_moving)
    del live.o_moving
    parts = ready(*chain_parts(3, live.mix, mix_rows, blocks, live.moving))
    live.moving = chain_sum(3, parts, blocks, live.moving)
    live.fg = scatter_one(live.fg)
    live.sums = (live.sums, swap(live.sums, 1))
    layer_output = (live.middle + scattered(live.fo)).astype(LOW)
    del live.fo, live.middle, live.feed_sum
    live.sync()

    live.moving = chain_sums(4, live.mix, mix_rows, blocks, live.moving)
    halves, sums, shard = ready(
        scatter_halves(live.fg),
        live.sums[0] + live.sums[1],
        chain_summed(live.mix, mix_rows, blocks, live.moving),
    )
    live.fg = scatter_two(live.fg, halves)
    live.sums = (sums, swap(sums, 2))
    live.mix = spread_row(shard)
    del live.moving
    live.sync()

    first_grad = scattered(live.fg)
    inner = (live.sums[0] + live.sums[1]).reshape(half)
    r1 = live.r1[:, :1]
    inputs = live.x.astype(F32)
    input_gradient = (
        live.middle_grad
        + r1 * first_grad
        - inputs * (r1 * r1 * inner[:, None] / model)
    )
    gains = jnp.stack([jnp.sum(first_grad * inputs * r1, axis=0) / first_gain, live.gain_part])
    carried = split_low(gains + other(gains))[None]
    carried = jnp.concatenate([carried, jnp.zeros((3,) + carried.shape[1:], LOW)], axis=0)
    live.mix = jnp.concatenate([live.mix, live.o, carried], axis=1)
    del live.fg, live.sums, live.r1, live.x, live.middle_grad, live.gain_part, live.o
    live.sync()
    live.moving = chain_spread(1, 2, live.mix, blocks, [])
    live.sync()
    live.moving = chain_spread(2, 3, live.mix, blocks, live.moving)
    placed = feed_place(row_info, feeds, second_gain[:, None])
    live.placed = placed
    live.sync()
    moving = chain_spread(3, blocks, live.mix, blocks, live.moving)
    mixes = chain_joined(live.mix, blocks, moving)
    gate_total, up_total, down_total = live.placed
    last = share + chunk // blocks
    query_total, key_total, value_total, output_total = mix_place(
        row_info,
        mixes[:, :, :share].reshape(4, width, width),
        mixes[:, :, share:last].reshape(4, chunk, width),
        first_gain[:, None],
    )
    gain_total = sum(unsplit(mixes[0, k, last:], 2) for k in range(blocks))
    return (
        layer_output,
        input_gradient,
        query_total,
        key_total,
        value_total,
        output_total,
        gate_total,
        up_total,
        down_total,
        gain_total[0],
        gain_total[1],
    )


def solution(mesh):
    return jax.shard_map(
        on_device,
        mesh=mesh,
        in_specs=(
            P(("dp", "col"), "row"),
            P("row"),
            P("row", "col"),
            P("row", "col"),
            P("row", "col"),
            P("col", "row"),
            P("row"),
            P("row", "col"),
            P("row", "col"),
            P("col", "row"),
            P("dp", None),
            P(("dp", "col"), "row"),
        ),
        out_specs=(
            P(("dp", "col"), "row"),
            P(("dp", "col"), "row"),
            P("row", "col"),
            P("row", "col"),
            P("row", "col"),
            P("col", "row"),
            P("row", "col"),
            P("row", "col"),
            P("col", "row"),
            P("row"),
            P("row"),
        ),
        check_vma=False,
    )
```

```python
import functools

import jax
import jax.numpy as jnp
from jax import lax
from jax.experimental import pallas as pl
from jax.experimental.pallas import tpu as pltpu
from jax.sharding import PartitionSpec as P

HEAD = 96
LANES = 128
SIDE = 48
TILE = 256
EPSILON = 1e-05
THETA = 100000.0
LOG2E = 1.4426950408889634
FACTOR = HEAD**-0.5
LOW = jnp.bfloat16
F32 = jnp.float32
NN = (((1,), (0,)), ((), ()))
NT = (((1,), (1,)), ((), ()))
TN = (((0,), (0,)), ((), ()))
VMEM_LIMIT = 48 * 1024 * 1024
WEIGHT = 1 / 64


def dot(left, right, dims=NN):
    return lax.dot_general(left, right, dims, preferred_element_type=F32)


def swap(value, step):
    return lax.ppermute(value, "row", [(i, i ^ step) for i in range(4)])


def other(value):
    return lax.ppermute(value, "col", [(0, 1), (1, 0)])


def pair(value, count):
    return lax.ppermute(value, "dp", [(i, i ^ 1) for i in range(count)])


def spread_row(shard):
    return jnp.stack([shard[0]] + [swap(shard[i], i) for i in (1, 2, 3)])


class Live:
    def sync(self):
        self.__dict__.update(lax.optimization_barrier(dict(self.__dict__)))


def ready(*values):
    return lax.optimization_barrier(values)


def gather_one(value):
    return [value, swap(value, 1), swap(value, 2)]


def gather_halves(found):
    half = found[0].shape[0] // 2
    return found[1][:half], found[2][half:]


def gather_two(found, halves):
    return found + [swap(halves[0], 2), swap(halves[1], 1)]


def fetch_halves(pieces, place, count):
    parts = 2 if count % 2 == 0 else 1
    rows = pieces[0].shape[0] // parts
    at = (place % parts) * rows
    return [lax.dynamic_slice_in_dim(pieces[i], at, rows, 0) for i in (1, 2, 3)]


def fetch_one(halves):
    return [swap(half, i) for i, half in enumerate(halves, 1)]


def fetch_two(mine, count):
    return pair(mine, count) if count % 2 == 0 else ()


def fetched(own, mine, theirs, place):
    if isinstance(theirs, tuple):
        return jnp.concatenate([own[None], mine])
    rows = mine.shape[1]
    bit = place % 2
    zero = jnp.zeros((), jnp.int32)
    result = jnp.zeros((4,) + own.shape, own.dtype)
    result = lax.dynamic_update_slice(result, own[None], (0, 0, 0))
    result = lax.dynamic_update_slice(result, mine, (zero + 1, bit * rows, zero))
    return lax.dynamic_update_slice(result, theirs, (zero + 1, (1 - bit) * rows, zero))


def scatter_one(parts):
    own, far_a, near_a, far_b, near_b = parts
    return own, swap(far_a, 1), near_a, swap(far_b, 2), near_b


def scatter_halves(parts):
    own, got_a, near_a, got_b, near_b = parts
    width = own.shape[1]
    send_a = (near_a.astype(F32) + got_a[:, width:].astype(F32)).astype(LOW)
    send_b = (near_b.astype(F32) + got_b[:, width:].astype(F32)).astype(LOW)
    return send_a, send_b


def scatter_two(parts, halves):
    own, got_a, _, got_b, _ = parts
    return own, got_a, swap(halves[0], 2), got_b, swap(halves[1], 1)


def scattered(parts):
    own, got_a, last_a, got_b, last_b = parts
    width, half = own.shape[1], got_a.shape[0]
    upper = own[:half].astype(F32) + got_a[:, :width].astype(F32) + last_a.astype(F32)
    lower = own[half:].astype(F32) + got_b[:, :width].astype(F32) + last_b.astype(F32)
    return jnp.concatenate([upper, lower], axis=0)


def shard_of(total, rows, number, count):
    found, at = [], 0
    for part in rows:
        size = part // count
        found.append(lax.dynamic_slice_in_dim(total, at + number * size, size, 1))
        at = at + part
    return found[0] if len(found) == 1 else jnp.concatenate(found, axis=1)


def turn(value, step, count):
    return lax.ppermute(value, "dp", [(i, (i + step) % count) for i in range(count)])


def chain_up(count, first, last):
    return [(i, i + 1) for i in range(first, last)]


def chain_down(count, first, last):
    return [(count - 1 - i, count - 2 - i) for i in range(first, last)]


def chain_parts(step, total, rows, count, before):
    if step >= count:
        return ()
    place = lax.axis_index("dp")
    up = shard_of(total, rows, jnp.clip(count - step + place, 0, count - 1), count)
    down = shard_of(total, rows, jnp.clip(place - (count - step), 0, count - 1), count)
    if before:
        up = (up.astype(F32) + before[0].astype(F32)).astype(LOW)
        down = (down.astype(F32) + before[1].astype(F32)).astype(LOW)
    return up, down


def chain_sum(step, parts, count, before):
    if step >= count:
        return before
    last = min(step, count - 1)
    up, down = parts
    return [lax.ppermute(up, "dp", chain_up(count, 0, last)), lax.ppermute(down, "dp", chain_down(count, 0, last))]


def chain_sums(first, total, rows, count, before):
    for step in range(first, count):
        before = chain_sum(step, chain_parts(step, total, rows, count, before), count, before)
    return before


def chain_summed(total, rows, count, before):
    own = shard_of(total, rows, lax.axis_index("dp"), count)
    if before:
        own = (own.astype(F32) + before[0].astype(F32) + before[1].astype(F32)).astype(LOW)
    return own


def chain_spread(first, last, shard, count, found):
    for step in range(first, min(last, count)):
        up, down = found[-1] if found else (shard, shard)
        up = lax.ppermute(up, "dp", chain_up(count, step - 1, count - 1))
        down = lax.ppermute(down, "dp", chain_down(count, step - 1, count - 1))
        found = found + [(up, down)]
    return found


def chain_joined(shard, count, found):
    place = lax.axis_index("dp")
    dims = (shard.shape[0], count) + shard.shape[1:]
    zero = jnp.zeros((), jnp.int32)
    result = jnp.zeros(dims, shard.dtype)

    def put(result, piece, at):
        return lax.dynamic_update_slice(result, piece[:, None], (zero, at) + (zero,) * (len(dims) - 2))

    for step, (up, down) in enumerate(found, 1):
        result = put(result, up, jnp.where(place - step >= 0, place - step, place))
        result = put(result, down, jnp.where(place + step < count, place + step, place))
    return put(result, shard, place)


def call(kernel, out_shape, in_specs, out_specs, grid=(), scratch=(), prefetch=0, flops=0, moved=0):
    return pl.pallas_call(
        kernel,
        out_shape=out_shape,
        grid_spec=pltpu.PrefetchScalarGridSpec(
            num_scalar_prefetch=prefetch,
            grid=grid,
            in_specs=in_specs,
            out_specs=out_specs,
            scratch_shapes=list(scratch),
        ),
        compiler_params=pltpu.CompilerParams(vmem_limit_bytes=VMEM_LIMIT),
        cost_estimate=pl.CostEstimate(
            flops=int(flops * WEIGHT), bytes_accessed=int(moved * WEIGHT), transcendentals=0
        ),
    )


def shape(dims, kind=LOW):
    return jax.ShapeDtypeStruct(tuple(dims), kind)


def whole(array):
    rank = len(array.shape)
    return pl.BlockSpec(tuple(array.shape), lambda *_: (0,) * rank)


def bytes_of(*arrays):
    return sum(int(a.size) * a.dtype.itemsize for a in arrays)


def read_pieces(refs, upper):
    x0, x1, x2, top, bottom = refs
    return jnp.concatenate([x0[...], x1[...], x2[...], jnp.where(upper, top[...], bottom[...])], axis=1)


def piece_specs(width, tile, blocks, shift=0):
    halfway = blocks // 2
    plain = pl.BlockSpec((tile, width), lambda b, *_: (b + shift, 0))
    top = pl.BlockSpec((tile, width), lambda b, *_: (jnp.minimum(b + shift, halfway - 1), 0))
    bottom = pl.BlockSpec((tile, width), lambda b, *_: (jnp.maximum(b + shift - halfway, 0), 0))
    return [plain, plain, plain, top, bottom]


def join_kernel(x0, x1, x2, top, bottom, out):
    width, half = x0.shape[1], top.shape[0]
    for i, ref in enumerate((x0, x1, x2)):
        out[:, i * width : (i + 1) * width] = ref[...]
    out[:half, 3 * width :] = top[...]
    out[half:, 3 * width :] = bottom[...]


def join(pieces):
    tokens, width = pieces[0].shape
    out = shape((tokens, 4 * width))
    return call(
        join_kernel, out, [whole(p) for p in pieces], whole(out), grid=(1,), moved=2 * bytes_of(out)
    )(*pieces)


def split_low(value):
    high = lax.reduce_precision(value, 8, 7)
    rest = value - high
    middle = lax.reduce_precision(rest, 8, 7)
    terms = [high, middle, rest - middle]
    spare = jnp.zeros((16 - 3 * value.shape[0], value.shape[1]), F32)
    return jnp.concatenate(terms + [spare], axis=0).astype(LOW)


def unsplit(rows, count):
    terms = [rows[i * count : (i + 1) * count].astype(F32) for i in range(3)]
    return terms[0] + terms[1] + terms[2]


def order_kernel(row_ref, own, oth, full, mine):
    row = row_ref[0]
    features, chunk = own.shape[2], own.shape[1] // 4
    for k in range(4):
        columns = slice(k * features, (k + 1) * features)
        for i in range(4):
            rows = pl.ds(pl.multiple_of(jnp.bitwise_xor(row, i) * chunk, chunk), chunk)
            for s, weight in enumerate((own, oth)):
                at = (2 * i + s) * chunk
                full[at : at + chunk, columns] = weight[k, rows, :]
    mine[...] = jnp.zeros(mine.shape, mine.dtype)
    for h in range(2 * chunk // HEAD):
        mine[h * LANES : h * LANES + HEAD, :] = full[h * HEAD : (h + 1) * HEAD, :]


def order(row, own, oth):
    _, rows, features = own.shape
    full, mine = shape((2 * rows, 4 * features)), shape((2 * rows // 4 // HEAD * LANES, 4 * features))
    return call(
        order_kernel,
        (full, mine),
        [whole(own), whole(oth)],
        (whole(full), whole(mine)),
        grid=(1,),
        prefetch=1,
        moved=2 * bytes_of(full) + bytes_of(mine),
    )(row, own, oth)


def heads_grad_kernel(x0, x1, x2, top, bottom, weight, own, oth):
    upper = pl.program_id(0) < pl.num_programs(0) // 2
    grad = dot(read_pieces((x0, x1, x2, top, bottom), upper), weight[...], NT).astype(LOW)
    own[...] = grad[:, : own.shape[1]]
    oth[...] = grad[:, own.shape[1] :]


def heads_grad_of(pieces, weight):
    tokens, width = pieces[0].shape
    columns = weight.shape[0] // 2
    outs = (shape((tokens, columns)), shape((tokens, columns)))
    rows = pl.BlockSpec((TILE, columns), lambda b: (b, 0))
    return call(
        heads_grad_kernel,
        outs,
        piece_specs(width, TILE, tokens // TILE) + [whole(weight)],
        (rows, rows),
        grid=(tokens // TILE,),
        flops=2 * tokens * 4 * width * weight.shape[0],
        moved=bytes_of(*pieces, weight, *outs),
    )(*pieces, weight)


def pack_kernel(row_ref, gain_ref, q_ref, k_ref, v_ref, out_ref):
    row = row_ref[0]
    gain = gain_ref[...]
    query, key = q_ref.shape[1] // 4, k_ref.shape[1] // 4
    scaled = lambda ref, size, j: (ref[:, j * size : (j + 1) * size].astype(F32) * gain).astype(LOW)
    for j in range(4):
        at = jnp.bitwise_xor(row, j)
        out_ref[at, :, :query] = scaled(q_ref, query, j)
        out_ref[at, :, query : query + key] = scaled(k_ref, key, j)
        out_ref[at, :, query + key :] = scaled(v_ref, key, j)


def pack(row, gain, query_weight, key_weight, value_weight):
    depth = query_weight.shape[0]
    width = (query_weight.shape[1] + 2 * key_weight.shape[1]) // 4
    out = shape((4, depth, width))
    arrays = (gain, query_weight, key_weight, value_weight)
    return call(
        pack_kernel,
        out,
        [whole(a) for a in arrays],
        whole(out),
        grid=(1,),
        prefetch=1,
        moved=2 * bytes_of(out),
    )(row, *arrays)


def project_kernel(x0, x1, x2, top, bottom, w_own, w_oth, cos, sin, first, r1, own, oth):
    upper = pl.program_id(0) < pl.num_programs(0) // 2
    x = read_pieces((x0, x1, x2, top, bottom), upper).astype(F32)
    inverse = lax.rsqrt(jnp.mean(x * x, axis=1, keepdims=True) + EPSILON)
    normed = (x * inverse).astype(LOW)
    first[...] = normed
    r1[...] = jnp.broadcast_to(inverse, r1.shape)
    for weight, out in ((w_own, own), (w_oth, oth)):
        heads = dot(normed, weight[...])
        for h in range(3):
            part = heads[:, h * LANES : (h + 1) * LANES]
            turned = part * cos[...] + pltpu.roll(part, LANES // 2, 1) * sin[...]
            out[:, h * LANES : (h + 1) * LANES] = turned.astype(LOW)
        out[:, 3 * LANES :] = heads[:, 3 * LANES :].astype(LOW)


def project(xs, w_own, w_oth, cos, sin):
    tokens, width = xs[0].shape
    rows = lambda n: pl.BlockSpec((TILE, n), lambda b: (b, 0))
    outs = (shape((tokens, 4 * width)), shape((tokens, LANES), F32), shape((tokens, 512)), shape((tokens, 512)))
    return call(
        project_kernel,
        outs,
        piece_specs(width, TILE, tokens // TILE)
        + [whole(w_own), whole(w_oth), rows(LANES), rows(LANES)],
        tuple(rows(o.shape[1]) for o in outs),
        grid=(tokens // TILE,),
        flops=2 * tokens * 4 * width * 1024,
        moved=bytes_of(*xs, w_own, w_oth, *outs),
    )(*xs, w_own, w_oth, cos, sin)


def stack_heads(ref, rows):
    return jnp.concatenate([ref[rows, :LANES], ref[rows, LANES : 2 * LANES]], axis=0)


def block_limits(start_ref, block):
    rows = pl.ds(pl.multiple_of(block * TILE, TILE), TILE)
    start = start_ref[:, rows]
    query = block * TILE + lax.broadcasted_iota(jnp.int32, (1, TILE), 1)
    return jnp.concatenate([start, start], axis=1), jnp.concatenate([query, query], axis=1)


def allowed_keys(number, start, query):
    key = number * TILE + lax.broadcasted_iota(jnp.int32, (TILE, 2 * TILE), 0)
    return (key >= start) & (key <= query)


def over_keys(info, block, step):
    count = (info.shape[0] - 1) // 2
    first, whole_from = info[1 + block], jnp.minimum(info[1 + count + block], block)

    def masked(number, carry):
        step(number, True)
        return carry

    def plain(number, carry):
        step(number, False)
        return carry

    lax.fori_loop(first, whole_from, masked, 0)
    def both(pair, carry):
        step(whole_from + 2 * pair, False)
        step(whole_from + 2 * pair + 1, False)
        return carry

    pairs = (block - whole_from) // 2
    lax.fori_loop(0, pairs, both, 0)
    lax.fori_loop(whole_from + 2 * pairs, block, plain, 0)
    step(block, True)


def attend_kernel(info, own, oth, start_ref, keep, send, out, lse, full, values, top, total, acc):
    block = pl.program_id(0)
    core = info[0]
    half = own.shape[0]

    @pl.when(block == 0)
    def _():
        full[pl.ds(pl.multiple_of(core * half, half), half), :] = own[...]
        full[pl.ds(pl.multiple_of((1 - core) * half, half), half), :] = oth[...]
        values[...] = full[:, 3 * LANES :].T

    rows = pl.ds(pl.multiple_of(block * TILE, TILE), TILE)
    query = stack_heads(full, rows)
    start, place = block_limits(start_ref, block)
    top[...] = jnp.full(top.shape, -1e30, F32)
    total[...] = jnp.zeros(total.shape, F32)
    acc[...] = jnp.zeros(acc.shape, F32)

    def step(number, masked):
        keys = pl.ds(pl.multiple_of(number * TILE, TILE), TILE)
        scores = dot(full[keys, 2 * LANES : 3 * LANES], query, NT) * (FACTOR * LOG2E)
        if masked:
            scores = jnp.where(allowed_keys(number, start, place), scores, -1e30)
        before = top[...]
        now = jnp.maximum(before, jnp.max(scores, axis=0, keepdims=True))
        weight = jnp.exp2(scores - now)
        scale = jnp.exp2(before - now)
        top[...] = now
        total[...] = total[...] * scale + jnp.sum(weight, axis=0, keepdims=True)
        acc[...] = acc[...] * scale + dot(values[:, keys], weight.astype(LOW))

    over_keys(info, block, step)
    lse[...] = top[...] + jnp.log2(total[...])
    result = (acc[...] / total[...]).T.astype(LOW)
    out[:, :LANES] = result[:TILE]
    out[:, LANES:] = result[TILE:]
    mine = (block // (half // TILE)) == core
    for target, wanted in ((keep, mine), (send, jnp.logical_not(mine))):

        @pl.when(wanted)
        def _(target=target):
            target[:, :HEAD] = result[:TILE, :HEAD]
            target[:, HEAD:] = result[TILE:, :HEAD]


def attend(info, own, oth, start):
    half = own.shape[0]
    tokens = 2 * half
    per_half = half // TILE
    outs = (
        shape((half, 2 * HEAD)),
        shape((half, 2 * HEAD)),
        shape((tokens, 2 * LANES)),
        shape((1, 2 * tokens), F32),
    )
    return call(
        attend_kernel,
        outs,
        [whole(own), whole(oth), whole(start)],
        (
            pl.BlockSpec((TILE, 2 * HEAD), lambda b, s: (jnp.clip(b - s[0] * per_half, 0, per_half - 1), 0)),
            pl.BlockSpec((TILE, 2 * HEAD), lambda b, s: (jnp.clip(b - (1 - s[0]) * per_half, 0, per_half - 1), 0)),
            pl.BlockSpec((TILE, 2 * LANES), lambda b, s: (b, 0)),
            pl.BlockSpec((1, 2 * TILE), lambda b, s: (0, b)),
        ),
        grid=(tokens // TILE,),
        scratch=(
            pltpu.VMEM((tokens, 4 * LANES), LOW),
            pltpu.VMEM((LANES, tokens), LOW),
            pltpu.VMEM((1, 2 * TILE), F32),
            pltpu.VMEM((1, 2 * TILE), F32),
            pltpu.VMEM((LANES, 2 * TILE), F32),
        ),
        prefetch=1,
        flops=4 * tokens * tokens * LANES * 2,
        moved=bytes_of(own, oth, *outs),
    )(info, own, oth, start)


def turn_back(part, cos, sin):
    return part * cos - pltpu.roll(part, LANES // 2, 1) * sin


def attend_back_kernel(
    info, own, oth, g_own, g_oth, out, lse, start_ref, cos, sin,
    keep, send, full, grads, keys_t, d_keys, d_values, d_query, result,
):
    block = pl.program_id(0)
    core = info[0]
    half = own.shape[0]

    @pl.when(block == 0)
    def _():
        mine = pl.ds(pl.multiple_of(core * half, half), half)
        theirs = pl.ds(pl.multiple_of((1 - core) * half, half), half)
        full[mine, :] = own[...]
        full[theirs, :] = oth[...]
        grads[mine, :] = g_own[...]
        grads[theirs, :] = g_oth[...]
        keys_t[...] = full[:, 2 * LANES : 3 * LANES].T
        d_keys[...] = jnp.zeros(d_keys.shape, F32)
        d_values[...] = jnp.zeros(d_values.shape, F32)

    rows = pl.ds(pl.multiple_of(block * TILE, TILE), TILE)
    query = stack_heads(full, rows)
    grad = stack_heads(grads, rows)
    reply = stack_heads(out, slice(None))
    start, place = block_limits(start_ref, block)
    level = lse[...]
    delta = jnp.sum((grad.astype(F32) * reply.astype(F32)).T, axis=0, keepdims=True)
    d_query[...] = jnp.zeros(d_query.shape, F32)

    def step(number, masked):
        keys = pl.ds(pl.multiple_of(number * TILE, TILE), TILE)
        scores = dot(full[keys, 2 * LANES : 3 * LANES], query, NT) * (FACTOR * LOG2E)
        if masked:
            scores = jnp.where(allowed_keys(number, start, place), scores, -1e30)
        weight = jnp.exp2(scores - level)
        pressure = dot(full[keys, 3 * LANES :], grad, NT)
        slope = (weight * (pressure - delta) * FACTOR).astype(LOW)
        d_values[keys, :] += dot(weight.astype(LOW), grad)
        d_keys[keys, :] += dot(slope, query)
        d_query[...] += dot(keys_t[:, keys], slope)

    over_keys(info, block, step)
    turned = d_query[...].T
    for h in range(2):
        part = turned[h * TILE : (h + 1) * TILE]
        result[rows, h * LANES : (h + 1) * LANES] = turn_back(part, cos[rows, :], sin[rows, :]).astype(LOW)

    @pl.when(block == pl.num_programs(0) - 1)
    def _():
        mine = pl.ds(pl.multiple_of(core * half, half), half)
        theirs = pl.ds(pl.multiple_of((1 - core) * half, half), half)
        for target, which in ((keep, mine), (send, theirs)):
            target[:, : 2 * LANES] = result[which, :]
            target[:, 2 * LANES : 3 * LANES] = turn_back(
                d_keys[which, :], cos[which, :], sin[which, :]
            ).astype(LOW)
            target[:, 3 * LANES :] = d_values[which, :].astype(LOW)


def attend_back(info, own, oth, g_own, g_oth, out, lse, start, cos, sin):
    half = own.shape[0]
    tokens = 2 * half
    outs = (shape((half, 4 * LANES)), shape((half, 4 * LANES)))
    return call(
        attend_back_kernel,
        outs,
        [
            whole(own),
            whole(oth),
            whole(g_own),
            whole(g_oth),
            pl.BlockSpec((TILE, 2 * LANES), lambda b, s: (b, 0)),
            pl.BlockSpec((1, 2 * TILE), lambda b, s: (0, b)),
            whole(start),
            whole(cos),
            whole(sin),
        ],
        tuple(whole(o) for o in outs),
        grid=(tokens // TILE,),
        scratch=(
            pltpu.VMEM((tokens, 4 * LANES), LOW),
            pltpu.VMEM((tokens, 2 * LANES), LOW),
            pltpu.VMEM((LANES, tokens), LOW),
            pltpu.VMEM((tokens, LANES), F32),
            pltpu.VMEM((tokens, LANES), F32),
            pltpu.VMEM((LANES, 2 * TILE), F32),
            pltpu.VMEM((tokens, 2 * LANES), LOW),
        ),
        prefetch=1,
        flops=10 * tokens * tokens * LANES * 2,
        moved=bytes_of(own, oth, g_own, g_oth, out, *outs),
    )(info, own, oth, g_own, g_oth, out, lse, start, cos, sin)


def middle_kernel(*refs):
    weight, second, middle, r2, joined = refs[10:]
    upper = pl.program_id(0) < pl.num_programs(0) // 2
    heads = read_pieces(refs[:5], upper)
    joined[...] = heads
    x = read_pieces(refs[5:10], upper).astype(F32)
    value = x + dot(heads, weight[...])
    inverse = lax.rsqrt(jnp.mean(value * value, axis=1, keepdims=True) + EPSILON)
    second[...] = (value * inverse).astype(LOW)
    middle[...] = value[:, : middle.shape[1]]
    r2[...] = jnp.broadcast_to(inverse, r2.shape)


def middle_of(heads, xs, weight):
    tokens, width = xs[0].shape
    rows = lambda n: pl.BlockSpec((TILE, n), lambda b: (b, 0))
    outs = (
        shape((tokens, 4 * width)),
        shape((tokens, width), F32),
        shape((tokens, LANES), F32),
        shape((tokens, 4 * width)),
    )
    return call(
        middle_kernel,
        outs,
        piece_specs(width, TILE, tokens // TILE) * 2 + [whole(weight)],
        tuple(rows(o.shape[1]) for o in outs),
        grid=(tokens // TILE,),
        flops=2 * tokens * 16 * width * width,
        moved=bytes_of(*heads, *xs, weight, *outs),
    )(*heads, *xs, weight)


def feed_kernel(second, cot, g_own, u_own, g_oth, u_oth, d_own, d_oth, hidden_own, hidden_oth, back_own, back_oth):
    block = pl.program_id(0)
    per = pl.num_programs(0) // 2
    tokens, units = hidden_own.shape
    width = d_own.shape[2]

    def body(gate_w, up_w, down_w, hidden, back, at):
        down = jnp.concatenate([down_w[i] for i in range(4)], axis=1)
        near = pl.ds(pl.multiple_of(at, TILE), TILE)
        far = pl.ds(pl.multiple_of(units + at, TILE), TILE)
        for m in range(0, tokens, TILE):
            rows = slice(m, m + TILE)
            gate = dot(second[rows, :], gate_w[...])
            up = dot(second[rows, :], up_w[...])
            hidden_grad = dot(cot[rows, :], down, NT)
            share = 1.0 / (1.0 + jnp.exp(-gate))
            silu = gate * share
            hidden[rows, near] = (silu * up).astype(LOW)
            back[rows, near] = (hidden_grad * up * share * (1.0 + gate * (1.0 - share))).astype(LOW)
            back[rows, far] = (hidden_grad * silu).astype(LOW)

    @pl.when(block < per)
    def _():
        body(g_own, u_own, d_own, hidden_own, back_own, block * TILE)

    @pl.when(block >= per)
    def _():
        body(g_oth, u_oth, d_oth, hidden_oth, back_oth, (block - per) * TILE)


def feed(second, cot, gu_own, gu_oth, d_own, d_oth):
    tokens, model = second.shape
    units = gu_own.shape[1] // 2
    per = units // TILE
    early = lambda b: jnp.minimum(b, per - 1)
    late = lambda b: jnp.maximum(b - per, 0)
    column = lambda at: pl.BlockSpec((model, TILE), lambda b: (0, at(b)))
    down = lambda at: pl.BlockSpec((4, TILE, model // 4), lambda b: (0, at(b), 0))
    outs = (shape((tokens, units)), shape((tokens, units)), shape((tokens, 2 * units)), shape((tokens, 2 * units)))
    return call(
        feed_kernel,
        outs,
        [
            whole(second),
            whole(cot),
            column(early),
            column(lambda b: per + early(b)),
            column(late),
            column(lambda b: per + late(b)),
            down(early),
            down(late),
        ],
        tuple(whole(o) for o in outs),
        grid=(2 * per,),
        flops=12 * tokens * model * units,
        moved=bytes_of(second, cot, gu_own, gu_oth, d_own, d_oth, *outs),
    )(second, cot, gu_own, gu_own, gu_oth, gu_oth, d_own, d_oth)


def partial_kernel(blocked, a_own, a_oth, w_own, w_oth, *rest):
    upper = pl.program_id(0) < pl.num_programs(0) // 2
    if len(rest) == 7:
        against, own, far_a, near_a, far_b, near_b, sums = rest
    else:
        own, far_a, near_a, far_b, near_b = rest
    width = own.shape[1]
    total = 0.0
    left, right = a_own[...], a_oth[...]
    found = []
    if blocked:
        for k in range(4):
            found.append((dot(left, w_own[k]) + dot(right, w_oth[k])).astype(LOW))
    else:
        value = dot(left, w_own[...], NT) + dot(right, w_oth[...], NT)
        total = jnp.sum(value * against[...].astype(F32), axis=1, keepdims=True)
        low = value.astype(LOW)
        found = [low[:, k * width : (k + 1) * width] for k in range(4)]
    own[...] = found[0]
    if len(rest) == 7:
        sums[...] = jnp.broadcast_to(total, sums.shape)

    @pl.when(upper)
    def _():
        far_a[:, :width] = found[1]
        far_a[:, width:] = found[3]
        near_a[...] = found[2]

    @pl.when(jnp.logical_not(upper))
    def _():
        far_b[:, :width] = found[2]
        far_b[:, width:] = found[3]
        near_b[...] = found[1]


def partial_sums(blocked, a_own, a_oth, w_own, w_oth, against=None):
    tokens, depth = a_own.shape
    model = 4 * w_own.shape[2] if blocked else w_own.shape[0]
    half, width = tokens // 2, model // 4
    blocks = tokens // TILE
    plain = lambda n: pl.BlockSpec((TILE, n), lambda b: (b, 0))
    early = lambda n: pl.BlockSpec((TILE, n), lambda b: (jnp.minimum(b, blocks // 2 - 1), 0))
    late = lambda n: pl.BlockSpec((TILE, n), lambda b: (jnp.maximum(b - blocks // 2, 0), 0))
    outs = [shape((tokens, width))] + [shape((half, 2 * width)), shape((half, width))] * 2
    writes = [plain(width), early(2 * width), early(width), late(2 * width), late(width)]
    args = [a_own, a_oth, w_own, w_oth]
    specs = [plain(depth), plain(depth), whole(w_own), whole(w_oth)]
    if against is not None:
        outs.append(shape((tokens, LANES), F32))
        writes.append(plain(LANES))
        args.append(against)
        specs.append(plain(model))
    found = call(
        functools.partial(partial_kernel, blocked),
        tuple(outs),
        specs,
        tuple(writes),
        grid=(blocks,),
        flops=4 * tokens * depth * model,
        moved=bytes_of(*args, *outs),
    )(*args)
    return found[:5], None if against is None else found[5][:, 0].reshape(8, tokens // 8)


def feed_grads_kernel(second, cot, back, hidden, out):
    double, share = back.shape[1], out.shape[2]
    for columns, left, right in ((slice(0, double), second, back), (slice(double, None), cot, hidden)):
        value = dot(left[...], right[...], TN).astype(LOW)
        for k in range(out.shape[0]):
            out[k, 0, :, columns] = value[k * share : (k + 1) * share]


def feed_grads(second, cot, back, hidden, count):
    tokens, model = second.shape
    width = model // 4
    out = shape((count, 4, width // count, back.shape[1] + hidden.shape[1]))
    block = pl.BlockSpec((tokens, width), lambda i: (0, i))
    return call(
        feed_grads_kernel,
        out,
        [block, block, whole(back), whole(hidden)],
        pl.BlockSpec((count, 1) + out.shape[2:], lambda i: (0, i, 0, 0)),
        grid=(4,),
        flops=2 * tokens * model * out.shape[3],
        moved=bytes_of(second, cot, back, hidden, out),
    )(second, cot, back, hidden)


def mix_grads_kernel(first, back, spread, out, flat):
    @pl.when(pl.program_id(0) == 0)
    def _():
        flat[...] = dot(back[...], spread[...], NT).astype(LOW)

    out[0] = dot(first[...], flat[...], TN).astype(LOW)


def mix_grads(first, back, spread):
    tokens, model = first.shape
    width = model // 4
    out = shape((4, width, spread.shape[0]))
    return call(
        mix_grads_kernel,
        out,
        [pl.BlockSpec((tokens, width), lambda i: (0, i)), whole(back), whole(spread)],
        pl.BlockSpec((1,) + out.shape[1:], lambda i: (i, 0, 0)),
        grid=(4,),
        scratch=(pltpu.VMEM((tokens, spread.shape[0]), LOW),),
        flops=2 * tokens * model * out.shape[2],
        moved=bytes_of(first, back, out),
    )(first, back, spread)


def feed_place_kernel(row_ref, piece, gain, gate, up, down):
    units, share = gate.shape[1], piece.shape[2]
    for k in range(piece.shape[0]):
        rows = slice(k * share, (k + 1) * share)
        gate[rows, :] = piece[k, 0, :, :units].astype(F32) * gain[rows, :]
        up[rows, :] = piece[k, 0, :, units : 2 * units].astype(F32) * gain[rows, :]
    down[...] = jnp.concatenate(
        [piece[k, 0, :, 2 * units :].astype(F32) for k in range(piece.shape[0])], axis=0
    ).T


def feed_place(row, pieces, gain):
    count, _, share, triple = pieces.shape
    units, depth = triple // 3, count * share
    outs = (shape((depth, 4 * units), F32), shape((depth, 4 * units), F32), shape((4 * units, depth), F32))
    return call(
        feed_place_kernel,
        outs,
        [
            pl.BlockSpec((count, 1, share, triple), lambda j, s: (0, jnp.bitwise_xor(s[0], j), 0, 0)),
            whole(gain),
        ],
        (
            pl.BlockSpec((depth, units), lambda j, s: (0, j)),
            pl.BlockSpec((depth, units), lambda j, s: (0, j)),
            pl.BlockSpec((units, depth), lambda j, s: (j, 0)),
        ),
        grid=(4,),
        prefetch=1,
        moved=bytes_of(pieces, *outs),
    )(row, pieces, gain)


def mix_place_kernel(row_ref, pieces, heads, gain, query, key, value, output):
    row = row_ref[0]
    wide, narrow = query.shape[1] // 4, key.shape[1] // 4
    for j in range(4):
        piece = pieces[jnp.bitwise_xor(row, j)].astype(F32) * gain[...]
        query[:, j * wide : (j + 1) * wide] = piece[:, :wide]
        key[:, j * narrow : (j + 1) * narrow] = piece[:, wide : wide + narrow]
        value[:, j * narrow : (j + 1) * narrow] = piece[:, wide + narrow :]
        output[j * wide : (j + 1) * wide, :] = heads[jnp.bitwise_xor(row, j)].astype(F32)


def mix_place(row, pieces, heads, gain):
    _, depth, width = pieces.shape
    wide, narrow = width // 2, width // 4
    outs = (
        shape((depth, 4 * wide), F32),
        shape((depth, 4 * narrow), F32),
        shape((depth, 4 * narrow), F32),
        shape((4 * wide, depth), F32),
    )
    return call(
        mix_place_kernel,
        outs,
        [whole(pieces), whole(heads), whole(gain)],
        tuple(whole(o) for o in outs),
        grid=(1,),
        prefetch=1,
        moved=bytes_of(pieces, heads, *outs),
    )(row, pieces, heads, gain)


def sequence_starts(lengths, tokens):
    places = jnp.arange(tokens, dtype=jnp.int32)
    starts = jnp.zeros((tokens,), jnp.int32)
    end = jnp.zeros((), jnp.int32)
    for k in range(lengths.shape[0]):
        end = end + lengths[k]
        starts = jnp.where(places >= end, end, starts)
    return places, starts


def tables(places):
    lane = jnp.arange(LANES, dtype=jnp.int32)
    entry = lane % (LANES // 2)
    frequency = THETA ** (-2.0 * entry.astype(F32) / HEAD)
    real = entry < SIDE
    angles = places.astype(F32)[:, None] * frequency[None, :]
    cosine = jnp.where(real[None, :], jnp.cos(angles), 0.0)
    sign = jnp.where(lane < LANES // 2, -1.0, 1.0)
    sine = jnp.where(real[None, :], jnp.sin(angles) * sign[None, :], 0.0)
    return cosine, sine


def spread_matrix():
    source = jnp.arange(4 * HEAD, dtype=jnp.int32)
    head, entry = source // HEAD, source % HEAD
    inside = jnp.where((head < 3) & (entry >= SIDE), entry - SIDE + LANES // 2, entry)
    target = head * LANES + inside
    return (target[:, None] == jnp.arange(4 * LANES, dtype=jnp.int32)[None, :]).astype(LOW)


def on_device(
    layer_input,
    first_gain,
    query_weight,
    key_projection_weight,
    value_projection_weight,
    output_weight,
    second_gain,
    gate_weight,
    up_weight,
    down_weight,
    sequence_lengths,
    cotangent,
):
    row = lax.axis_index("row")
    core = lax.axis_index("col")
    place = lax.axis_index("dp")
    blocks = lax.axis_size("dp")
    row_info = row.reshape(1).astype(jnp.int32)
    half, width = layer_input.shape
    tokens, model = 2 * half, 4 * width
    units = gate_weight.shape[1] // 4
    rows = output_weight.shape[0]
    chunk = rows // 4
    relative = [jnp.bitwise_xor(row, i) for i in range(4)]
    live = Live()
    live.x, live.cot = layer_input, cotangent

    live.xs = gather_one(live.x)
    gains = [gain[:, None] for gain in (first_gain, second_gain)]
    packed = pack(row_info, gains[0], query_weight, key_projection_weight, value_projection_weight)
    mixer = [packed[i] for i in range(4)]
    halves, weights = ready(
        fetch_halves(mixer, place, blocks), (gate_weight, up_weight, down_weight, output_weight, gains[1])
    )
    live.mixer_one = fetch_one(halves)
    live.mixer_own, live.lengths = mixer[0], sequence_lengths[0]
    gate, up, down, out, gain = weights
    downs = [lax.dynamic_slice_in_dim(down, relative[i] * units, units, 0) for i in range(4)]
    out_down = [jnp.concatenate([out, downs[i]], axis=0) for i in range(4)]
    scaled = lambda weight, i: (
        lax.dynamic_slice_in_dim(weight, relative[i] * units, units, 1).astype(F32) * gain
    ).astype(LOW)
    gate_up = [jnp.concatenate([scaled(gate, i), scaled(up, i)], axis=1) for i in range(4)]
    live.od_own, live.od_halves = out_down[0], fetch_halves(out_down, place, blocks)
    live.gu_own, live.gu_halves = gate_up[0], fetch_halves(gate_up, place, blocks)
    live.sync()

    halves, mine = ready(gather_halves(live.xs), jnp.stack(live.mixer_one))
    live.xs = gather_two(live.xs, halves)
    live.mixer = (live.mixer_own, mine, fetch_two(mine, blocks))
    places, starts = sequence_starts(live.lengths, tokens)
    live.cos, live.sin = tables(places - starts)
    live.start = starts[None, :]
    last_starts = (starts[TILE - 1 :: TILE] + TILE - 1) // TILE
    live.info = jnp.concatenate([core.reshape(1), starts[::TILE] // TILE, last_starts]).astype(jnp.int32)
    spread = spread_matrix()
    del live.mixer_one, live.mixer_own, live.lengths
    live.sync()

    live.gu_one = fetch_one(live.gu_halves)
    live.w_own = dot(fetched(*live.mixer, place).reshape(model, 4 * HEAD), spread).astype(LOW)
    live.w_oth = other(live.w_own)
    cos_own = lax.dynamic_slice_in_dim(live.cos, core * half, half, 0)
    sin_own = lax.dynamic_slice_in_dim(live.sin, core * half, half, 0)
    live.first, live.r1, live.qkv, live.send = project(
        live.xs, live.w_own, live.w_oth, cos_own, sin_own
    )
    del live.mixer, live.gu_halves
    live.sync()
    halves, send, live.gu_mine = ready(live.od_halves, live.send, jnp.stack(live.gu_one))
    live.gu_theirs = fetch_two(live.gu_mine, blocks)
    live.od_one = fetch_one(halves)
    live.qkv_got = other(send)
    live.keep, live.send, live.attended, live.lse = attend(live.info, live.qkv, live.qkv_got, live.start)
    del live.gu_one, live.od_halves
    live.sync()
    live.heads = jnp.concatenate([live.keep, other(live.send)], axis=1)
    live.od_mine = jnp.stack(live.od_one)
    del live.keep, live.send, live.od_one
    live.sync()

    live.od_theirs = fetch_two(live.od_mine, blocks)
    live.heads = gather_one(live.heads)
    live.cots = gather_one(live.cot)
    live.gu_own = fetched(live.gu_own, live.gu_mine, live.gu_theirs, place).reshape(model, 2 * units)
    del live.gu_mine, live.gu_theirs
    live.sync()

    halves, more = ready(gather_halves(live.heads), gather_halves(live.cots))
    live.heads = gather_two(live.heads, halves)
    live.cots = gather_two(live.cots, more)
    live.od_own = fetched(live.od_own, live.od_mine, live.od_theirs, place)
    od_oth = other(live.od_own)
    live.out_full, live.out_mine = order(row_info, live.od_own[:, :rows], od_oth[:, :rows])
    live.d_own, live.d_oth = live.od_own[:, rows:], od_oth[:, rows:]
    del live.od_own, live.od_mine, live.od_theirs
    live.sync()
    live.gu_oth = other(live.gu_own)
    live.cot_all = join(live.cots)
    del live.cots

    live.second, live.middle, live.r2, live.heads_all = middle_of(live.heads, live.xs, live.out_full)
    del live.heads, live.xs, live.out_full
    live.hid_own, live.hid_oth, live.back_own, live.back_oth = feed(
        live.second, live.cot_all, live.gu_own, live.gu_oth, live.d_own, live.d_oth
    )
    live.sg, live.sums = partial_sums(False, live.back_own, live.back_oth, live.gu_own, live.gu_oth, live.second)
    del live.gu_own, live.gu_oth
    live.sync()

    def added(own, got):
        return (own.astype(F32) + got.astype(F32)).astype(LOW)

    live.sg = scatter_one(live.sg)
    live.sums = (live.sums, swap(live.sums, 1))
    live.feed_oth = feed_grads(live.second, live.cot_all, live.back_oth, live.hid_oth, blocks)
    live.feed_own = feed_grads(live.second, live.cot_all, live.back_own, live.hid_own, blocks)
    del live.back_own, live.back_oth, live.second, live.cot_all
    live.sync()

    halves, sums, feed_oth = ready(scatter_halves(live.sg), live.sums[0] + live.sums[1], live.feed_oth)
    live.sg = scatter_two(live.sg, halves)
    live.sums = (sums, swap(sums, 2))
    live.feed_got = other(feed_oth)
    del live.feed_oth
    live.sync()

    second_grad = scattered(live.sg)
    inner = (live.sums[0] + live.sums[1]).reshape(half)
    r2 = live.r2[:, :1]
    live.middle_grad = (
        live.cot.astype(F32)
        + r2 * second_grad
        - live.middle * (r2 * r2 * inner[:, None] / model)
    )
    live.branch = live.middle_grad.astype(LOW)
    live.branches = gather_one(*ready(live.branch))
    feed_sum = lax.psum_scatter(added(live.feed_own, live.feed_got), "dp", scatter_dimension=0)
    live.fo, _ = partial_sums(True, live.hid_own, live.hid_oth, live.d_own, live.d_oth)
    del live.feed_own, live.feed_got, live.hid_own, live.hid_oth, live.d_own, live.d_oth
    live.gain_part = jnp.sum(second_grad * live.middle * r2, axis=0) / second_gain
    del live.sg, live.sums, live.cot, live.r2
    live.sync()

    live.branches = gather_two(live.branches, ready(*gather_halves(live.branches)))
    live.o_all = dot(live.heads_all, live.branch, TN).astype(LOW).reshape(4, 2, chunk, width)
    del live.heads_all, live.branch
    live.sync()
    live.grad, live.send = heads_grad_of(live.branches, live.out_mine)
    live.grad_got = other(live.send)
    live.o = added(live.o_all[:, 0], other(live.o_all[:, 1]))
    del live.branches, live.out_mine, live.send, live.o_all
    live.sync()

    o_rows, mix_rows, share = (chunk,), (width,), width // blocks
    parts = ready(*chain_parts(1, live.o, o_rows, blocks, []))
    live.o_moving = chain_sum(1, parts, blocks, [])
    live.fo = scatter_one(live.fo)
    live.bk, live.send = attend_back(
        live.info, live.qkv, live.qkv_got, live.grad, live.grad_got,
        live.attended, live.lse, live.start, live.cos, live.sin,
    )
    del live.qkv, live.qkv_got, live.grad, live.grad_got, live.attended, live.lse, live.start, live.info
    live.sync()

    halves, send, parts = ready(
        scatter_halves(live.fo), live.send, chain_parts(2, live.o, o_rows, blocks, live.o_moving)
    )
    live.o_moving = chain_sum(2, parts, blocks, live.o_moving)
    live.fo = scatter_two(live.fo, halves)
    live.bg = other(send)
    live.mix_oth = mix_grads(live.first, live.bg, spread)
    live.mix_own = mix_grads(live.first, live.bk, spread)
    del live.send
    live.sync()
    live.feed_sum = spread_row(feed_sum)
    live.mix = added(live.mix_own, other(live.mix_oth))
    live.moving = chain_sum(1, chain_parts(1, live.mix, mix_rows, blocks, []), blocks, [])
    del live.mix_own, live.mix_oth
    live.sync()
    parts, more, (bk, bg) = ready(
        chain_parts(2, live.mix, mix_rows, blocks, live.moving),
        chain_parts(3, live.o, o_rows, blocks, live.o_moving),
        (live.bk, live.bg),
    )
    live.moving = chain_sum(2, parts, blocks, live.moving)
    live.o_moving = chain_sum(3, more, blocks, live.o_moving)
    feeds = lax.all_gather(live.feed_sum, "dp", axis=0)
    live.fg, live.sums = partial_sums(False, bk, bg, live.w_own, live.w_oth, live.first)
    del live.bk, live.bg, live.w_own, live.w_oth, live.first
    live.sync()

    live.o_moving = chain_sums(4, live.o, o_rows, blocks, live.o_moving)
    live.o = chain_summed(live.o, o_rows, blocks, live.o_moving)
    del live.o_moving
    parts = ready(*chain_parts(3, live.mix, mix_rows, blocks, live.moving))
    live.moving = chain_sum(3, parts, blocks, live.moving)
    live.fg = scatter_one(live.fg)
    live.sums = (live.sums, swap(live.sums, 1))
    layer_output = (live.middle + scattered(live.fo)).astype(LOW)
    del live.fo, live.middle, live.feed_sum
    live.sync()

    live.moving = chain_sums(4, live.mix, mix_rows, blocks, live.moving)
    halves, sums, shard = ready(
        scatter_halves(live.fg),
        live.sums[0] + live.sums[1],
        chain_summed(live.mix, mix_rows, blocks, live.moving),
    )
    live.fg = scatter_two(live.fg, halves)
    live.sums = (sums, swap(sums, 2))
    live.mix = spread_row(shard)
    del live.moving
    live.sync()

    first_grad = scattered(live.fg)
    inner = (live.sums[0] + live.sums[1]).reshape(half)
    r1 = live.r1[:, :1]
    inputs = live.x.astype(F32)
    input_gradient = (
        live.middle_grad
        + r1 * first_grad
        - inputs * (r1 * r1 * inner[:, None] / model)
    )
    gains = jnp.stack([jnp.sum(first_grad * inputs * r1, axis=0) / first_gain, live.gain_part])
    carried = split_low(gains + other(gains))[None]
    carried = jnp.concatenate([carried, jnp.zeros((3,) + carried.shape[1:], LOW)], axis=0)
    live.mix = jnp.concatenate([live.mix, live.o, carried], axis=1)
    del live.fg, live.sums, live.r1, live.x, live.middle_grad, live.gain_part, live.o
    live.sync()
    live.moving = chain_spread(1, 2, live.mix, blocks, [])
    live.sync()
    live.moving = chain_spread(2, 3, live.mix, blocks, live.moving)
    placed = feed_place(row_info, feeds, second_gain[:, None])
    live.placed = placed
    live.sync()
    moving = chain_spread(3, blocks, live.mix, blocks, live.moving)
    mixes = chain_joined(live.mix, blocks, moving)
    gate_total, up_total, down_total = live.placed
    last = share + chunk // blocks
    query_total, key_total, value_total, output_total = mix_place(
        row_info,
        mixes[:, :, :share].reshape(4, width, width),
        mixes[:, :, share:last].reshape(4, chunk, width),
        first_gain[:, None],
    )
    gain_total = sum(unsplit(mixes[0, k, last:], 2) for k in range(blocks))
    return (
        layer_output,
        input_gradient,
        query_total,
        key_total,
        value_total,
        output_total,
        gate_total,
        up_total,
        down_total,
        gain_total[0],
        gain_total[1],
    )


def solution(mesh):
    return jax.shard_map(
        on_device,
        mesh=mesh,
        in_specs=(
            P(("dp", "col"), "row"),
            P("row"),
            P("row", "col"),
            P("row", "col"),
            P("row", "col"),
            P("col", "row"),
            P("row"),
            P("row", "col"),
            P("row", "col"),
            P("col", "row"),
            P("dp", None),
            P(("dp", "col"), "row"),
        ),
        out_specs=(
            P(("dp", "col"), "row"),
            P(("dp", "col"), "row"),
            P("row", "col"),
            P("row", "col"),
            P("row", "col"),
            P("col", "row"),
            P("row", "col"),
            P("row", "col"),
            P("col", "row"),
            P("row"),
            P("row"),
        ),
        check_vma=False,
    )
```

```python
import functools

import jax
import jax.numpy as jnp
from jax import lax
from jax.experimental import pallas as pl
from jax.experimental.pallas import tpu as pltpu
from jax.sharding import PartitionSpec as P

HEAD = 96
LANES = 128
SIDE = 48
TILE = 256
EPSILON = 1e-05
THETA = 100000.0
LOG2E = 1.4426950408889634
FACTOR = HEAD**-0.5
LOW = jnp.bfloat16
F32 = jnp.float32
NN = (((1,), (0,)), ((), ()))
NT = (((1,), (1,)), ((), ()))
TN = (((0,), (0,)), ((), ()))
VMEM_LIMIT = 48 * 1024 * 1024
WEIGHT = 1 / 64


def dot(left, right, dims=NN):
    return lax.dot_general(left, right, dims, preferred_element_type=F32)


def swap(value, step):
    return lax.ppermute(value, "row", [(i, i ^ step) for i in range(4)])


def other(value):
    return lax.ppermute(value, "col", [(0, 1), (1, 0)])


def pair(value, count):
    return lax.ppermute(value, "dp", [(i, i ^ 1) for i in range(count)])


def spread_row(shard):
    return jnp.stack([shard[0]] + [swap(shard[i], i) for i in (1, 2, 3)])


class Live:
    def sync(self):
        self.__dict__.update(lax.optimization_barrier(dict(self.__dict__)))


def ready(*values):
    return lax.optimization_barrier(values)


def gather_one(value):
    return [value, swap(value, 1), swap(value, 2)]


def gather_halves(found):
    half = found[0].shape[0] // 2
    return found[1][:half], found[2][half:]


def gather_two(found, halves):
    return found + [swap(halves[0], 2), swap(halves[1], 1)]


def fetch_halves(pieces, place, count):
    parts = 2 if count % 2 == 0 else 1
    rows = pieces[0].shape[0] // parts
    at = (place % parts) * rows
    return [lax.dynamic_slice_in_dim(pieces[i], at, rows, 0) for i in (1, 2, 3)]


def fetch_one(halves):
    return [swap(half, i) for i, half in enumerate(halves, 1)]


def fetch_two(mine, count):
    return pair(mine, count) if count % 2 == 0 else ()


def fetched(own, mine, theirs, place):
    if isinstance(theirs, tuple):
        return jnp.concatenate([own[None], mine])
    rows = mine.shape[1]
    bit = place % 2
    zero = jnp.zeros((), jnp.int32)
    result = jnp.zeros((4,) + own.shape, own.dtype)
    result = lax.dynamic_update_slice(result, own[None], (0, 0, 0))
    result = lax.dynamic_update_slice(result, mine, (zero + 1, bit * rows, zero))
    return lax.dynamic_update_slice(result, theirs, (zero + 1, (1 - bit) * rows, zero))


def scatter_one(parts):
    own, far_a, near_a, far_b, near_b = parts
    return own, swap(far_a, 1), near_a, swap(far_b, 2), near_b


def scatter_halves(parts):
    own, got_a, near_a, got_b, near_b = parts
    width = own.shape[1]
    send_a = (near_a.astype(F32) + got_a[:, width:].astype(F32)).astype(LOW)
    send_b = (near_b.astype(F32) + got_b[:, width:].astype(F32)).astype(LOW)
    return send_a, send_b


def scatter_two(parts, halves):
    own, got_a, _, got_b, _ = parts
    return own, got_a, swap(halves[0], 2), got_b, swap(halves[1], 1)


def scattered(parts):
    own, got_a, last_a, got_b, last_b = parts
    width, half = own.shape[1], got_a.shape[0]
    upper = own[:half].astype(F32) + got_a[:, :width].astype(F32) + last_a.astype(F32)
    lower = own[half:].astype(F32) + got_b[:, :width].astype(F32) + last_b.astype(F32)
    return jnp.concatenate([upper, lower], axis=0)


def shard_of(total, rows, number, count):
    found, at = [], 0
    for part in rows:
        size = part // count
        found.append(lax.dynamic_slice_in_dim(total, at + number * size, size, 1))
        at = at + part
    return found[0] if len(found) == 1 else jnp.concatenate(found, axis=1)


def turn(value, step, count):
    return lax.ppermute(value, "dp", [(i, (i + step) % count) for i in range(count)])


def chain_up(count, first, last):
    return [(i, i + 1) for i in range(first, last)]


def chain_down(count, first, last):
    return [(count - 1 - i, count - 2 - i) for i in range(first, last)]


def chain_parts(step, total, rows, count, before):
    if step >= count:
        return ()
    place = lax.axis_index("dp")
    up = shard_of(total, rows, jnp.clip(count - step + place, 0, count - 1), count)
    down = shard_of(total, rows, jnp.clip(place - (count - step), 0, count - 1), count)
    if before:
        up = (up.astype(F32) + before[0].astype(F32)).astype(LOW)
        down = (down.astype(F32) + before[1].astype(F32)).astype(LOW)
    return up, down


def chain_sum(step, parts, count, before):
    if step >= count:
        return before
    last = min(step, count - 1)
    up, down = parts
    if step == 1 and count > 3:
        place = lax.axis_index("dp")
        sent = jnp.where(place == 0, up, down)
        got = lax.ppermute(sent, "dp", chain_up(count, 0, 1) + chain_down(count, 0, 1))
        return [jnp.where(place == 1, got, 0), jnp.where(place == count - 2, got, 0)]
    return [lax.ppermute(up, "dp", chain_up(count, 0, last)), lax.ppermute(down, "dp", chain_down(count, 0, last))]


def chain_sums(first, total, rows, count, before):
    for step in range(first, count):
        before = chain_sum(step, chain_parts(step, total, rows, count, before), count, before)
    return before


def chain_summed(total, rows, count, before):
    own = shard_of(total, rows, lax.axis_index("dp"), count)
    if before:
        own = (own.astype(F32) + before[0].astype(F32) + before[1].astype(F32)).astype(LOW)
    return own


def chain_spread(first, last, shard, count, found):
    for step in range(first, min(last, count)):
        up, down = found[-1] if found else (shard, shard)
        if step == count - 1 and count > 3:
            place = lax.axis_index("dp")
            sent = jnp.where(place == count - 2, up, down)
            got = lax.ppermute(
                sent, "dp", chain_up(count, count - 2, count - 1) + chain_down(count, count - 2, count - 1)
            )
            found = found + [(got, got)]
            continue
        up = lax.ppermute(up, "dp", chain_up(count, step - 1, count - 1))
        down = lax.ppermute(down, "dp", chain_down(count, step - 1, count - 1))
        found = found + [(up, down)]
    return found


def chain_joined(shard, count, found):
    place = lax.axis_index("dp")
    dims = (shard.shape[0], count) + shard.shape[1:]
    zero = jnp.zeros((), jnp.int32)
    result = jnp.zeros(dims, shard.dtype)

    def put(result, piece, at):
        return lax.dynamic_update_slice(result, piece[:, None], (zero, at) + (zero,) * (len(dims) - 2))

    for step, (up, down) in enumerate(found, 1):
        result = put(result, up, jnp.where(place - step >= 0, place - step, place))
        result = put(result, down, jnp.where(place + step < count, place + step, place))
    return put(result, shard, place)


def call(kernel, out_shape, in_specs, out_specs, grid=(), scratch=(), prefetch=0, flops=0, moved=0):
    return pl.pallas_call(
        kernel,
        out_shape=out_shape,
        grid_spec=pltpu.PrefetchScalarGridSpec(
            num_scalar_prefetch=prefetch,
            grid=grid,
            in_specs=in_specs,
            out_specs=out_specs,
            scratch_shapes=list(scratch),
        ),
        compiler_params=pltpu.CompilerParams(vmem_limit_bytes=VMEM_LIMIT),
        cost_estimate=pl.CostEstimate(
            flops=int(flops * WEIGHT), bytes_accessed=int(moved * WEIGHT), transcendentals=0
        ),
    )


def shape(dims, kind=LOW):
    return jax.ShapeDtypeStruct(tuple(dims), kind)


def whole(array):
    rank = len(array.shape)
    return pl.BlockSpec(tuple(array.shape), lambda *_: (0,) * rank)


def bytes_of(*arrays):
    return sum(int(a.size) * a.dtype.itemsize for a in arrays)


def read_pieces(refs, upper):
    x0, x1, x2, top, bottom = refs
    return jnp.concatenate([x0[...], x1[...], x2[...], jnp.where(upper, top[...], bottom[...])], axis=1)


def piece_specs(width, tile, blocks, shift=0):
    halfway = blocks // 2
    plain = pl.BlockSpec((tile, width), lambda b, *_: (b + shift, 0))
    top = pl.BlockSpec((tile, width), lambda b, *_: (jnp.minimum(b + shift, halfway - 1), 0))
    bottom = pl.BlockSpec((tile, width), lambda b, *_: (jnp.maximum(b + shift - halfway, 0), 0))
    return [plain, plain, plain, top, bottom]


def join_kernel(x0, x1, x2, top, bottom, out):
    width, half = x0.shape[1], top.shape[0]
    for i, ref in enumerate((x0, x1, x2)):
        out[:, i * width : (i + 1) * width] = ref[...]
    out[:half, 3 * width :] = top[...]
    out[half:, 3 * width :] = bottom[...]


def join(pieces):
    tokens, width = pieces[0].shape
    out = shape((tokens, 4 * width))
    return call(
        join_kernel, out, [whole(p) for p in pieces], whole(out), grid=(1,), moved=2 * bytes_of(out)
    )(*pieces)


def split_low(value):
    high = lax.reduce_precision(value, 8, 7)
    rest = value - high
    middle = lax.reduce_precision(rest, 8, 7)
    terms = [high, middle, rest - middle]
    spare = jnp.zeros((16 - 3 * value.shape[0], value.shape[1]), F32)
    return jnp.concatenate(terms + [spare], axis=0).astype(LOW)


def unsplit(rows, count):
    terms = [rows[i * count : (i + 1) * count].astype(F32) for i in range(3)]
    return terms[0] + terms[1] + terms[2]


def order_kernel(row_ref, own, oth, full, mine):
    row = row_ref[0]
    features, chunk = own.shape[2], own.shape[1] // 4
    for k in range(4):
        columns = slice(k * features, (k + 1) * features)
        for i in range(4):
            rows = pl.ds(pl.multiple_of(jnp.bitwise_xor(row, i) * chunk, chunk), chunk)
            for s, weight in enumerate((own, oth)):
                at = (2 * i + s) * chunk
                full[at : at + chunk, columns] = weight[k, rows, :]
    mine[...] = jnp.zeros(mine.shape, mine.dtype)
    for h in range(2 * chunk // HEAD):
        mine[h * LANES : h * LANES + HEAD, :] = full[h * HEAD : (h + 1) * HEAD, :]


def order(row, own, oth):
    _, rows, features = own.shape
    full, mine = shape((2 * rows, 4 * features)), shape((2 * rows // 4 // HEAD * LANES, 4 * features))
    return call(
        order_kernel,
        (full, mine),
        [whole(own), whole(oth)],
        (whole(full), whole(mine)),
        grid=(1,),
        prefetch=1,
        moved=2 * bytes_of(full) + bytes_of(mine),
    )(row, own, oth)


def heads_grad_kernel(x0, x1, x2, top, bottom, weight, own, oth):
    upper = pl.program_id(0) < pl.num_programs(0) // 2
    grad = dot(read_pieces((x0, x1, x2, top, bottom), upper), weight[...], NT).astype(LOW)
    own[...] = grad[:, : own.shape[1]]
    oth[...] = grad[:, own.shape[1] :]


def heads_grad_of(pieces, weight):
    tokens, width = pieces[0].shape
    columns = weight.shape[0] // 2
    outs = (shape((tokens, columns)), shape((tokens, columns)))
    rows = pl.BlockSpec((TILE, columns), lambda b: (b, 0))
    return call(
        heads_grad_kernel,
        outs,
        piece_specs(width, TILE, tokens // TILE) + [whole(weight)],
        (rows, rows),
        grid=(tokens // TILE,),
        flops=2 * tokens * 4 * width * weight.shape[0],
        moved=bytes_of(*pieces, weight, *outs),
    )(*pieces, weight)


def pack_kernel(row_ref, gain_ref, q_ref, k_ref, v_ref, out_ref):
    row = row_ref[0]
    gain = gain_ref[...]
    query, key = q_ref.shape[1] // 4, k_ref.shape[1] // 4
    scaled = lambda ref, size, j: (ref[:, j * size : (j + 1) * size].astype(F32) * gain).astype(LOW)
    for j in range(4):
        at = jnp.bitwise_xor(row, j)
        out_ref[at, :, :query] = scaled(q_ref, query, j)
        out_ref[at, :, query : query + key] = scaled(k_ref, key, j)
        out_ref[at, :, query + key :] = scaled(v_ref, key, j)


def pack(row, gain, query_weight, key_weight, value_weight):
    depth = query_weight.shape[0]
    width = (query_weight.shape[1] + 2 * key_weight.shape[1]) // 4
    out = shape((4, depth, width))
    arrays = (gain, query_weight, key_weight, value_weight)
    return call(
        pack_kernel,
        out,
        [whole(a) for a in arrays],
        whole(out),
        grid=(1,),
        prefetch=1,
        moved=2 * bytes_of(out),
    )(row, *arrays)


def project_kernel(x0, x1, x2, top, bottom, w_own, w_oth, cos, sin, first, r1, own, oth):
    upper = pl.program_id(0) < pl.num_programs(0) // 2
    x = read_pieces((x0, x1, x2, top, bottom), upper).astype(F32)
    inverse = lax.rsqrt(jnp.mean(x * x, axis=1, keepdims=True) + EPSILON)
    normed = (x * inverse).astype(LOW)
    first[...] = normed
    r1[...] = jnp.broadcast_to(inverse, r1.shape)
    for weight, out in ((w_own, own), (w_oth, oth)):
        heads = dot(normed, weight[...])
        for h in range(3):
            part = heads[:, h * LANES : (h + 1) * LANES]
            turned = part * cos[...] + pltpu.roll(part, LANES // 2, 1) * sin[...]
            out[:, h * LANES : (h + 1) * LANES] = turned.astype(LOW)
        out[:, 3 * LANES :] = heads[:, 3 * LANES :].astype(LOW)


def project(xs, w_own, w_oth, cos, sin):
    tokens, width = xs[0].shape
    rows = lambda n: pl.BlockSpec((TILE, n), lambda b: (b, 0))
    outs = (shape((tokens, 4 * width)), shape((tokens, LANES), F32), shape((tokens, 512)), shape((tokens, 512)))
    return call(
        project_kernel,
        outs,
        piece_specs(width, TILE, tokens // TILE)
        + [whole(w_own), whole(w_oth), rows(LANES), rows(LANES)],
        tuple(rows(o.shape[1]) for o in outs),
        grid=(tokens // TILE,),
        flops=2 * tokens * 4 * width * 1024,
        moved=bytes_of(*xs, w_own, w_oth, *outs),
    )(*xs, w_own, w_oth, cos, sin)


def stack_heads(ref, rows):
    return jnp.concatenate([ref[rows, :LANES], ref[rows, LANES : 2 * LANES]], axis=0)


def block_limits(start_ref, block):
    rows = pl.ds(pl.multiple_of(block * TILE, TILE), TILE)
    start = start_ref[:, rows]
    query = block * TILE + lax.broadcasted_iota(jnp.int32, (1, TILE), 1)
    return jnp.concatenate([start, start], axis=1), jnp.concatenate([query, query], axis=1)


def allowed_keys(number, start, query):
    key = number * TILE + lax.broadcasted_iota(jnp.int32, (TILE, 2 * TILE), 0)
    return (key >= start) & (key <= query)


def over_keys(info, block, step):
    count = (info.shape[0] - 1) // 2
    first, whole_from = info[1 + block], jnp.minimum(info[1 + count + block], block)

    def masked(number, carry):
        step(number, True)
        return carry

    def plain(number, carry):
        step(number, False)
        return carry

    lax.fori_loop(first, whole_from, masked, 0)
    def both(pair, carry):
        step(whole_from + 2 * pair, False)
        step(whole_from + 2 * pair + 1, False)
        return carry

    pairs = (block - whole_from) // 2
    lax.fori_loop(0, pairs, both, 0)
    lax.fori_loop(whole_from + 2 * pairs, block, plain, 0)
    step(block, True)


def attend_kernel(info, own, oth, start_ref, keep, send, out, lse, full, values, top, total, acc):
    block = pl.program_id(0)
    core = info[0]
    half = own.shape[0]

    @pl.when(block == 0)
    def _():
        full[pl.ds(pl.multiple_of(core * half, half), half), :] = own[...]
        full[pl.ds(pl.multiple_of((1 - core) * half, half), half), :] = oth[...]
        values[...] = full[:, 3 * LANES :].T

    rows = pl.ds(pl.multiple_of(block * TILE, TILE), TILE)
    query = stack_heads(full, rows)
    start, place = block_limits(start_ref, block)
    top[...] = jnp.full(top.shape, -1e30, F32)
    total[...] = jnp.zeros(total.shape, F32)
    acc[...] = jnp.zeros(acc.shape, F32)

    def step(number, masked):
        keys = pl.ds(pl.multiple_of(number * TILE, TILE), TILE)
        scores = dot(full[keys, 2 * LANES : 3 * LANES], query, NT) * (FACTOR * LOG2E)
        if masked:
            scores = jnp.where(allowed_keys(number, start, place), scores, -1e30)
        before = top[...]
        now = jnp.maximum(before, jnp.max(scores, axis=0, keepdims=True))
        weight = jnp.exp2(scores - now)
        scale = jnp.exp2(before - now)
        top[...] = now
        total[...] = total[...] * scale + jnp.sum(weight, axis=0, keepdims=True)
        acc[...] = acc[...] * scale + dot(values[:, keys], weight.astype(LOW))

    over_keys(info, block, step)
    lse[...] = top[...] + jnp.log2(total[...])
    result = (acc[...] / total[...]).T.astype(LOW)
    out[:, :LANES] = result[:TILE]
    out[:, LANES:] = result[TILE:]
    mine = (block // (half // TILE)) == core
    for target, wanted in ((keep, mine), (send, jnp.logical_not(mine))):

        @pl.when(wanted)
        def _(target=target):
            target[:, :HEAD] = result[:TILE, :HEAD]
            target[:, HEAD:] = result[TILE:, :HEAD]


def attend(info, own, oth, start):
    half = own.shape[0]
    tokens = 2 * half
    per_half = half // TILE
    outs = (
        shape((half, 2 * HEAD)),
        shape((half, 2 * HEAD)),
        shape((tokens, 2 * LANES)),
        shape((1, 2 * tokens), F32),
    )
    return call(
        attend_kernel,
        outs,
        [whole(own), whole(oth), whole(start)],
        (
            pl.BlockSpec((TILE, 2 * HEAD), lambda b, s: (jnp.clip(b - s[0] * per_half, 0, per_half - 1), 0)),
            pl.BlockSpec((TILE, 2 * HEAD), lambda b, s: (jnp.clip(b - (1 - s[0]) * per_half, 0, per_half - 1), 0)),
            pl.BlockSpec((TILE, 2 * LANES), lambda b, s: (b, 0)),
            pl.BlockSpec((1, 2 * TILE), lambda b, s: (0, b)),
        ),
        grid=(tokens // TILE,),
        scratch=(
            pltpu.VMEM((tokens, 4 * LANES), LOW),
            pltpu.VMEM((LANES, tokens), LOW),
            pltpu.VMEM((1, 2 * TILE), F32),
            pltpu.VMEM((1, 2 * TILE), F32),
            pltpu.VMEM((LANES, 2 * TILE), F32),
        ),
        prefetch=1,
        flops=4 * tokens * tokens * LANES * 2,
        moved=bytes_of(own, oth, *outs),
    )(info, own, oth, start)


def turn_back(part, cos, sin):
    return part * cos - pltpu.roll(part, LANES // 2, 1) * sin


def attend_back_kernel(
    info, own, oth, g_own, g_oth, out, lse, start_ref, cos, sin,
    keep, send, full, grads, keys_t, d_keys, d_values, d_query, result,
):
    block = pl.program_id(0)
    core = info[0]
    half = own.shape[0]

    @pl.when(block == 0)
    def _():
        mine = pl.ds(pl.multiple_of(core * half, half), half)
        theirs = pl.ds(pl.multiple_of((1 - core) * half, half), half)
        full[mine, :] = own[...]
        full[theirs, :] = oth[...]
        grads[mine, :] = g_own[...]
        grads[theirs, :] = g_oth[...]
        keys_t[...] = full[:, 2 * LANES : 3 * LANES].T
        d_keys[...] = jnp.zeros(d_keys.shape, F32)
        d_values[...] = jnp.zeros(d_values.shape, F32)

    rows = pl.ds(pl.multiple_of(block * TILE, TILE), TILE)
    query = stack_heads(full, rows)
    grad = stack_heads(grads, rows)
    reply = stack_heads(out, slice(None))
    start, place = block_limits(start_ref, block)
    level = lse[...]
    delta = jnp.sum((grad.astype(F32) * reply.astype(F32)).T, axis=0, keepdims=True)
    d_query[...] = jnp.zeros(d_query.shape, F32)

    def step(number, masked):
        keys = pl.ds(pl.multiple_of(number * TILE, TILE), TILE)
        scores = dot(full[keys, 2 * LANES : 3 * LANES], query, NT) * (FACTOR * LOG2E)
        if masked:
            scores = jnp.where(allowed_keys(number, start, place), scores, -1e30)
        weight = jnp.exp2(scores - level)
        pressure = dot(full[keys, 3 * LANES :], grad, NT)
        slope = (weight * (pressure - delta) * FACTOR).astype(LOW)
        d_values[keys, :] += dot(weight.astype(LOW), grad)
        d_keys[keys, :] += dot(slope, query)
        d_query[...] += dot(keys_t[:, keys], slope)

    over_keys(info, block, step)
    turned = d_query[...].T
    for h in range(2):
        part = turned[h * TILE : (h + 1) * TILE]
        result[rows, h * LANES : (h + 1) * LANES] = turn_back(part, cos[rows, :], sin[rows, :]).astype(LOW)

    @pl.when(block == pl.num_programs(0) - 1)
    def _():
        mine = pl.ds(pl.multiple_of(core * half, half), half)
        theirs = pl.ds(pl.multiple_of((1 - core) * half, half), half)
        for target, which in ((keep, mine), (send, theirs)):
            target[:, : 2 * LANES] = result[which, :]
            target[:, 2 * LANES : 3 * LANES] = turn_back(
                d_keys[which, :], cos[which, :], sin[which, :]
            ).astype(LOW)
            target[:, 3 * LANES :] = d_values[which, :].astype(LOW)


def attend_back(info, own, oth, g_own, g_oth, out, lse, start, cos, sin):
    half = own.shape[0]
    tokens = 2 * half
    outs = (shape((half, 4 * LANES)), shape((half, 4 * LANES)))
    return call(
        attend_back_kernel,
        outs,
        [
            whole(own),
            whole(oth),
            whole(g_own),
            whole(g_oth),
            pl.BlockSpec((TILE, 2 * LANES), lambda b, s: (b, 0)),
            pl.BlockSpec((1, 2 * TILE), lambda b, s: (0, b)),
            whole(start),
            whole(cos),
            whole(sin),
        ],
        tuple(whole(o) for o in outs),
        grid=(tokens // TILE,),
        scratch=(
            pltpu.VMEM((tokens, 4 * LANES), LOW),
            pltpu.VMEM((tokens, 2 * LANES), LOW),
            pltpu.VMEM((LANES, tokens), LOW),
            pltpu.VMEM((tokens, LANES), F32),
            pltpu.VMEM((tokens, LANES), F32),
            pltpu.VMEM((LANES, 2 * TILE), F32),
            pltpu.VMEM((tokens, 2 * LANES), LOW),
        ),
        prefetch=1,
        flops=10 * tokens * tokens * LANES * 2,
        moved=bytes_of(own, oth, g_own, g_oth, out, *outs),
    )(info, own, oth, g_own, g_oth, out, lse, start, cos, sin)


def middle_kernel(*refs):
    weight, second, middle, r2, joined = refs[10:]
    upper = pl.program_id(0) < pl.num_programs(0) // 2
    heads = read_pieces(refs[:5], upper)
    joined[...] = heads
    x = read_pieces(refs[5:10], upper).astype(F32)
    value = x + dot(heads, weight[...])
    inverse = lax.rsqrt(jnp.mean(value * value, axis=1, keepdims=True) + EPSILON)
    second[...] = (value * inverse).astype(LOW)
    middle[...] = value[:, : middle.shape[1]]
    r2[...] = jnp.broadcast_to(inverse, r2.shape)


def middle_of(heads, xs, weight):
    tokens, width = xs[0].shape
    rows = lambda n: pl.BlockSpec((TILE, n), lambda b: (b, 0))
    outs = (
        shape((tokens, 4 * width)),
        shape((tokens, width), F32),
        shape((tokens, LANES), F32),
        shape((tokens, 4 * width)),
    )
    return call(
        middle_kernel,
        outs,
        piece_specs(width, TILE, tokens // TILE) * 2 + [whole(weight)],
        tuple(rows(o.shape[1]) for o in outs),
        grid=(tokens // TILE,),
        flops=2 * tokens * 16 * width * width,
        moved=bytes_of(*heads, *xs, weight, *outs),
    )(*heads, *xs, weight)


def feed_kernel(second, cot, g_own, u_own, g_oth, u_oth, d_own, d_oth, hidden_own, hidden_oth, back_own, back_oth):
    block = pl.program_id(0)
    per = pl.num_programs(0) // 2
    tokens, units = hidden_own.shape
    width = d_own.shape[2]

    def body(gate_w, up_w, down_w, hidden, back, at):
        down = jnp.concatenate([down_w[i] for i in range(4)], axis=1)
        near = pl.ds(pl.multiple_of(at, TILE), TILE)
        far = pl.ds(pl.multiple_of(units + at, TILE), TILE)
        for m in range(0, tokens, TILE):
            rows = slice(m, m + TILE)
            gate = dot(second[rows, :], gate_w[...])
            up = dot(second[rows, :], up_w[...])
            hidden_grad = dot(cot[rows, :], down, NT)
            share = 1.0 / (1.0 + jnp.exp(-gate))
            silu = gate * share
            hidden[rows, near] = (silu * up).astype(LOW)
            back[rows, near] = (hidden_grad * up * share * (1.0 + gate * (1.0 - share))).astype(LOW)
            back[rows, far] = (hidden_grad * silu).astype(LOW)

    @pl.when(block < per)
    def _():
        body(g_own, u_own, d_own, hidden_own, back_own, block * TILE)

    @pl.when(block >= per)
    def _():
        body(g_oth, u_oth, d_oth, hidden_oth, back_oth, (block - per) * TILE)


def feed(second, cot, gu_own, gu_oth, d_own, d_oth):
    tokens, model = second.shape
    units = gu_own.shape[1] // 2
    per = units // TILE
    early = lambda b: jnp.minimum(b, per - 1)
    late = lambda b: jnp.maximum(b - per, 0)
    column = lambda at: pl.BlockSpec((model, TILE), lambda b: (0, at(b)))
    down = lambda at: pl.BlockSpec((4, TILE, model // 4), lambda b: (0, at(b), 0))
    outs = (shape((tokens, units)), shape((tokens, units)), shape((tokens, 2 * units)), shape((tokens, 2 * units)))
    return call(
        feed_kernel,
        outs,
        [
            whole(second),
            whole(cot),
            column(early),
            column(lambda b: per + early(b)),
            column(late),
            column(lambda b: per + late(b)),
            down(early),
            down(late),
        ],
        tuple(whole(o) for o in outs),
        grid=(2 * per,),
        flops=12 * tokens * model * units,
        moved=bytes_of(second, cot, gu_own, gu_oth, d_own, d_oth, *outs),
    )(second, cot, gu_own, gu_own, gu_oth, gu_oth, d_own, d_oth)


def partial_kernel(blocked, a_own, a_oth, w_own, w_oth, *rest):
    upper = pl.program_id(0) < pl.num_programs(0) // 2
    if len(rest) == 7:
        against, own, far_a, near_a, far_b, near_b, sums = rest
    else:
        own, far_a, near_a, far_b, near_b = rest
    width = own.shape[1]
    total = 0.0
    left, right = a_own[...], a_oth[...]
    found = []
    if blocked:
        for k in range(4):
            found.append((dot(left, w_own[k]) + dot(right, w_oth[k])).astype(LOW))
    else:
        value = dot(left, w_own[...], NT) + dot(right, w_oth[...], NT)
        total = jnp.sum(value * against[...].astype(F32), axis=1, keepdims=True)
        low = value.astype(LOW)
        found = [low[:, k * width : (k + 1) * width] for k in range(4)]
    own[...] = found[0]
    if len(rest) == 7:
        sums[...] = jnp.broadcast_to(total, sums.shape)

    @pl.when(upper)
    def _():
        far_a[:, :width] = found[1]
        far_a[:, width:] = found[3]
        near_a[...] = found[2]

    @pl.when(jnp.logical_not(upper))
    def _():
        far_b[:, :width] = found[2]
        far_b[:, width:] = found[3]
        near_b[...] = found[1]


def partial_sums(blocked, a_own, a_oth, w_own, w_oth, against=None):
    tokens, depth = a_own.shape
    model = 4 * w_own.shape[2] if blocked else w_own.shape[0]
    half, width = tokens // 2, model // 4
    blocks = tokens // TILE
    plain = lambda n: pl.BlockSpec((TILE, n), lambda b: (b, 0))
    early = lambda n: pl.BlockSpec((TILE, n), lambda b: (jnp.minimum(b, blocks // 2 - 1), 0))
    late = lambda n: pl.BlockSpec((TILE, n), lambda b: (jnp.maximum(b - blocks // 2, 0), 0))
    outs = [shape((tokens, width))] + [shape((half, 2 * width)), shape((half, width))] * 2
    writes = [plain(width), early(2 * width), early(width), late(2 * width), late(width)]
    args = [a_own, a_oth, w_own, w_oth]
    specs = [plain(depth), plain(depth), whole(w_own), whole(w_oth)]
    if against is not None:
        outs.append(shape((tokens, LANES), F32))
        writes.append(plain(LANES))
        args.append(against)
        specs.append(plain(model))
    found = call(
        functools.partial(partial_kernel, blocked),
        tuple(outs),
        specs,
        tuple(writes),
        grid=(blocks,),
        flops=4 * tokens * depth * model,
        moved=bytes_of(*args, *outs),
    )(*args)
    return found[:5], None if against is None else found[5][:, 0].reshape(8, tokens // 8)


def feed_grads_kernel(second, cot, back, hidden, out):
    double, share = back.shape[1], out.shape[2]
    for columns, left, right in ((slice(0, double), second, back), (slice(double, None), cot, hidden)):
        value = dot(left[...], right[...], TN).astype(LOW)
        for k in range(out.shape[0]):
            out[k, 0, :, columns] = value[k * share : (k + 1) * share]


def feed_grads(second, cot, back, hidden, count):
    tokens, model = second.shape
    width = model // 4
    out = shape((count, 4, width // count, back.shape[1] + hidden.shape[1]))
    block = pl.BlockSpec((tokens, width), lambda i: (0, i))
    return call(
        feed_grads_kernel,
        out,
        [block, block, whole(back), whole(hidden)],
        pl.BlockSpec((count, 1) + out.shape[2:], lambda i: (0, i, 0, 0)),
        grid=(4,),
        flops=2 * tokens * model * out.shape[3],
        moved=bytes_of(second, cot, back, hidden, out),
    )(second, cot, back, hidden)


def mix_grads_kernel(first, back, spread, out, flat):
    @pl.when(pl.program_id(0) == 0)
    def _():
        flat[...] = dot(back[...], spread[...], NT).astype(LOW)

    out[0] = dot(first[...], flat[...], TN).astype(LOW)


def mix_grads(first, back, spread):
    tokens, model = first.shape
    width = model // 4
    out = shape((4, width, spread.shape[0]))
    return call(
        mix_grads_kernel,
        out,
        [pl.BlockSpec((tokens, width), lambda i: (0, i)), whole(back), whole(spread)],
        pl.BlockSpec((1,) + out.shape[1:], lambda i: (i, 0, 0)),
        grid=(4,),
        scratch=(pltpu.VMEM((tokens, spread.shape[0]), LOW),),
        flops=2 * tokens * model * out.shape[2],
        moved=bytes_of(first, back, out),
    )(first, back, spread)


def feed_place_kernel(row_ref, piece, gain, gate, up, down):
    units, share = gate.shape[1], piece.shape[2]
    for k in range(piece.shape[0]):
        rows = slice(k * share, (k + 1) * share)
        gate[rows, :] = piece[k, 0, :, :units].astype(F32) * gain[rows, :]
        up[rows, :] = piece[k, 0, :, units : 2 * units].astype(F32) * gain[rows, :]
    down[...] = jnp.concatenate(
        [piece[k, 0, :, 2 * units :].astype(F32) for k in range(piece.shape[0])], axis=0
    ).T


def feed_place(row, pieces, gain):
    count, _, share, triple = pieces.shape
    units, depth = triple // 3, count * share
    outs = (shape((depth, 4 * units), F32), shape((depth, 4 * units), F32), shape((4 * units, depth), F32))
    return call(
        feed_place_kernel,
        outs,
        [
            pl.BlockSpec((count, 1, share, triple), lambda j, s: (0, jnp.bitwise_xor(s[0], j), 0, 0)),
            whole(gain),
        ],
        (
            pl.BlockSpec((depth, units), lambda j, s: (0, j)),
            pl.BlockSpec((depth, units), lambda j, s: (0, j)),
            pl.BlockSpec((units, depth), lambda j, s: (j, 0)),
        ),
        grid=(4,),
        prefetch=1,
        moved=bytes_of(pieces, *outs),
    )(row, pieces, gain)


def mix_place_kernel(row_ref, pieces, heads, gain, query, key, value, output):
    row = row_ref[0]
    wide, narrow = query.shape[1] // 4, key.shape[1] // 4
    for j in range(4):
        piece = pieces[jnp.bitwise_xor(row, j)].astype(F32) * gain[...]
        query[:, j * wide : (j + 1) * wide] = piece[:, :wide]
        key[:, j * narrow : (j + 1) * narrow] = piece[:, wide : wide + narrow]
        value[:, j * narrow : (j + 1) * narrow] = piece[:, wide + narrow :]
        output[j * wide : (j + 1) * wide, :] = heads[jnp.bitwise_xor(row, j)].astype(F32)


def mix_place(row, pieces, heads, gain):
    _, depth, width = pieces.shape
    wide, narrow = width // 2, width // 4
    outs = (
        shape((depth, 4 * wide), F32),
        shape((depth, 4 * narrow), F32),
        shape((depth, 4 * narrow), F32),
        shape((4 * wide, depth), F32),
    )
    return call(
        mix_place_kernel,
        outs,
        [whole(pieces), whole(heads), whole(gain)],
        tuple(whole(o) for o in outs),
        grid=(1,),
        prefetch=1,
        moved=bytes_of(pieces, heads, *outs),
    )(row, pieces, heads, gain)


def sequence_starts(lengths, tokens):
    places = jnp.arange(tokens, dtype=jnp.int32)
    starts = jnp.zeros((tokens,), jnp.int32)
    end = jnp.zeros((), jnp.int32)
    for k in range(lengths.shape[0]):
        end = end + lengths[k]
        starts = jnp.where(places >= end, end, starts)
    return places, starts


def tables(places):
    lane = jnp.arange(LANES, dtype=jnp.int32)
    entry = lane % (LANES // 2)
    frequency = THETA ** (-2.0 * entry.astype(F32) / HEAD)
    real = entry < SIDE
    angles = places.astype(F32)[:, None] * frequency[None, :]
    cosine = jnp.where(real[None, :], jnp.cos(angles), 0.0)
    sign = jnp.where(lane < LANES // 2, -1.0, 1.0)
    sine = jnp.where(real[None, :], jnp.sin(angles) * sign[None, :], 0.0)
    return cosine, sine


def spread_matrix():
    source = jnp.arange(4 * HEAD, dtype=jnp.int32)
    head, entry = source // HEAD, source % HEAD
    inside = jnp.where((head < 3) & (entry >= SIDE), entry - SIDE + LANES // 2, entry)
    target = head * LANES + inside
    return (target[:, None] == jnp.arange(4 * LANES, dtype=jnp.int32)[None, :]).astype(LOW)


def on_device(
    layer_input,
    first_gain,
    query_weight,
    key_projection_weight,
    value_projection_weight,
    output_weight,
    second_gain,
    gate_weight,
    up_weight,
    down_weight,
    sequence_lengths,
    cotangent,
):
    row = lax.axis_index("row")
    core = lax.axis_index("col")
    place = lax.axis_index("dp")
    blocks = lax.axis_size("dp")
    row_info = row.reshape(1).astype(jnp.int32)
    half, width = layer_input.shape
    tokens, model = 2 * half, 4 * width
    units = gate_weight.shape[1] // 4
    rows = output_weight.shape[0]
    chunk = rows // 4
    relative = [jnp.bitwise_xor(row, i) for i in range(4)]
    live = Live()
    live.x, live.cot = layer_input, cotangent

    live.xs = gather_one(live.x)
    gains = [gain[:, None] for gain in (first_gain, second_gain)]
    packed = pack(row_info, gains[0], query_weight, key_projection_weight, value_projection_weight)
    mixer = [packed[i] for i in range(4)]
    halves, weights = ready(
        fetch_halves(mixer, place, blocks), (gate_weight, up_weight, down_weight, output_weight, gains[1])
    )
    live.mixer_one = fetch_one(halves)
    live.mixer_own, live.lengths = mixer[0], sequence_lengths[0]
    gate, up, down, out, gain = weights
    downs = [lax.dynamic_slice_in_dim(down, relative[i] * units, units, 0) for i in range(4)]
    out_down = [jnp.concatenate([out, downs[i]], axis=0) for i in range(4)]
    scaled = lambda weight, i: (
        lax.dynamic_slice_in_dim(weight, relative[i] * units, units, 1).astype(F32) * gain
    ).astype(LOW)
    gate_up = [jnp.concatenate([scaled(gate, i), scaled(up, i)], axis=1) for i in range(4)]
    live.od_own, live.od_halves = out_down[0], fetch_halves(out_down, place, blocks)
    live.gu_own, live.gu_halves = gate_up[0], fetch_halves(gate_up, place, blocks)
    live.sync()

    halves, mine = ready(gather_halves(live.xs), jnp.stack(live.mixer_one))
    live.xs = gather_two(live.xs, halves)
    live.mixer = (live.mixer_own, mine, fetch_two(mine, blocks))
    places, starts = sequence_starts(live.lengths, tokens)
    live.cos, live.sin = tables(places - starts)
    live.start = starts[None, :]
    last_starts = (starts[TILE - 1 :: TILE] + TILE - 1) // TILE
    live.info = jnp.concatenate([core.reshape(1), starts[::TILE] // TILE, last_starts]).astype(jnp.int32)
    spread = spread_matrix()
    del live.mixer_one, live.mixer_own, live.lengths
    live.sync()

    live.gu_one = fetch_one(live.gu_halves)
    live.w_own = dot(fetched(*live.mixer, place).reshape(model, 4 * HEAD), spread).astype(LOW)
    live.w_oth = other(live.w_own)
    cos_own = lax.dynamic_slice_in_dim(live.cos, core * half, half, 0)
    sin_own = lax.dynamic_slice_in_dim(live.sin, core * half, half, 0)
    live.first, live.r1, live.qkv, live.send = project(
        live.xs, live.w_own, live.w_oth, cos_own, sin_own
    )
    del live.mixer, live.gu_halves
    live.sync()
    halves, send, live.gu_mine = ready(live.od_halves, live.send, jnp.stack(live.gu_one))
    live.gu_theirs = fetch_two(live.gu_mine, blocks)
    live.od_one = fetch_one(halves)
    live.qkv_got = other(send)
    live.keep, live.send, live.attended, live.lse = attend(live.info, live.qkv, live.qkv_got, live.start)
    del live.gu_one, live.od_halves
    live.sync()
    live.heads = jnp.concatenate([live.keep, other(live.send)], axis=1)
    live.od_mine = jnp.stack(live.od_one)
    del live.keep, live.send, live.od_one
    live.sync()

    live.od_theirs = fetch_two(live.od_mine, blocks)
    live.heads = gather_one(live.heads)
    live.cots = gather_one(live.cot)
    live.gu_own = fetched(live.gu_own, live.gu_mine, live.gu_theirs, place).reshape(model, 2 * units)
    del live.gu_mine, live.gu_theirs
    live.sync()

    halves, more = ready(gather_halves(live.heads), gather_halves(live.cots))
    live.heads = gather_two(live.heads, halves)
    live.cots = gather_two(live.cots, more)
    live.od_own = fetched(live.od_own, live.od_mine, live.od_theirs, place)
    od_oth = other(live.od_own)
    live.out_full, live.out_mine = order(row_info, live.od_own[:, :rows], od_oth[:, :rows])
    live.d_own, live.d_oth = live.od_own[:, rows:], od_oth[:, rows:]
    del live.od_own, live.od_mine, live.od_theirs
    live.sync()
    live.gu_oth = other(live.gu_own)
    live.cot_all = join(live.cots)
    del live.cots

    live.second, live.middle, live.r2, live.heads_all = middle_of(live.heads, live.xs, live.out_full)
    del live.heads, live.xs, live.out_full
    live.hid_own, live.hid_oth, live.back_own, live.back_oth = feed(
        live.second, live.cot_all, live.gu_own, live.gu_oth, live.d_own, live.d_oth
    )
    live.sg, live.sums = partial_sums(False, live.back_own, live.back_oth, live.gu_own, live.gu_oth, live.second)
    del live.gu_own, live.gu_oth
    live.sync()

    def added(own, got):
        return (own.astype(F32) + got.astype(F32)).astype(LOW)

    live.sg = scatter_one(live.sg)
    live.sums = (live.sums, swap(live.sums, 1))
    live.feed_oth = feed_grads(live.second, live.cot_all, live.back_oth, live.hid_oth, blocks)
    live.feed_own = feed_grads(live.second, live.cot_all, live.back_own, live.hid_own, blocks)
    del live.back_own, live.back_oth, live.second, live.cot_all
    live.sync()

    halves, sums, feed_oth = ready(scatter_halves(live.sg), live.sums[0] + live.sums[1], live.feed_oth)
    live.sg = scatter_two(live.sg, halves)
    live.sums = (sums, swap(sums, 2))
    live.feed_got = other(feed_oth)
    del live.feed_oth
    live.sync()

    second_grad = scattered(live.sg)
    inner = (live.sums[0] + live.sums[1]).reshape(half)
    r2 = live.r2[:, :1]
    live.middle_grad = (
        live.cot.astype(F32)
        + r2 * second_grad
        - live.middle * (r2 * r2 * inner[:, None] / model)
    )
    live.branch = live.middle_grad.astype(LOW)
    live.branches = gather_one(*ready(live.branch))
    feed_sum = lax.psum_scatter(added(live.feed_own, live.feed_got), "dp", scatter_dimension=0)
    live.fo, _ = partial_sums(True, live.hid_own, live.hid_oth, live.d_own, live.d_oth)
    del live.feed_own, live.feed_got, live.hid_own, live.hid_oth, live.d_own, live.d_oth
    live.gain_part = jnp.sum(second_grad * live.middle * r2, axis=0) / second_gain
    del live.sg, live.sums, live.cot, live.r2
    live.sync()

    live.branches = gather_two(live.branches, ready(*gather_halves(live.branches)))
    live.o_all = dot(live.heads_all, live.branch, TN).astype(LOW).reshape(4, 2, chunk, width)
    del live.heads_all, live.branch
    live.sync()
    live.grad, live.send = heads_grad_of(live.branches, live.out_mine)
    live.grad_got = other(live.send)
    live.o = added(live.o_all[:, 0], other(live.o_all[:, 1]))
    del live.branches, live.out_mine, live.send, live.o_all
    live.sync()

    o_rows, mix_rows, share = (chunk,), (width,), width // blocks
    parts = ready(*chain_parts(1, live.o, o_rows, blocks, []))
    live.o_moving = chain_sum(1, parts, blocks, [])
    live.fo = scatter_one(live.fo)
    live.bk, live.send = attend_back(
        live.info, live.qkv, live.qkv_got, live.grad, live.grad_got,
        live.attended, live.lse, live.start, live.cos, live.sin,
    )
    del live.qkv, live.qkv_got, live.grad, live.grad_got, live.attended, live.lse, live.start, live.info
    live.sync()

    halves, send, parts = ready(
        scatter_halves(live.fo), live.send, chain_parts(2, live.o, o_rows, blocks, live.o_moving)
    )
    live.o_moving = chain_sum(2, parts, blocks, live.o_moving)
    live.fo = scatter_two(live.fo, halves)
    live.bg = other(send)
    live.mix_oth = mix_grads(live.first, live.bg, spread)
    live.mix_own = mix_grads(live.first, live.bk, spread)
    del live.send
    live.sync()
    live.feed_sum = spread_row(feed_sum)
    live.mix = added(live.mix_own, other(live.mix_oth))
    live.moving = chain_sum(1, chain_parts(1, live.mix, mix_rows, blocks, []), blocks, [])
    del live.mix_own, live.mix_oth
    live.sync()
    parts, more, (bk, bg) = ready(
        chain_parts(2, live.mix, mix_rows, blocks, live.moving),
        chain_parts(3, live.o, o_rows, blocks, live.o_moving),
        (live.bk, live.bg),
    )
    live.moving = chain_sum(2, parts, blocks, live.moving)
    live.o_moving = chain_sum(3, more, blocks, live.o_moving)
    feeds = lax.all_gather(live.feed_sum, "dp", axis=0)
    live.fg, live.sums = partial_sums(False, bk, bg, live.w_own, live.w_oth, live.first)
    del live.bk, live.bg, live.w_own, live.w_oth, live.first
    live.sync()

    live.o_moving = chain_sums(4, live.o, o_rows, blocks, live.o_moving)
    live.o = chain_summed(live.o, o_rows, blocks, live.o_moving)
    del live.o_moving
    parts = ready(*chain_parts(3, live.mix, mix_rows, blocks, live.moving))
    live.moving = chain_sum(3, parts, blocks, live.moving)
    live.fg = scatter_one(live.fg)
    live.sums = (live.sums, swap(live.sums, 1))
    layer_output = (live.middle + scattered(live.fo)).astype(LOW)
    del live.fo, live.middle, live.feed_sum
    live.sync()

    live.moving = chain_sums(4, live.mix, mix_rows, blocks, live.moving)
    halves, sums, shard = ready(
        scatter_halves(live.fg),
        live.sums[0] + live.sums[1],
        chain_summed(live.mix, mix_rows, blocks, live.moving),
    )
    live.fg = scatter_two(live.fg, halves)
    live.sums = (sums, swap(sums, 2))
    live.mix = spread_row(shard)
    del live.moving
    live.sync()

    first_grad = scattered(live.fg)
    inner = (live.sums[0] + live.sums[1]).reshape(half)
    r1 = live.r1[:, :1]
    inputs = live.x.astype(F32)
    input_gradient = (
        live.middle_grad
        + r1 * first_grad
        - inputs * (r1 * r1 * inner[:, None] / model)
    )
    gains = jnp.stack([jnp.sum(first_grad * inputs * r1, axis=0) / first_gain, live.gain_part])
    carried = split_low(gains + other(gains))[None]
    carried = jnp.concatenate([carried, jnp.zeros((3,) + carried.shape[1:], LOW)], axis=0)
    live.mix = jnp.concatenate([live.mix, live.o, carried], axis=1)
    del live.fg, live.sums, live.r1, live.x, live.middle_grad, live.gain_part, live.o
    live.sync()
    live.moving = chain_spread(1, 2, live.mix, blocks, [])
    live.sync()
    live.moving = chain_spread(2, 3, live.mix, blocks, live.moving)
    placed = feed_place(row_info, feeds, second_gain[:, None])
    live.placed = placed
    live.sync()
    moving = chain_spread(3, blocks, live.mix, blocks, live.moving)
    mixes = chain_joined(live.mix, blocks, moving)
    gate_total, up_total, down_total = live.placed
    last = share + chunk // blocks
    query_total, key_total, value_total, output_total = mix_place(
        row_info,
        mixes[:, :, :share].reshape(4, width, width),
        mixes[:, :, share:last].reshape(4, chunk, width),
        first_gain[:, None],
    )
    gain_total = sum(unsplit(mixes[0, k, last:], 2) for k in range(blocks))
    return (
        layer_output,
        input_gradient,
        query_total,
        key_total,
        value_total,
        output_total,
        gate_total,
        up_total,
        down_total,
        gain_total[0],
        gain_total[1],
    )


def solution(mesh):
    return jax.shard_map(
        on_device,
        mesh=mesh,
        in_specs=(
            P(("dp", "col"), "row"),
            P("row"),
            P("row", "col"),
            P("row", "col"),
            P("row", "col"),
            P("col", "row"),
            P("row"),
            P("row", "col"),
            P("row", "col"),
            P("col", "row"),
            P("dp", None),
            P(("dp", "col"), "row"),
        ),
        out_specs=(
            P(("dp", "col"), "row"),
            P(("dp", "col"), "row"),
            P("row", "col"),
            P("row", "col"),
            P("row", "col"),
            P("col", "row"),
            P("row", "col"),
            P("row", "col"),
            P("col", "row"),
            P("row"),
            P("row"),
        ),
        check_vma=False,
    )
```

```python
import functools

import jax
import jax.numpy as jnp
from jax import lax
from jax.experimental import pallas as pl
from jax.experimental.pallas import tpu as pltpu
from jax.sharding import PartitionSpec as P

HEAD = 96
LANES = 128
SIDE = 48
TILE = 256
EPSILON = 1e-05
THETA = 100000.0
LOG2E = 1.4426950408889634
FACTOR = HEAD**-0.5
LOW = jnp.bfloat16
F32 = jnp.float32
NN = (((1,), (0,)), ((), ()))
NT = (((1,), (1,)), ((), ()))
TN = (((0,), (0,)), ((), ()))
VMEM_LIMIT = 48 * 1024 * 1024
WEIGHT = 1 / 64


def dot(left, right, dims=NN):
    return lax.dot_general(left, right, dims, preferred_element_type=F32)


def swap(value, step):
    return lax.ppermute(value, "row", [(i, i ^ step) for i in range(4)])


def other(value):
    return lax.ppermute(value, "col", [(0, 1), (1, 0)])


def pair(value, count):
    return lax.ppermute(value, "dp", [(i, i ^ 1) for i in range(count)])


def spread_row(shard):
    return jnp.stack([shard[0]] + [swap(shard[i], i) for i in (1, 2, 3)])


class Live:
    def sync(self):
        self.__dict__.update(lax.optimization_barrier(dict(self.__dict__)))


def ready(*values):
    return lax.optimization_barrier(values)


def gather_one(value):
    return [value, swap(value, 1), swap(value, 2)]


def gather_halves(found):
    half = found[0].shape[0] // 2
    return found[1][:half], found[2][half:]


def gather_two(found, halves):
    return found + [swap(halves[0], 2), swap(halves[1], 1)]


def fetch_halves(pieces, place, count):
    parts = 2 if count % 2 == 0 else 1
    rows = pieces[0].shape[0] // parts
    at = (place % parts) * rows
    return [lax.dynamic_slice_in_dim(pieces[i], at, rows, 0) for i in (1, 2, 3)]


def fetch_one(halves):
    return [swap(half, i) for i, half in enumerate(halves, 1)]


def fetch_two(mine, count):
    return pair(mine, count) if count % 2 == 0 else ()


def fetched(own, mine, theirs, place):
    if isinstance(theirs, tuple):
        return jnp.concatenate([own[None], mine])
    rows = mine.shape[1]
    bit = place % 2
    zero = jnp.zeros((), jnp.int32)
    result = jnp.zeros((4,) + own.shape, own.dtype)
    result = lax.dynamic_update_slice(result, own[None], (0, 0, 0))
    result = lax.dynamic_update_slice(result, mine, (zero + 1, bit * rows, zero))
    return lax.dynamic_update_slice(result, theirs, (zero + 1, (1 - bit) * rows, zero))


def scatter_one(parts):
    own, far_a, near_a, far_b, near_b = parts
    return own, swap(far_a, 1), near_a, swap(far_b, 2), near_b


def scatter_halves(parts):
    own, got_a, near_a, got_b, near_b = parts
    width = own.shape[1]
    send_a = (near_a.astype(F32) + got_a[:, width:].astype(F32)).astype(LOW)
    send_b = (near_b.astype(F32) + got_b[:, width:].astype(F32)).astype(LOW)
    return send_a, send_b


def scatter_two(parts, halves):
    own, got_a, _, got_b, _ = parts
    return own, got_a, swap(halves[0], 2), got_b, swap(halves[1], 1)


def scattered(parts):
    own, got_a, last_a, got_b, last_b = parts
    width, half = own.shape[1], got_a.shape[0]
    upper = own[:half].astype(F32) + got_a[:, :width].astype(F32) + last_a.astype(F32)
    lower = own[half:].astype(F32) + got_b[:, :width].astype(F32) + last_b.astype(F32)
    return jnp.concatenate([upper, lower], axis=0)


def shard_of(total, rows, number, count):
    found, at = [], 0
    for part in rows:
        size = part // count
        found.append(lax.dynamic_slice_in_dim(total, at + number * size, size, 1))
        at = at + part
    return found[0] if len(found) == 1 else jnp.concatenate(found, axis=1)


def turn(value, step, count):
    return lax.ppermute(value, "dp", [(i, (i + step) % count) for i in range(count)])


def chain_up(count, first, last):
    return [(i, i + 1) for i in range(first, last)]


def chain_down(count, first, last):
    return [(count - 1 - i, count - 2 - i) for i in range(first, last)]


def chain_parts(step, total, rows, count, before):
    if step >= count:
        return ()
    place = lax.axis_index("dp")
    up = shard_of(total, rows, jnp.clip(count - step + place, 0, count - 1), count)
    down = shard_of(total, rows, jnp.clip(place - (count - step), 0, count - 1), count)
    if before:
        up = (up.astype(F32) + before[0].astype(F32)).astype(LOW)
        down = (down.astype(F32) + before[1].astype(F32)).astype(LOW)
    return up, down


def chain_sum(step, parts, count, before):
    if step >= count:
        return before
    last = min(step, count - 1)
    up, down = parts
    if step == 1 and count > 3:
        place = lax.axis_index("dp")
        sent = jnp.where(place == 0, up, down)
        got = lax.ppermute(sent, "dp", chain_up(count, 0, 1) + chain_down(count, 0, 1))
        return [jnp.where(place == 1, got, 0), jnp.where(place == count - 2, got, 0)]
    return [lax.ppermute(up, "dp", chain_up(count, 0, last)), lax.ppermute(down, "dp", chain_down(count, 0, last))]


def chain_sums(first, total, rows, count, before):
    for step in range(first, count):
        before = chain_sum(step, chain_parts(step, total, rows, count, before), count, before)
    return before


def chain_summed(total, rows, count, before):
    own = shard_of(total, rows, lax.axis_index("dp"), count)
    if before:
        own = (own.astype(F32) + before[0].astype(F32) + before[1].astype(F32)).astype(LOW)
    return own


def chain_spread(first, last, shard, count, found):
    for step in range(first, min(last, count)):
        up, down = found[-1] if found else (shard, shard)
        if step == count - 1 and count > 3:
            place = lax.axis_index("dp")
            sent = jnp.where(place == count - 2, up, down)
            got = lax.ppermute(
                sent, "dp", chain_up(count, count - 2, count - 1) + chain_down(count, count - 2, count - 1)
            )
            found = found + [(got, got)]
            continue
        up = lax.ppermute(up, "dp", chain_up(count, step - 1, count - 1))
        down = lax.ppermute(down, "dp", chain_down(count, step - 1, count - 1))
        found = found + [(up, down)]
    return found


def chain_joined(shard, count, found):
    place = lax.axis_index("dp")
    dims = (shard.shape[0], count) + shard.shape[1:]
    zero = jnp.zeros((), jnp.int32)
    result = jnp.zeros(dims, shard.dtype)

    def put(result, piece, at):
        return lax.dynamic_update_slice(result, piece[:, None], (zero, at) + (zero,) * (len(dims) - 2))

    for step, (up, down) in enumerate(found, 1):
        result = put(result, up, jnp.where(place - step >= 0, place - step, place))
        result = put(result, down, jnp.where(place + step < count, place + step, place))
    return put(result, shard, place)


def call(kernel, out_shape, in_specs, out_specs, grid=(), scratch=(), prefetch=0, flops=0, moved=0):
    return pl.pallas_call(
        kernel,
        out_shape=out_shape,
        grid_spec=pltpu.PrefetchScalarGridSpec(
            num_scalar_prefetch=prefetch,
            grid=grid,
            in_specs=in_specs,
            out_specs=out_specs,
            scratch_shapes=list(scratch),
        ),
        compiler_params=pltpu.CompilerParams(vmem_limit_bytes=VMEM_LIMIT),
        cost_estimate=pl.CostEstimate(
            flops=int(flops * WEIGHT), bytes_accessed=int(moved * WEIGHT), transcendentals=0
        ),
    )


def shape(dims, kind=LOW):
    return jax.ShapeDtypeStruct(tuple(dims), kind)


def whole(array):
    rank = len(array.shape)
    return pl.BlockSpec(tuple(array.shape), lambda *_: (0,) * rank)


def bytes_of(*arrays):
    return sum(int(a.size) * a.dtype.itemsize for a in arrays)


def read_pieces(refs, upper):
    x0, x1, x2, top, bottom = refs
    return jnp.concatenate([x0[...], x1[...], x2[...], jnp.where(upper, top[...], bottom[...])], axis=1)


def piece_specs(width, tile, blocks, shift=0):
    halfway = blocks // 2
    plain = pl.BlockSpec((tile, width), lambda b, *_: (b + shift, 0))
    top = pl.BlockSpec((tile, width), lambda b, *_: (jnp.minimum(b + shift, halfway - 1), 0))
    bottom = pl.BlockSpec((tile, width), lambda b, *_: (jnp.maximum(b + shift - halfway, 0), 0))
    return [plain, plain, plain, top, bottom]


def join_kernel(x0, x1, x2, top, bottom, out):
    width, half = x0.shape[1], top.shape[0]
    for i, ref in enumerate((x0, x1, x2)):
        out[:, i * width : (i + 1) * width] = ref[...]
    out[:half, 3 * width :] = top[...]
    out[half:, 3 * width :] = bottom[...]


def join(pieces):
    tokens, width = pieces[0].shape
    out = shape((tokens, 4 * width))
    return call(
        join_kernel, out, [whole(p) for p in pieces], whole(out), grid=(1,), moved=2 * bytes_of(out)
    )(*pieces)


def split_low(value):
    high = lax.reduce_precision(value, 8, 7)
    rest = value - high
    middle = lax.reduce_precision(rest, 8, 7)
    terms = [high, middle, rest - middle]
    spare = jnp.zeros((16 - 3 * value.shape[0], value.shape[1]), F32)
    return jnp.concatenate(terms + [spare], axis=0).astype(LOW)


def unsplit(rows, count):
    terms = [rows[i * count : (i + 1) * count].astype(F32) for i in range(3)]
    return terms[0] + terms[1] + terms[2]


def order_kernel(row_ref, own, oth, full, mine):
    row = row_ref[0]
    features, chunk = own.shape[2], own.shape[1] // 4
    for k in range(4):
        columns = slice(k * features, (k + 1) * features)
        for i in range(4):
            rows = pl.ds(pl.multiple_of(jnp.bitwise_xor(row, i) * chunk, chunk), chunk)
            for s, weight in enumerate((own, oth)):
                at = (2 * i + s) * chunk
                full[at : at + chunk, columns] = weight[k, rows, :]
    mine[...] = jnp.zeros(mine.shape, mine.dtype)
    for h in range(2 * chunk // HEAD):
        mine[h * LANES : h * LANES + HEAD, :] = full[h * HEAD : (h + 1) * HEAD, :]


def order(row, own, oth):
    _, rows, features = own.shape
    full, mine = shape((2 * rows, 4 * features)), shape((2 * rows // 4 // HEAD * LANES, 4 * features))
    return call(
        order_kernel,
        (full, mine),
        [whole(own), whole(oth)],
        (whole(full), whole(mine)),
        grid=(1,),
        prefetch=1,
        moved=2 * bytes_of(full) + bytes_of(mine),
    )(row, own, oth)


def heads_grad_kernel(x0, x1, x2, top, bottom, weight, own, oth):
    upper = pl.program_id(0) < pl.num_programs(0) // 2
    grad = dot(read_pieces((x0, x1, x2, top, bottom), upper), weight[...], NT).astype(LOW)
    own[...] = grad[:, : own.shape[1]]
    oth[...] = grad[:, own.shape[1] :]


def heads_grad_of(pieces, weight):
    tokens, width = pieces[0].shape
    columns = weight.shape[0] // 2
    outs = (shape((tokens, columns)), shape((tokens, columns)))
    rows = pl.BlockSpec((TILE, columns), lambda b: (b, 0))
    return call(
        heads_grad_kernel,
        outs,
        piece_specs(width, TILE, tokens // TILE) + [whole(weight)],
        (rows, rows),
        grid=(tokens // TILE,),
        flops=2 * tokens * 4 * width * weight.shape[0],
        moved=bytes_of(*pieces, weight, *outs),
    )(*pieces, weight)


def pack_kernel(row_ref, gain_ref, q_ref, k_ref, v_ref, out_ref):
    row = row_ref[0]
    gain = gain_ref[...]
    query, key = q_ref.shape[1] // 4, k_ref.shape[1] // 4
    scaled = lambda ref, size, j: (ref[:, j * size : (j + 1) * size].astype(F32) * gain).astype(LOW)
    for j in range(4):
        at = jnp.bitwise_xor(row, j)
        out_ref[at, :, :query] = scaled(q_ref, query, j)
        out_ref[at, :, query : query + key] = scaled(k_ref, key, j)
        out_ref[at, :, query + key :] = scaled(v_ref, key, j)


def pack(row, gain, query_weight, key_weight, value_weight):
    depth = query_weight.shape[0]
    width = (query_weight.shape[1] + 2 * key_weight.shape[1]) // 4
    out = shape((4, depth, width))
    arrays = (gain, query_weight, key_weight, value_weight)
    return call(
        pack_kernel,
        out,
        [whole(a) for a in arrays],
        whole(out),
        grid=(1,),
        prefetch=1,
        moved=2 * bytes_of(out),
    )(row, *arrays)


def project_kernel(x0, x1, x2, top, bottom, w_own, w_oth, cos, sin, first, r1, own, oth):
    upper = pl.program_id(0) < pl.num_programs(0) // 2
    x = read_pieces((x0, x1, x2, top, bottom), upper).astype(F32)
    inverse = lax.rsqrt(jnp.mean(x * x, axis=1, keepdims=True) + EPSILON)
    normed = (x * inverse).astype(LOW)
    first[...] = normed
    r1[...] = jnp.broadcast_to(inverse, r1.shape)
    for weight, out in ((w_own, own), (w_oth, oth)):
        heads = dot(normed, weight[...])
        for h in range(3):
            part = heads[:, h * LANES : (h + 1) * LANES]
            turned = part * cos[...] + pltpu.roll(part, LANES // 2, 1) * sin[...]
            out[:, h * LANES : (h + 1) * LANES] = turned.astype(LOW)
        out[:, 3 * LANES :] = heads[:, 3 * LANES :].astype(LOW)


def project(xs, w_own, w_oth, cos, sin):
    tokens, width = xs[0].shape
    rows = lambda n: pl.BlockSpec((TILE, n), lambda b: (b, 0))
    outs = (shape((tokens, 4 * width)), shape((tokens, LANES), F32), shape((tokens, 512)), shape((tokens, 512)))
    return call(
        project_kernel,
        outs,
        piece_specs(width, TILE, tokens // TILE)
        + [whole(w_own), whole(w_oth), rows(LANES), rows(LANES)],
        tuple(rows(o.shape[1]) for o in outs),
        grid=(tokens // TILE,),
        flops=2 * tokens * 4 * width * 1024,
        moved=bytes_of(*xs, w_own, w_oth, *outs),
    )(*xs, w_own, w_oth, cos, sin)


def stack_heads(ref, rows):
    return jnp.concatenate([ref[rows, :LANES], ref[rows, LANES : 2 * LANES]], axis=0)


def block_limits(start_ref, block):
    rows = pl.ds(pl.multiple_of(block * TILE, TILE), TILE)
    start = start_ref[:, rows]
    query = block * TILE + lax.broadcasted_iota(jnp.int32, (1, TILE), 1)
    return jnp.concatenate([start, start], axis=1), jnp.concatenate([query, query], axis=1)


def allowed_keys(number, start, query):
    key = number * TILE + lax.broadcasted_iota(jnp.int32, (TILE, 2 * TILE), 0)
    return (key >= start) & (key <= query)


def over_keys(info, block, step):
    count = (info.shape[0] - 1) // 2
    first, whole_from = info[1 + block], jnp.minimum(info[1 + count + block], block)

    def masked(number, carry):
        step(number, True)
        return carry

    lax.fori_loop(first, whole_from, masked, 0)
    def both(pair, carry):
        step(whole_from + 2 * pair, False)
        step(whole_from + 2 * pair + 1, False)
        return carry

    pairs = (block - whole_from) // 2
    lax.fori_loop(0, pairs, both, 0)
    alone = (block - whole_from) % 2 == 1

    @pl.when(alone)
    def _():
        step(block - 1, False)
        step(block, True)

    @pl.when(jnp.logical_not(alone))
    def _():
        step(block, True)


def attend_kernel(info, own, oth, start_ref, keep, send, out, lse, full, values, top, total, acc):
    block = pl.program_id(0)
    core = info[0]
    half = own.shape[0]

    @pl.when(block == 0)
    def _():
        full[pl.ds(pl.multiple_of(core * half, half), half), :] = own[...]
        full[pl.ds(pl.multiple_of((1 - core) * half, half), half), :] = oth[...]
        values[...] = full[:, 3 * LANES :].T

    rows = pl.ds(pl.multiple_of(block * TILE, TILE), TILE)
    query = stack_heads(full, rows)
    start, place = block_limits(start_ref, block)
    top[...] = jnp.full(top.shape, -1e30, F32)
    total[...] = jnp.zeros(total.shape, F32)
    acc[...] = jnp.zeros(acc.shape, F32)

    def step(number, masked):
        keys = pl.ds(pl.multiple_of(number * TILE, TILE), TILE)
        scores = dot(full[keys, 2 * LANES : 3 * LANES], query, NT) * (FACTOR * LOG2E)
        if masked:
            scores = jnp.where(allowed_keys(number, start, place), scores, -1e30)
        before = top[...]
        now = jnp.maximum(before, jnp.max(scores, axis=0, keepdims=True))
        weight = jnp.exp2(scores - now)
        scale = jnp.exp2(before - now)
        top[...] = now
        total[...] = total[...] * scale + jnp.sum(weight, axis=0, keepdims=True)
        acc[...] = acc[...] * scale + dot(values[:, keys], weight.astype(LOW))

    over_keys(info, block, step)
    lse[...] = top[...] + jnp.log2(total[...])
    result = (acc[...] / total[...]).T.astype(LOW)
    out[:, :LANES] = result[:TILE]
    out[:, LANES:] = result[TILE:]
    mine = (block // (half // TILE)) == core
    for target, wanted in ((keep, mine), (send, jnp.logical_not(mine))):

        @pl.when(wanted)
        def _(target=target):
            target[:, :HEAD] = result[:TILE, :HEAD]
            target[:, HEAD:] = result[TILE:, :HEAD]


def attend(info, own, oth, start):
    half = own.shape[0]
    tokens = 2 * half
    per_half = half // TILE
    outs = (
        shape((half, 2 * HEAD)),
        shape((half, 2 * HEAD)),
        shape((tokens, 2 * LANES)),
        shape((1, 2 * tokens), F32),
    )
    return call(
        attend_kernel,
        outs,
        [whole(own), whole(oth), whole(start)],
        (
            pl.BlockSpec((TILE, 2 * HEAD), lambda b, s: (jnp.clip(b - s[0] * per_half, 0, per_half - 1), 0)),
            pl.BlockSpec((TILE, 2 * HEAD), lambda b, s: (jnp.clip(b - (1 - s[0]) * per_half, 0, per_half - 1), 0)),
            pl.BlockSpec((TILE, 2 * LANES), lambda b, s: (b, 0)),
            pl.BlockSpec((1, 2 * TILE), lambda b, s: (0, b)),
        ),
        grid=(tokens // TILE,),
        scratch=(
            pltpu.VMEM((tokens, 4 * LANES), LOW),
            pltpu.VMEM((LANES, tokens), LOW),
            pltpu.VMEM((1, 2 * TILE), F32),
            pltpu.VMEM((1, 2 * TILE), F32),
            pltpu.VMEM((LANES, 2 * TILE), F32),
        ),
        prefetch=1,
        flops=4 * tokens * tokens * LANES * 2,
        moved=bytes_of(own, oth, *outs),
    )(info, own, oth, start)


def turn_back(part, cos, sin):
    return part * cos - pltpu.roll(part, LANES // 2, 1) * sin


def attend_back_kernel(
    info, own, oth, g_own, g_oth, out, lse, start_ref, cos, sin,
    keep, send, full, grads, keys_t, d_keys, d_values, d_query, result,
):
    block = pl.program_id(0)
    core = info[0]
    half = own.shape[0]

    @pl.when(block == 0)
    def _():
        mine = pl.ds(pl.multiple_of(core * half, half), half)
        theirs = pl.ds(pl.multiple_of((1 - core) * half, half), half)
        full[mine, :] = own[...]
        full[theirs, :] = oth[...]
        grads[mine, :] = g_own[...]
        grads[theirs, :] = g_oth[...]
        keys_t[...] = full[:, 2 * LANES : 3 * LANES].T
        d_keys[...] = jnp.zeros(d_keys.shape, F32)
        d_values[...] = jnp.zeros(d_values.shape, F32)

    rows = pl.ds(pl.multiple_of(block * TILE, TILE), TILE)
    query = stack_heads(full, rows)
    grad = stack_heads(grads, rows)
    reply = stack_heads(out, slice(None))
    start, place = block_limits(start_ref, block)
    level = lse[...]
    delta = jnp.sum((grad.astype(F32) * reply.astype(F32)).T, axis=0, keepdims=True)
    d_query[...] = jnp.zeros(d_query.shape, F32)

    def step(number, masked):
        keys = pl.ds(pl.multiple_of(number * TILE, TILE), TILE)
        scores = dot(full[keys, 2 * LANES : 3 * LANES], query, NT) * (FACTOR * LOG2E)
        if masked:
            scores = jnp.where(allowed_keys(number, start, place), scores, -1e30)
        weight = jnp.exp2(scores - level)
        pressure = dot(full[keys, 3 * LANES :], grad, NT)
        slope = (weight * (pressure - delta) * FACTOR).astype(LOW)
        d_values[keys, :] += dot(weight.astype(LOW), grad)
        d_keys[keys, :] += dot(slope, query)
        d_query[...] += dot(keys_t[:, keys], slope)

    over_keys(info, block, step)
    turned = d_query[...].T
    for h in range(2):
        part = turned[h * TILE : (h + 1) * TILE]
        result[rows, h * LANES : (h + 1) * LANES] = turn_back(part, cos[rows, :], sin[rows, :]).astype(LOW)

    @pl.when(block == pl.num_programs(0) - 1)
    def _():
        mine = pl.ds(pl.multiple_of(core * half, half), half)
        theirs = pl.ds(pl.multiple_of((1 - core) * half, half), half)
        for target, which in ((keep, mine), (send, theirs)):
            target[:, : 2 * LANES] = result[which, :]
            target[:, 2 * LANES : 3 * LANES] = turn_back(
                d_keys[which, :], cos[which, :], sin[which, :]
            ).astype(LOW)
            target[:, 3 * LANES :] = d_values[which, :].astype(LOW)


def attend_back(info, own, oth, g_own, g_oth, out, lse, start, cos, sin):
    half = own.shape[0]
    tokens = 2 * half
    outs = (shape((half, 4 * LANES)), shape((half, 4 * LANES)))
    return call(
        attend_back_kernel,
        outs,
        [
            whole(own),
            whole(oth),
            whole(g_own),
            whole(g_oth),
            pl.BlockSpec((TILE, 2 * LANES), lambda b, s: (b, 0)),
            pl.BlockSpec((1, 2 * TILE), lambda b, s: (0, b)),
            whole(start),
            whole(cos),
            whole(sin),
        ],
        tuple(whole(o) for o in outs),
        grid=(tokens // TILE,),
        scratch=(
            pltpu.VMEM((tokens, 4 * LANES), LOW),
            pltpu.VMEM((tokens, 2 * LANES), LOW),
            pltpu.VMEM((LANES, tokens), LOW),
            pltpu.VMEM((tokens, LANES), F32),
            pltpu.VMEM((tokens, LANES), F32),
            pltpu.VMEM((LANES, 2 * TILE), F32),
            pltpu.VMEM((tokens, 2 * LANES), LOW),
        ),
        prefetch=1,
        flops=10 * tokens * tokens * LANES * 2,
        moved=bytes_of(own, oth, g_own, g_oth, out, *outs),
    )(info, own, oth, g_own, g_oth, out, lse, start, cos, sin)


def middle_kernel(*refs):
    weight, second, middle, r2, joined = refs[10:]
    upper = pl.program_id(0) < pl.num_programs(0) // 2
    heads = read_pieces(refs[:5], upper)
    joined[...] = heads
    x = read_pieces(refs[5:10], upper).astype(F32)
    value = x + dot(heads, weight[...])
    inverse = lax.rsqrt(jnp.mean(value * value, axis=1, keepdims=True) + EPSILON)
    second[...] = (value * inverse).astype(LOW)
    middle[...] = value[:, : middle.shape[1]]
    r2[...] = jnp.broadcast_to(inverse, r2.shape)


def middle_of(heads, xs, weight):
    tokens, width = xs[0].shape
    rows = lambda n: pl.BlockSpec((TILE, n), lambda b: (b, 0))
    outs = (
        shape((tokens, 4 * width)),
        shape((tokens, width), F32),
        shape((tokens, LANES), F32),
        shape((tokens, 4 * width)),
    )
    return call(
        middle_kernel,
        outs,
        piece_specs(width, TILE, tokens // TILE) * 2 + [whole(weight)],
        tuple(rows(o.shape[1]) for o in outs),
        grid=(tokens // TILE,),
        flops=2 * tokens * 16 * width * width,
        moved=bytes_of(*heads, *xs, weight, *outs),
    )(*heads, *xs, weight)


def feed_kernel(second, cot, g_own, u_own, g_oth, u_oth, d_own, d_oth, hidden_own, hidden_oth, back_own, back_oth):
    block = pl.program_id(0)
    per = pl.num_programs(0) // 2
    tokens, units = hidden_own.shape
    width = d_own.shape[2]

    def body(gate_w, up_w, down_w, hidden, back, at):
        down = jnp.concatenate([down_w[i] for i in range(4)], axis=1)
        near = pl.ds(pl.multiple_of(at, TILE), TILE)
        far = pl.ds(pl.multiple_of(units + at, TILE), TILE)
        for m in range(0, tokens, TILE):
            rows = slice(m, m + TILE)
            gate = dot(second[rows, :], gate_w[...])
            up = dot(second[rows, :], up_w[...])
            hidden_grad = dot(cot[rows, :], down, NT)
            share = 1.0 / (1.0 + jnp.exp(-gate))
            silu = gate * share
            hidden[rows, near] = (silu * up).astype(LOW)
            back[rows, near] = (hidden_grad * up * share * (1.0 + gate * (1.0 - share))).astype(LOW)
            back[rows, far] = (hidden_grad * silu).astype(LOW)

    @pl.when(block < per)
    def _():
        body(g_own, u_own, d_own, hidden_own, back_own, block * TILE)

    @pl.when(block >= per)
    def _():
        body(g_oth, u_oth, d_oth, hidden_oth, back_oth, (block - per) * TILE)


def feed(second, cot, gu_own, gu_oth, d_own, d_oth):
    tokens, model = second.shape
    units = gu_own.shape[1] // 2
    per = units // TILE
    early = lambda b: jnp.minimum(b, per - 1)
    late = lambda b: jnp.maximum(b - per, 0)
    column = lambda at: pl.BlockSpec((model, TILE), lambda b: (0, at(b)))
    down = lambda at: pl.BlockSpec((4, TILE, model // 4), lambda b: (0, at(b), 0))
    outs = (shape((tokens, units)), shape((tokens, units)), shape((tokens, 2 * units)), shape((tokens, 2 * units)))
    return call(
        feed_kernel,
        outs,
        [
            whole(second),
            whole(cot),
            column(early),
            column(lambda b: per + early(b)),
            column(late),
            column(lambda b: per + late(b)),
            down(early),
            down(late),
        ],
        tuple(whole(o) for o in outs),
        grid=(2 * per,),
        flops=12 * tokens * model * units,
        moved=bytes_of(second, cot, gu_own, gu_oth, d_own, d_oth, *outs),
    )(second, cot, gu_own, gu_own, gu_oth, gu_oth, d_own, d_oth)


def partial_kernel(blocked, a_own, a_oth, w_own, w_oth, *rest):
    upper = pl.program_id(0) < pl.num_programs(0) // 2
    if len(rest) == 7:
        against, own, far_a, near_a, far_b, near_b, sums = rest
    else:
        own, far_a, near_a, far_b, near_b = rest
    width = own.shape[1]
    total = 0.0
    left, right = a_own[...], a_oth[...]
    found = []
    if blocked:
        for k in range(4):
            found.append((dot(left, w_own[k]) + dot(right, w_oth[k])).astype(LOW))
    else:
        value = dot(left, w_own[...], NT) + dot(right, w_oth[...], NT)
        total = jnp.sum(value * against[...].astype(F32), axis=1, keepdims=True)
        low = value.astype(LOW)
        found = [low[:, k * width : (k + 1) * width] for k in range(4)]
    own[...] = found[0]
    if len(rest) == 7:
        sums[...] = jnp.broadcast_to(total, sums.shape)

    @pl.when(upper)
    def _():
        far_a[:, :width] = found[1]
        far_a[:, width:] = found[3]
        near_a[...] = found[2]

    @pl.when(jnp.logical_not(upper))
    def _():
        far_b[:, :width] = found[2]
        far_b[:, width:] = found[3]
        near_b[...] = found[1]


def partial_sums(blocked, a_own, a_oth, w_own, w_oth, against=None):
    tokens, depth = a_own.shape
    model = 4 * w_own.shape[2] if blocked else w_own.shape[0]
    half, width = tokens // 2, model // 4
    blocks = tokens // TILE
    plain = lambda n: pl.BlockSpec((TILE, n), lambda b: (b, 0))
    early = lambda n: pl.BlockSpec((TILE, n), lambda b: (jnp.minimum(b, blocks // 2 - 1), 0))
    late = lambda n: pl.BlockSpec((TILE, n), lambda b: (jnp.maximum(b - blocks // 2, 0), 0))
    outs = [shape((tokens, width))] + [shape((half, 2 * width)), shape((half, width))] * 2
    writes = [plain(width), early(2 * width), early(width), late(2 * width), late(width)]
    args = [a_own, a_oth, w_own, w_oth]
    specs = [plain(depth), plain(depth), whole(w_own), whole(w_oth)]
    if against is not None:
        outs.append(shape((tokens, LANES), F32))
        writes.append(plain(LANES))
        args.append(against)
        specs.append(plain(model))
    found = call(
        functools.partial(partial_kernel, blocked),
        tuple(outs),
        specs,
        tuple(writes),
        grid=(blocks,),
        flops=4 * tokens * depth * model,
        moved=bytes_of(*args, *outs),
    )(*args)
    return found[:5], None if against is None else found[5][:, 0].reshape(8, tokens // 8)


def feed_grads_kernel(second, cot, back, hidden, out):
    double, share = back.shape[1], out.shape[2]
    for columns, left, right in ((slice(0, double), second, back), (slice(double, None), cot, hidden)):
        value = dot(left[...], right[...], TN).astype(LOW)
        for k in range(out.shape[0]):
            out[k, 0, :, columns] = value[k * share : (k + 1) * share]


def feed_grads(second, cot, back, hidden, count):
    tokens, model = second.shape
    width = model // 4
    out = shape((count, 4, width // count, back.shape[1] + hidden.shape[1]))
    block = pl.BlockSpec((tokens, width), lambda i: (0, i))
    return call(
        feed_grads_kernel,
        out,
        [block, block, whole(back), whole(hidden)],
        pl.BlockSpec((count, 1) + out.shape[2:], lambda i: (0, i, 0, 0)),
        grid=(4,),
        flops=2 * tokens * model * out.shape[3],
        moved=bytes_of(second, cot, back, hidden, out),
    )(second, cot, back, hidden)


def mix_grads_kernel(first, back, spread, out, flat):
    @pl.when(pl.program_id(0) == 0)
    def _():
        flat[...] = dot(back[...], spread[...], NT).astype(LOW)

    out[0] = dot(first[...], flat[...], TN).astype(LOW)


def mix_grads(first, back, spread):
    tokens, model = first.shape
    width = model // 4
    out = shape((4, width, spread.shape[0]))
    return call(
        mix_grads_kernel,
        out,
        [pl.BlockSpec((tokens, width), lambda i: (0, i)), whole(back), whole(spread)],
        pl.BlockSpec((1,) + out.shape[1:], lambda i: (i, 0, 0)),
        grid=(4,),
        scratch=(pltpu.VMEM((tokens, spread.shape[0]), LOW),),
        flops=2 * tokens * model * out.shape[2],
        moved=bytes_of(first, back, out),
    )(first, back, spread)


def feed_place_kernel(row_ref, piece, gain, gate, up, down):
    units, share = gate.shape[1], piece.shape[2]
    for k in range(piece.shape[0]):
        rows = slice(k * share, (k + 1) * share)
        gate[rows, :] = piece[k, 0, :, :units].astype(F32) * gain[rows, :]
        up[rows, :] = piece[k, 0, :, units : 2 * units].astype(F32) * gain[rows, :]
    down[...] = jnp.concatenate(
        [piece[k, 0, :, 2 * units :].astype(F32) for k in range(piece.shape[0])], axis=0
    ).T


def feed_place(row, pieces, gain):
    count, _, share, triple = pieces.shape
    units, depth = triple // 3, count * share
    outs = (shape((depth, 4 * units), F32), shape((depth, 4 * units), F32), shape((4 * units, depth), F32))
    return call(
        feed_place_kernel,
        outs,
        [
            pl.BlockSpec((count, 1, share, triple), lambda j, s: (0, jnp.bitwise_xor(s[0], j), 0, 0)),
            whole(gain),
        ],
        (
            pl.BlockSpec((depth, units), lambda j, s: (0, j)),
            pl.BlockSpec((depth, units), lambda j, s: (0, j)),
            pl.BlockSpec((units, depth), lambda j, s: (j, 0)),
        ),
        grid=(4,),
        prefetch=1,
        moved=bytes_of(pieces, *outs),
    )(row, pieces, gain)


def mix_place_kernel(row_ref, pieces, heads, gain, query, key, value, output):
    row = row_ref[0]
    wide, narrow = query.shape[1] // 4, key.shape[1] // 4
    for j in range(4):
        piece = pieces[jnp.bitwise_xor(row, j)].astype(F32) * gain[...]
        query[:, j * wide : (j + 1) * wide] = piece[:, :wide]
        key[:, j * narrow : (j + 1) * narrow] = piece[:, wide : wide + narrow]
        value[:, j * narrow : (j + 1) * narrow] = piece[:, wide + narrow :]
        output[j * wide : (j + 1) * wide, :] = heads[jnp.bitwise_xor(row, j)].astype(F32)


def mix_place(row, pieces, heads, gain):
    _, depth, width = pieces.shape
    wide, narrow = width // 2, width // 4
    outs = (
        shape((depth, 4 * wide), F32),
        shape((depth, 4 * narrow), F32),
        shape((depth, 4 * narrow), F32),
        shape((4 * wide, depth), F32),
    )
    return call(
        mix_place_kernel,
        outs,
        [whole(pieces), whole(heads), whole(gain)],
        tuple(whole(o) for o in outs),
        grid=(1,),
        prefetch=1,
        moved=bytes_of(pieces, heads, *outs),
    )(row, pieces, heads, gain)


def sequence_starts(lengths, tokens):
    places = jnp.arange(tokens, dtype=jnp.int32)
    starts = jnp.zeros((tokens,), jnp.int32)
    end = jnp.zeros((), jnp.int32)
    for k in range(lengths.shape[0]):
        end = end + lengths[k]
        starts = jnp.where(places >= end, end, starts)
    return places, starts


def tables(places):
    lane = jnp.arange(LANES, dtype=jnp.int32)
    entry = lane % (LANES // 2)
    frequency = THETA ** (-2.0 * entry.astype(F32) / HEAD)
    real = entry < SIDE
    angles = places.astype(F32)[:, None] * frequency[None, :]
    cosine = jnp.where(real[None, :], jnp.cos(angles), 0.0)
    sign = jnp.where(lane < LANES // 2, -1.0, 1.0)
    sine = jnp.where(real[None, :], jnp.sin(angles) * sign[None, :], 0.0)
    return cosine, sine


def spread_matrix():
    source = jnp.arange(4 * HEAD, dtype=jnp.int32)
    head, entry = source // HEAD, source % HEAD
    inside = jnp.where((head < 3) & (entry >= SIDE), entry - SIDE + LANES // 2, entry)
    target = head * LANES + inside
    return (target[:, None] == jnp.arange(4 * LANES, dtype=jnp.int32)[None, :]).astype(LOW)


def on_device(
    layer_input,
    first_gain,
    query_weight,
    key_projection_weight,
    value_projection_weight,
    output_weight,
    second_gain,
    gate_weight,
    up_weight,
    down_weight,
    sequence_lengths,
    cotangent,
):
    row = lax.axis_index("row")
    core = lax.axis_index("col")
    place = lax.axis_index("dp")
    blocks = lax.axis_size("dp")
    row_info = row.reshape(1).astype(jnp.int32)
    half, width = layer_input.shape
    tokens, model = 2 * half, 4 * width
    units = gate_weight.shape[1] // 4
    rows = output_weight.shape[0]
    chunk = rows // 4
    relative = [jnp.bitwise_xor(row, i) for i in range(4)]
    live = Live()
    live.x, live.cot = layer_input, cotangent

    live.xs = gather_one(live.x)
    gains = [gain[:, None] for gain in (first_gain, second_gain)]
    packed = pack(row_info, gains[0], query_weight, key_projection_weight, value_projection_weight)
    mixer = [packed[i] for i in range(4)]
    halves, weights = ready(
        fetch_halves(mixer, place, blocks), (gate_weight, up_weight, down_weight, output_weight, gains[1])
    )
    live.mixer_one = fetch_one(halves)
    live.mixer_own, live.lengths = mixer[0], sequence_lengths[0]
    gate, up, down, out, gain = weights
    downs = [lax.dynamic_slice_in_dim(down, relative[i] * units, units, 0) for i in range(4)]
    out_down = [jnp.concatenate([out, downs[i]], axis=0) for i in range(4)]
    scaled = lambda weight, i: (
        lax.dynamic_slice_in_dim(weight, relative[i] * units, units, 1).astype(F32) * gain
    ).astype(LOW)
    gate_up = [jnp.concatenate([scaled(gate, i), scaled(up, i)], axis=1) for i in range(4)]
    live.od_own, live.od_halves = out_down[0], fetch_halves(out_down, place, blocks)
    live.gu_own, live.gu_halves = gate_up[0], fetch_halves(gate_up, place, blocks)
    live.sync()

    halves, mine = ready(gather_halves(live.xs), jnp.stack(live.mixer_one))
    live.xs = gather_two(live.xs, halves)
    live.mixer = (live.mixer_own, mine, fetch_two(mine, blocks))
    places, starts = sequence_starts(live.lengths, tokens)
    live.cos, live.sin = tables(places - starts)
    live.start = starts[None, :]
    last_starts = (starts[TILE - 1 :: TILE] + TILE - 1) // TILE
    live.info = jnp.concatenate([core.reshape(1), starts[::TILE] // TILE, last_starts]).astype(jnp.int32)
    spread = spread_matrix()
    del live.mixer_one, live.mixer_own, live.lengths
    live.sync()

    live.gu_one = fetch_one(live.gu_halves)
    live.w_own = dot(fetched(*live.mixer, place).reshape(model, 4 * HEAD), spread).astype(LOW)
    live.w_oth = other(live.w_own)
    cos_own = lax.dynamic_slice_in_dim(live.cos, core * half, half, 0)
    sin_own = lax.dynamic_slice_in_dim(live.sin, core * half, half, 0)
    live.first, live.r1, live.qkv, live.send = project(
        live.xs, live.w_own, live.w_oth, cos_own, sin_own
    )
    del live.mixer, live.gu_halves
    live.sync()
    halves, send, live.gu_mine = ready(live.od_halves, live.send, jnp.stack(live.gu_one))
    live.gu_theirs = fetch_two(live.gu_mine, blocks)
    live.od_one = fetch_one(halves)
    live.qkv_got = other(send)
    live.keep, live.send, live.attended, live.lse = attend(live.info, live.qkv, live.qkv_got, live.start)
    del live.gu_one, live.od_halves
    live.sync()
    live.heads = jnp.concatenate([live.keep, other(live.send)], axis=1)
    live.od_mine = jnp.stack(live.od_one)
    del live.keep, live.send, live.od_one
    live.sync()

    live.od_theirs = fetch_two(live.od_mine, blocks)
    live.heads = gather_one(live.heads)
    live.cots = gather_one(live.cot)
    live.gu_own = fetched(live.gu_own, live.gu_mine, live.gu_theirs, place).reshape(model, 2 * units)
    del live.gu_mine, live.gu_theirs
    live.sync()

    halves, more = ready(gather_halves(live.heads), gather_halves(live.cots))
    live.heads = gather_two(live.heads, halves)
    live.cots = gather_two(live.cots, more)
    live.od_own = fetched(live.od_own, live.od_mine, live.od_theirs, place)
    od_oth = other(live.od_own)
    live.out_full, live.out_mine = order(row_info, live.od_own[:, :rows], od_oth[:, :rows])
    live.d_own, live.d_oth = live.od_own[:, rows:], od_oth[:, rows:]
    del live.od_own, live.od_mine, live.od_theirs
    live.sync()
    live.gu_oth = other(live.gu_own)
    live.cot_all = join(live.cots)
    del live.cots

    live.second, live.middle, live.r2, live.heads_all = middle_of(live.heads, live.xs, live.out_full)
    del live.heads, live.xs, live.out_full
    live.hid_own, live.hid_oth, live.back_own, live.back_oth = feed(
        live.second, live.cot_all, live.gu_own, live.gu_oth, live.d_own, live.d_oth
    )
    live.sg, live.sums = partial_sums(False, live.back_own, live.back_oth, live.gu_own, live.gu_oth, live.second)
    del live.gu_own, live.gu_oth
    live.sync()

    def added(own, got):
        return (own.astype(F32) + got.astype(F32)).astype(LOW)

    live.sg = scatter_one(live.sg)
    live.sums = (live.sums, swap(live.sums, 1))
    live.feed_oth = feed_grads(live.second, live.cot_all, live.back_oth, live.hid_oth, blocks)
    live.feed_own = feed_grads(live.second, live.cot_all, live.back_own, live.hid_own, blocks)
    del live.back_own, live.back_oth, live.second, live.cot_all
    live.sync()

    halves, sums, feed_oth = ready(scatter_halves(live.sg), live.sums[0] + live.sums[1], live.feed_oth)
    live.sg = scatter_two(live.sg, halves)
    live.sums = (sums, swap(sums, 2))
    live.feed_got = other(feed_oth)
    del live.feed_oth
    live.sync()

    second_grad = scattered(live.sg)
    inner = (live.sums[0] + live.sums[1]).reshape(half)
    r2 = live.r2[:, :1]
    live.middle_grad = (
        live.cot.astype(F32)
        + r2 * second_grad
        - live.middle * (r2 * r2 * inner[:, None] / model)
    )
    live.branch = live.middle_grad.astype(LOW)
    live.branches = gather_one(*ready(live.branch))
    feed_sum = lax.psum_scatter(added(live.feed_own, live.feed_got), "dp", scatter_dimension=0)
    live.fo, _ = partial_sums(True, live.hid_own, live.hid_oth, live.d_own, live.d_oth)
    del live.feed_own, live.feed_got, live.hid_own, live.hid_oth, live.d_own, live.d_oth
    live.gain_part = jnp.sum(second_grad * live.middle * r2, axis=0) / second_gain
    del live.sg, live.sums, live.cot, live.r2
    live.sync()

    live.branches = gather_two(live.branches, ready(*gather_halves(live.branches)))
    live.o_all = dot(live.heads_all, live.branch, TN).astype(LOW).reshape(4, 2, chunk, width)
    del live.heads_all, live.branch
    live.sync()
    live.grad, live.send = heads_grad_of(live.branches, live.out_mine)
    live.grad_got = other(live.send)
    live.o = added(live.o_all[:, 0], other(live.o_all[:, 1]))
    del live.branches, live.out_mine, live.send, live.o_all
    live.sync()

    o_rows, mix_rows, share = (chunk,), (width,), width // blocks
    parts = ready(*chain_parts(1, live.o, o_rows, blocks, []))
    live.o_moving = chain_sum(1, parts, blocks, [])
    live.fo = scatter_one(live.fo)
    live.bk, live.send = attend_back(
        live.info, live.qkv, live.qkv_got, live.grad, live.grad_got,
        live.attended, live.lse, live.start, live.cos, live.sin,
    )
    del live.qkv, live.qkv_got, live.grad, live.grad_got, live.attended, live.lse, live.start, live.info
    live.sync()

    halves, send, parts = ready(
        scatter_halves(live.fo), live.send, chain_parts(2, live.o, o_rows, blocks, live.o_moving)
    )
    live.o_moving = chain_sum(2, parts, blocks, live.o_moving)
    live.fo = scatter_two(live.fo, halves)
    live.bg = other(send)
    live.mix_oth = mix_grads(live.first, live.bg, spread)
    live.mix_own = mix_grads(live.first, live.bk, spread)
    del live.send
    live.sync()
    live.feed_sum = spread_row(feed_sum)
    live.mix = added(live.mix_own, other(live.mix_oth))
    live.moving = chain_sum(1, chain_parts(1, live.mix, mix_rows, blocks, []), blocks, [])
    del live.mix_own, live.mix_oth
    live.sync()
    parts, more, (bk, bg) = ready(
        chain_parts(2, live.mix, mix_rows, blocks, live.moving),
        chain_parts(3, live.o, o_rows, blocks, live.o_moving),
        (live.bk, live.bg),
    )
    live.moving = chain_sum(2, parts, blocks, live.moving)
    live.o_moving = chain_sum(3, more, blocks, live.o_moving)
    feeds = lax.all_gather(live.feed_sum, "dp", axis=0)
    live.fg, live.sums = partial_sums(False, bk, bg, live.w_own, live.w_oth, live.first)
    del live.bk, live.bg, live.w_own, live.w_oth, live.first
    live.sync()

    live.o_moving = chain_sums(4, live.o, o_rows, blocks, live.o_moving)
    live.o = chain_summed(live.o, o_rows, blocks, live.o_moving)
    del live.o_moving
    parts = ready(*chain_parts(3, live.mix, mix_rows, blocks, live.moving))
    live.moving = chain_sum(3, parts, blocks, live.moving)
    live.fg = scatter_one(live.fg)
    live.sums = (live.sums, swap(live.sums, 1))
    layer_output = (live.middle + scattered(live.fo)).astype(LOW)
    del live.fo, live.middle, live.feed_sum
    live.sync()

    live.moving = chain_sums(4, live.mix, mix_rows, blocks, live.moving)
    halves, sums, shard = ready(
        scatter_halves(live.fg),
        live.sums[0] + live.sums[1],
        chain_summed(live.mix, mix_rows, blocks, live.moving),
    )
    live.fg = scatter_two(live.fg, halves)
    live.sums = (sums, swap(sums, 2))
    live.mix = spread_row(shard)
    del live.moving
    live.sync()

    first_grad = scattered(live.fg)
    inner = (live.sums[0] + live.sums[1]).reshape(half)
    r1 = live.r1[:, :1]
    inputs = live.x.astype(F32)
    input_gradient = (
        live.middle_grad
        + r1 * first_grad
        - inputs * (r1 * r1 * inner[:, None] / model)
    )
    gains = jnp.stack([jnp.sum(first_grad * inputs * r1, axis=0) / first_gain, live.gain_part])
    carried = split_low(gains + other(gains))[None]
    carried = jnp.concatenate([carried, jnp.zeros((3,) + carried.shape[1:], LOW)], axis=0)
    live.mix = jnp.concatenate([live.mix, live.o, carried], axis=1)
    del live.fg, live.sums, live.r1, live.x, live.middle_grad, live.gain_part, live.o
    live.sync()
    live.moving = chain_spread(1, 2, live.mix, blocks, [])
    live.sync()
    live.moving = chain_spread(2, 3, live.mix, blocks, live.moving)
    placed = feed_place(row_info, feeds, second_gain[:, None])
    live.placed = placed
    live.sync()
    moving = chain_spread(3, blocks, live.mix, blocks, live.moving)
    mixes = chain_joined(live.mix, blocks, moving)
    gate_total, up_total, down_total = live.placed
    last = share + chunk // blocks
    query_total, key_total, value_total, output_total = mix_place(
        row_info,
        mixes[:, :, :share].reshape(4, width, width),
        mixes[:, :, share:last].reshape(4, chunk, width),
        first_gain[:, None],
    )
    gain_total = sum(unsplit(mixes[0, k, last:], 2) for k in range(blocks))
    return (
        layer_output,
        input_gradient,
        query_total,
        key_total,
        value_total,
        output_total,
        gate_total,
        up_total,
        down_total,
        gain_total[0],
        gain_total[1],
    )


def solution(mesh):
    return jax.shard_map(
        on_device,
        mesh=mesh,
        in_specs=(
            P(("dp", "col"), "row"),
            P("row"),
            P("row", "col"),
            P("row", "col"),
            P("row", "col"),
            P("col", "row"),
            P("row"),
            P("row", "col"),
            P("row", "col"),
            P("col", "row"),
            P("dp", None),
            P(("dp", "col"), "row"),
        ),
        out_specs=(
            P(("dp", "col"), "row"),
            P(("dp", "col"), "row"),
            P("row", "col"),
            P("row", "col"),
            P("row", "col"),
            P("col", "row"),
            P("row", "col"),
            P("row", "col"),
            P("col", "row"),
            P("row"),
            P("row"),
        ),
        check_vma=False,
    )
```
